32 devices in a mesh: member: 2 (over y), gx: 16 (over z, x, core).
Axes of the slice: x: 2, y: 2, z: 4, core: 2. Of those that a mesh axis runs over, the one named last changes fastest.
Arguments:
- inputs: float32 [32768, 557], P(('member', 'gx')), parts along dimension 0, may hold values from -6 to 6
- tracer: float32 [60, 256, 128], P(None, ('member', 'gx')), parts along dimension 1, may hold values from -6 to 6
- speed_along: float32 [256, 128], P(('member', 'gx')), parts along dimension 0, may hold values from -0.5 to 0.5
- speed_across: float32 [256, 128], P(('member', 'gx')), parts along dimension 0, may hold values from -0.3 to 0.3
- inverse_list: int32 [32768], P(('member', 'gx')), parts along dimension 0, may hold values from -1 to 1023, as said below
- weight_one: float32 [557, 768], replicated, may hold values from -0.25 to 0.25
- bias_one: float32 [768], replicated, may hold values from -3 to 3
- weight_two: float32 [768, 640], replicated, may hold values from -0.3125 to 0.3125
- bias_two: float32 [640], replicated, may hold values from -3 to 3
- weight_three: float32 [640, 512], replicated, may hold values from -0.3125 to 0.3125
- bias_three: float32 [512], replicated, may hold values from -3 to 3
- weight_four: float32 [512, 640], replicated, may hold values from -0.375 to 0.375
- bias_four: float32 [640], replicated, may hold values from -3 to 3
- weight_five: float32 [640, 640], replicated, may hold values from -0.3125 to 0.3125
- bias_five: float32 [640], replicated, may hold values from -3 to 3
- weight_six: float32 [640, 368], replicated, may hold values from -0.3125 to 0.3125
- bias_six: float32 [368], replicated, may hold values from -3 to 3
Outputs:
- tendencies: float32 [32768, 368], P(('member', 'gx')), parts along dimension 0
- advected: float32 [60, 256, 128], P(None, ('member', 'gx')), parts along dimension 1
The draws below stay inside these ranges and needn't reach their ends.
There are 2 independent parts, one for each index of `member`. The reference program is written for one: setup_inputs(seed, part) draws one part's arguments, and reference() takes and returns one part's arrays. A program takes and returns all parts, laid end to end along the dimension named above; an argument that names none is the same for every part. Nothing has to cross between parts.
Inputs may be any that keep to these rules, and one draw needn't show every extreme that they name: `inverse_list`: no two day columns of one tile share a slot position. Every tile evaluates exactly 512 day columns in all, and half of all columns are day columns. Some tile's columns are all day; such a tile fills all 64 slots to every tile.
All inputs are finite; a program needn't handle non-finite values.
Results may differ from the reference program's by a relative error of at most 0.0003.
Values sent between devices are 32-bit elements; how exact they have to be, the bound alone decides.
No kernel may reach another device: no remote copies, remote signals or barrier semaphores. Data moves between devices by JAX's collectives and lax.ppermute only.
A program may use at most 64 MiB of HBM per device.

```python
import math
import jax
import jax.numpy as jnp
from jax import lax

GY = 128
LEV = 60
IN = 557
H1 = 768
H2 = 640
H3 = 512
H4 = 640
H5 = 640
OUT = 368
NTILES = 16
COLS_DEV = 1024
CAP = 64
GX = 128
TOTAL = 16384


def draw_inverse_list(key, part):
    key = jax.random.fold_in(key, 13)
    start = jax.random.randint(key, (), 0, TOTAL, dtype=jnp.int32)
    order = jax.random.permutation(jax.random.fold_in(key, 1), NTILES).astype(jnp.int32)
    places = jnp.arange(TOTAL, dtype=jnp.int32)
    ranking = (places - start) % TOTAL
    is_day = ranking < TOTAL // 2
    source = places // COLS_DEV
    masked = jnp.where(is_day, ranking, TOTAL).reshape(NTILES, COLS_DEV)
    earliest = jnp.min(masked, axis=1)
    slot_index = jnp.where(is_day, (ranking - earliest[source]) // NTILES, 0)
    target = order[ranking % NTILES]
    return jnp.where(is_day, target * CAP + slot_index, -1).astype(jnp.int32)


def draw_tracer(key, part):
    key = jax.random.fold_in(key, 31)
    subkeys = jax.random.split(key, 4)
    wave_count = max(GX // 12, 1)
    row_ids = jnp.arange(GX, dtype=jnp.int32)
    fraction = (row_ids * wave_count % GX).astype(jnp.float32) / GX
    shifts = jax.random.uniform(subkeys[1], (LEV, 1, GY), jnp.float32, 0.0, 2.0 * math.pi)
    pattern = jnp.sin(2.0 * math.pi * fraction[None, :, None] + shifts)
    height = jnp.exp(jax.random.uniform(subkeys[0], (LEV, 1, GY), jnp.float32, math.log(1.5), math.log(4.5)))
    offset = 0.5 * jax.random.normal(subkeys[2], (LEV, 1, GY), jnp.float32)
    jitter = 0.15 * jax.random.normal(subkeys[3], (LEV, GX, GY), jnp.float32)
    return jnp.clip(height * pattern + offset + jitter, -6.0, 6.0)


def draw_speed_along(key, part):
    key = jax.random.fold_in(key, 47)
    subkeys = jax.random.split(key, 2)
    row_ids = jnp.arange(GX, dtype=jnp.int32)[:, None]
    offsets = jax.random.randint(subkeys[0], (1, GY), 0, GX, dtype=jnp.int32)
    band_index = (row_ids + offsets) % GX * 4 // GX % 2
    magnitude = jnp.exp(jax.random.uniform(subkeys[1], (GX, GY), jnp.float32, math.log(0.25), math.log(0.5)))
    return jnp.where(band_index == 0, magnitude, -magnitude)


def levels(key, dims, shards, smallest, high):
    def one(axis_at, blocks):
        heights = jax.random.uniform(jax.random.fold_in(jax.random.fold_in(key, 6), axis_at), (blocks,), jnp.float32, smallest / len(shards), high / len(shards))
        return jnp.repeat(jnp.exp(heights), dims[axis_at] // blocks).reshape((-1,) + (1,) * (len(dims) - axis_at - 1))

    level = one(*shards[0])
    for cut in shards[1:]:
        level = level * one(*cut)
    return level


def scatter_about(stream_key, extent, scale, most, shards=(), kind=jnp.bfloat16):
    array = jax.random.normal(stream_key, extent, jnp.float32) * scale
    if len(shards) > 0:
        array = levels(stream_key, extent, shards, -0.22, 0.18) * array
    return jnp.clip(array, min=-most, max=most).astype(kind)


def setup_inputs(seed: int = 0, part: int = 0) -> dict:
    key_list = jax.random.split(jax.random.key(seed), 18)
    own_keys = jax.random.split(jax.random.fold_in(key_list[17], part), 18)
    return {
        "inputs": scatter_about(own_keys[0], (TOTAL, IN), 1.0, 6.0, ((0, 16),), jnp.float32),
        "tracer": draw_tracer(jax.random.fold_in(jax.random.fold_in(key_list[17], part), 71), part),
        "speed_along": draw_speed_along(jax.random.fold_in(jax.random.fold_in(key_list[17], part), 71), part),
        "speed_across": jnp.clip(jax.random.uniform(own_keys[3], (GX, GY), jnp.float32, -0.3, 0.3) * levels(own_keys[3], (GX, GY), ((0, 16),), -0.4, 0.0), -0.3, 0.3),
        "inverse_list": draw_inverse_list(jax.random.fold_in(jax.random.fold_in(key_list[17], part), 71), part),
        "weight_one": scatter_about(key_list[5], (IN, H1), IN ** -0.5, 0.25, (), jnp.float32),
        "bias_one": scatter_about(key_list[6], (H1,), 0.5, 3.0, (), jnp.float32),
        "weight_two": scatter_about(key_list[7], (H1, H2), (H1 // 2) ** -0.5, 0.3125, (), jnp.float32),
        "bias_two": scatter_about(key_list[8], (H2,), 0.5, 3.0, (), jnp.float32),
        "weight_three": scatter_about(key_list[9], (H2, H3), (H2 // 2) ** -0.5, 0.3125, (), jnp.float32),
        "bias_three": scatter_about(key_list[10], (H3,), 0.5, 3.0, (), jnp.float32),
        "weight_four": scatter_about(key_list[11], (H3, H4), (H3 // 2) ** -0.5, 0.375, (), jnp.float32),
        "bias_four": scatter_about(key_list[12], (H4,), 0.5, 3.0, (), jnp.float32),
        "weight_five": scatter_about(key_list[13], (H4, H5), (H4 // 2) ** -0.5, 0.3125, (), jnp.float32),
        "bias_five": scatter_about(key_list[14], (H5,), 0.5, 3.0, (), jnp.float32),
        "weight_six": scatter_about(key_list[15], (H5, OUT), (H5 // 2) ** -0.5, 0.3125, (), jnp.float32),
        "bias_six": scatter_about(key_list[16], (OUT,), 0.5, 3.0, (), jnp.float32),
    }


def network(rows, weights, biases):
    for layer in range(5):
        rows = jax.nn.silu(jnp.dot(rows, weights[layer], precision=lax.Precision.HIGHEST, preferred_element_type=jnp.float32) + biases[layer])
    return jnp.dot(rows, weights[5], precision=lax.Precision.HIGHEST, preferred_element_type=jnp.float32) + biases[5]


def minmod(first, second):
    smaller = jnp.where(jnp.abs(first) < jnp.abs(second), first, second)
    return jnp.where(first * second > 0, smaller, jnp.zeros_like(first))


def limited(field, courant, axis):
    back_two = jnp.roll(field, 2, axis)
    back_one = jnp.roll(field, 1, axis)
    ahead = jnp.roll(field, -1, axis)
    left = back_one + 0.5 * minmod(field - back_one, back_one - back_two)
    right = field - 0.5 * minmod(ahead - field, field - back_one)
    flux = jnp.where(courant > 0, courant * left, courant * right)
    return flux - jnp.roll(flux, -1, axis)


def operator(field, speed_along, speed_across):
    return limited(field, speed_along[None], 1) + limited(field, speed_across[None], 2)


def reference(inputs, tracer, speed_along, speed_across, inverse_list, weight_one, bias_one, weight_two, bias_two, weight_three, bias_three, weight_four, bias_four, weight_five, bias_five, weight_six, bias_six):
    weights = (weight_one, weight_two, weight_three, weight_four, weight_five, weight_six)
    biases = (bias_one, bias_two, bias_three, bias_four, bias_five, bias_six)

    def evaluate(portion):
        return network(portion, weights, biases)

    blocks = inputs.reshape(TOTAL // COLS_DEV, COLS_DEV, IN)
    outputs = lax.map(evaluate, blocks).reshape(TOTAL, OUT)
    tendencies = jnp.where((inverse_list >= 0)[:, None], outputs, jnp.zeros_like(outputs))
    start = tracer + tendencies[:, :LEV].reshape(GX, GY, LEV).transpose(2, 0, 1)
    section_one = start + operator(start, speed_along, speed_across)
    section_two = 0.75 * start + 0.25 * (section_one + operator(section_one, speed_along, speed_across))
    advected = (1.0 / 3.0) * start + (2.0 / 3.0) * (section_two + operator(section_two, speed_along, speed_across))
    return tendencies, advected
```

```python
import functools
import jax
import jax.numpy as jnp
from jax import lax
from jax.experimental import pallas as pl
from jax.experimental.pallas import tpu as pltpu
from jax.sharding import PartitionSpec as P

F32, BF16 = jnp.float32, jnp.bfloat16
LANES = 128
CHUNK = 256
HALO = 6


def round_up(value, unit):
    return -(-value // unit) * unit


def split(value):
    high = value.astype(BF16)
    low = (value - high.astype(F32)).astype(BF16)
    return high, low


def network_kernel(
    *refs, sizes, levels, axis
):
    (inverse, tracer, along, across, *rest) = refs
    biases, rest = rest[:6], rest[6:]
    x_hbm, weights_hbm, rest = rest[0], rest[1:7], rest[7:]
    tend_hbm, field, pay_a, pay_b, rest = rest[0], rest[1], rest[2], rest[3], rest[4:]
    x_in, weights_in, rest = rest[0], rest[1:7], rest[7:]
    cats, columns, rest = rest[:6], rest[6:12], rest[12:]
    hold_a, hold_b, w_tail, x_tail, b_six, tend, x_sems, w_sems, out_sems = rest

    width = x_hbm.shape[1]
    chunks = width // CHUNK
    depth_in = sizes[0]
    aligned = depth_in // 8 * 8
    whole = depth_in // LANES * LANES

    def x_copy(c):
        part = pl.ds(c * CHUNK, CHUNK)
        return pltpu.make_async_copy(x_hbm.at[:, part], x_in.at[:, part], x_sems.at[c])

    def w_copy(layer):
        return pltpu.make_async_copy(
            weights_hbm[layer], weights_in[layer], w_sems.at[layer]
        )

    def out_copy(c):
        part = pl.ds(c * CHUNK, CHUNK)
        return pltpu.make_async_copy(
            tend.at[:, part], tend_hbm.at[:, part], out_sems.at[c]
        )

    def bias_columns(layer):
        count = sizes[layer + 1]
        source = biases[layer]
        if count % LANES:
            b_six[0:1, :] = jnp.zeros((1, b_six.shape[1]), F32)
            b_six[0:1, 0:count] = source[...].reshape(1, count)
            row = b_six[0:1, :]
        else:
            row = source[...].reshape(1, count)
        scale = 0.5 if layer < 5 else 1.0
        for n in range(0, count, LANES):
            block = jnp.broadcast_to(row[:, n : n + LANES], (LANES, LANES)).T * scale
            keep = min(LANES, count - n)
            columns[layer][n : n + keep, :] = block[:keep]

    def put_weights(layer, rows, start, block):
        depth = cats[layer].shape[1] // 3
        high, low = split(block)
        size = block.shape[1]
        cats[layer][rows, start : start + size] = high
        cats[layer][rows, depth + start : depth + start + size] = high
        cats[layer][rows, 2 * depth + start : 2 * depth + start + size] = low

    def prepare(layer, part, parts):
        count = sizes[layer + 1]
        if layer == 5:
            step = 16
            for n in range(0, count, step):
                if (n // step) % parts == part:
                    put_weights(
                        layer, slice(n, n + step), 0, weights_in[5][n : n + step, :]
                    )
            return
        for n in range(0, count, LANES):
            if (n // LANES) % parts != part:
                continue
            rows = slice(n, n + LANES)
            for k in range(0, sizes[layer], LANES):
                if layer == 0 and k >= whole:
                    block = w_tail[:, n : n + LANES]
                else:
                    block = weights_in[layer][k : k + LANES, n : n + LANES]
                put_weights(layer, rows, k, block.T * 0.5)

    def put_rows(hold, depth, start, cols, value):
        high, low = split(value)
        size = value.shape[0]
        hold[start : start + size, cols] = high
        hold[depth + start : depth + start + size, cols] = low
        hold[2 * depth + start : 2 * depth + start + size, cols] = high

    w_copy(0).start()
    x_copy(0).start()
    for c in range(1, chunks):
        x_copy(c).start()
    w_copy(1).start()
    w_tail[...] = jnp.zeros(w_tail.shape, F32)
    x_tail[...] = jnp.zeros(x_tail.shape, F32)
    for layer in range(6):
        bias_columns(layer)
    rows, levels_wide = field.shape[0], field.shape[1]
    for r in range(rows):
        field[r, levels : levels + 1, :] = along[r : r + 1, :]
        field[r, levels + 1 : levels + 2, :] = across[r : r + 1, :]
        field[r, levels + 2 : levels_wide, :] = jnp.zeros(
            (levels_wide - levels - 2, LANES), F32
        )
    w_copy(0).wait()
    w_tail[0 : aligned - whole, :] = weights_in[0][whole:aligned, :]
    w_tail[aligned - whole : depth_in - whole, :] = weights_in[0][aligned:depth_in, :]
    prepare(0, 0, 1)
    depth_pad = cats[0].shape[1] // 3
    for layer in range(2, 6):
        w_copy(layer).start()
    for c in range(chunks):
        x_copy(c).wait()
        cols = slice(c * CHUNK, (c + 1) * CHUNK)
        x_tail[0 : aligned - whole, cols] = x_in[whole:aligned, cols]
        x_tail[aligned - whole : depth_in - whole, cols] = x_in[aligned:depth_in, cols]
        for k in range(0, whole, LANES):
            put_rows(hold_a, depth_pad, k, cols, x_in[k : k + LANES, cols])
        put_rows(hold_a, depth_pad, whole, cols, x_tail[:, cols])

    held, other = hold_a, hold_b
    for layer in range(6):
        if layer + 1 < 6:
            w_copy(layer + 1).wait()
        count = sizes[layer + 1]
        deep = cats[layer].shape[1]
        for c in range(chunks):
            cols = slice(c * CHUNK, (c + 1) * CHUNK)
            total = jnp.dot(
                cats[layer][...], held[0:deep, cols], preferred_element_type=F32
            )
            if layer + 1 < 6:
                prepare(layer + 1, c, chunks)
            bias = columns[layer][...]
            bias = jnp.concatenate([bias, bias], axis=1)
            value = total + bias
            if layer < 5:
                value = value + value * jnp.tanh(value)
                put_rows(other, count, 0, cols, value)
            else:
                for half in range(CHUNK // LANES):
                    r = c * (CHUNK // LANES) + half
                    day = inverse[r : r + 1, :] >= 0
                    shown = jnp.where(
                        day, value[:, half * LANES : (half + 1) * LANES], 0.0
                    )
                    tend[:, r * LANES : (r + 1) * LANES] = shown
                    field[r, 0:levels, :] = (
                        tracer[pl.ds(r, levels, stride=rows), :] + shown[0:levels]
                    )
                out_copy(c).start()
        held, other = other, held

    odd = lax.rem(lax.axis_index(axis), 2)
    pay_a[...] = field[pl.ds((rows - HALO) * odd, HALO)]
    pay_b[...] = field[pl.ds((rows - HALO) * (1 - odd), HALO)]
    for c in range(chunks):
        out_copy(c).wait()


def network(inverse, tracer, along, across, biases, x, weights, axis):
    sizes = [x.shape[0]] + [b.shape[0] for b in biases]
    width = x.shape[1]
    rows = along.shape[0]
    levels = tracer.shape[0] // rows
    levels_wide = round_up(levels + 2, 8)
    chunks = width // CHUNK
    padded = [round_up(s, LANES) for s in sizes[:6]]
    deepest = 3 * max(padded)
    tail = padded[0] - sizes[0] // LANES * LANES
    vmem, hbm = pl.BlockSpec(memory_space=pltpu.VMEM), pl.BlockSpec(memory_space=pl.ANY)
    total = sum(sizes[i] * sizes[i + 1] for i in range(6)) * width
    return pl.pallas_call(
        functools.partial(network_kernel, sizes=sizes, levels=levels, axis=axis),
        out_shape=(
            jax.ShapeDtypeStruct((sizes[6], width), F32),
            jax.ShapeDtypeStruct((rows, levels_wide, LANES), F32),
            jax.ShapeDtypeStruct((HALO, levels_wide, LANES), F32),
            jax.ShapeDtypeStruct((HALO, levels_wide, LANES), F32),
        ),
        in_specs=[vmem] * 10 + [hbm] * 7,
        out_specs=(hbm, vmem, vmem, vmem),
        scratch_shapes=[
            pltpu.VMEM(x.shape, F32),
            *[pltpu.VMEM(w.shape, F32) for w in weights],
            *[pltpu.VMEM((sizes[i + 1], 3 * padded[i]), BF16) for i in range(6)],
            *[pltpu.VMEM((sizes[i + 1], LANES), F32) for i in range(6)],
            pltpu.VMEM((deepest, width), BF16),
            pltpu.VMEM((deepest, width), BF16),
            pltpu.VMEM((tail, sizes[1]), F32),
            pltpu.VMEM((tail, width), F32),
            pltpu.VMEM((8, round_up(sizes[6], LANES)), F32),
            pltpu.VMEM((sizes[6], width), F32),
            pltpu.SemaphoreType.DMA((chunks,)),
            pltpu.SemaphoreType.DMA((6,)),
            pltpu.SemaphoreType.DMA((chunks,)),
        ],
        compiler_params=pltpu.CompilerParams(vmem_limit_bytes=52 * 2**20),
        cost_estimate=pl.CostEstimate(
            flops=6 * total, bytes_accessed=14_000_000, transcendentals=3_000_000
        ),
        name="column_network",
    )(inverse, tracer, along, across, *biases, x, *weights)


def half_minmod(first, second):
    return 0.5 * (
        jnp.maximum(jnp.minimum(first, second), 0.0)
        + jnp.minimum(jnp.maximum(first, second), 0.0)
    )


def change(rows, along, across):
    low, high = min(rows), max(rows)
    step = {i: rows[i] - rows[i - 1] for i in range(low + 1, high + 1)}
    plus, minus = {}, {}
    for i in range(low + 1, high):
        slope = half_minmod(step[i + 1], step[i])
        plus[i], minus[i] = rows[i] + slope, rows[i] - slope
    flux = {
        i: along[i] * jnp.where(along[i] > 0, plus[i - 1], minus[i])
        for i in range(low + 2, high)
    }
    result = {}
    for i in range(low + 2, high - 1):
        here = rows[i]
        back = here - pltpu.roll(here, 1, 1)
        slope = half_minmod(pltpu.roll(back, LANES - 1, 1), back)
        side = across[i] * jnp.where(
            across[i] > 0, pltpu.roll(here + slope, 1, 1), here - slope
        )
        result[i] = (flux[i] - flux[i + 1]) + (side - pltpu.roll(side, LANES - 1, 1))
    return result


def advect_kernel(field, got_a, got_b, out, wide, *, levels, axis):
    rows = field.shape[0]
    odd = lax.rem(lax.axis_index(axis), 2)
    wide[HALO : HALO + rows] = field[...]
    wide[pl.ds((HALO + rows) * odd, HALO)] = got_a[...]
    wide[pl.ds((HALO + rows) * (1 - odd), HALO)] = got_b[...]
    span = range(-HALO, rows + HALO)
    along = {i: wide[i + HALO, levels : levels + 1, :] for i in span}
    across = {i: wide[i + HALO, levels + 1 : levels + 2, :] for i in span}
    for base in range(0, levels, 8):
        start = {i: wide[i + HALO, base : base + 8, :] for i in span}
        moved = change(start, along, across)
        one = {i: start[i] + moved[i] for i in moved}
        moved = change(one, along, across)
        two = {i: 0.75 * start[i] + 0.25 * (one[i] + moved[i]) for i in moved}
        moved = change(two, along, across)
        keep = min(8, levels - base)
        for i in moved:
            value = 1.0 / 3.0 * start[i] + 2.0 / 3.0 * (two[i] + moved[i])
            out[pl.ds(base * rows + i, keep, stride=rows), :] = value[:keep]


def advect(field, got_a, got_b, levels, axis):
    rows, levels_wide, across = field.shape
    vmem = pl.BlockSpec(memory_space=pltpu.VMEM)
    return pl.pallas_call(
        functools.partial(advect_kernel, levels=levels, axis=axis),
        out_shape=jax.ShapeDtypeStruct((levels * rows, across), F32),
        in_specs=[vmem] * 3,
        out_specs=vmem,
        scratch_shapes=[pltpu.VMEM((rows + 2 * HALO, levels_wide, across), F32)],
        name="advect_sections",
    )(field, got_a, got_b)


def shards(inputs, tracer, speed_along, speed_across, inverse_list, *params):
    weights, biases = list(params[0::2]), params[1::2]
    weights[5] = weights[5].T
    levels, rows, across = tracer.shape
    tendencies, field, pay_a, pay_b = network(
        inverse_list.reshape(rows, across),
        tracer.reshape(levels * rows, across),
        speed_along,
        speed_across,
        biases,
        inputs.T,
        weights,
        "gx",
    )
    count = lax.axis_size("gx")
    outer = [(i, (i - 1 if i % 2 == 0 else i + 1) % count) for i in range(count)]
    inner = [(i, i + 1 if i % 2 == 0 else i - 1) for i in range(count)]
    got_a = lax.ppermute(pay_a, "gx", outer)
    got_b = lax.ppermute(pay_b, "gx", inner)
    advected = advect(field, got_a, got_b, levels, "gx")
    return tendencies.T, advected.reshape(levels, rows, across)


def solution(mesh):
    placed = (
        P(("member", "gx"), None),
        P(None, ("member", "gx"), None),
        P(("member", "gx"), None),
        P(("member", "gx"), None),
        P(("member", "gx")),
        *[P()] * 12,
    )
    return jax.shard_map(
        shards,
        mesh=mesh,
        in_specs=placed,
        out_specs=(P(("member", "gx"), None), P(None, ("member", "gx"), None)),
        check_vma=False,
    )
```

```python
import functools
import jax
import jax.numpy as jnp
from jax import lax
from jax.experimental import pallas as pl
from jax.experimental.pallas import tpu as pltpu
from jax.sharding import PartitionSpec as P

F32, BF16 = jnp.float32, jnp.bfloat16
LANES = 128
CHUNK = 256
HALO = 6
NETWORK_VMEM = 60_000_000
ADVECT_VMEM = 8 * 2**20


def round_up(value, unit):
    return -(-value // unit) * unit


def split(value):
    high = value.astype(BF16)
    low = (value - high.astype(F32)).astype(BF16)
    return high, low


def network_kernel(
    *refs, sizes, levels, axis
):
    small_hbm, rest = refs[:10], refs[10:]
    x_hbm, weights_hbm, rest = rest[0], rest[1:7], rest[7:]
    tend_hbm, field, pay_a, pay_b, rest = rest[0], rest[1], rest[2], rest[3], rest[4:]
    x_in, weights_in, rest = rest[0], rest[1:7], rest[7:]
    cats, columns, rest = rest[:6], rest[6:12], rest[12:]
    inverse, tracer, along, across, *biases = rest[:10]
    hold_a, hold_b, w_tail, x_tail, b_six, tend, x_sems, w_sems, out_sems, small_sems = rest[10:]

    width = x_hbm.shape[1]
    chunks = width // CHUNK
    depth_in = sizes[0]
    aligned = depth_in // 8 * 8
    whole = depth_in // LANES * LANES

    def x_copy(c):
        part = pl.ds(c * CHUNK, CHUNK)
        return pltpu.make_async_copy(x_hbm.at[:, part], x_in.at[:, part], x_sems.at[c])

    def w_copy(layer):
        return pltpu.make_async_copy(
            weights_hbm[layer], weights_in[layer], w_sems.at[layer]
        )

    def small_copy(i):
        target = (inverse, tracer, along, across, *biases)[i]
        return pltpu.make_async_copy(small_hbm[i], target, small_sems.at[i])

    def out_copy(c):
        part = pl.ds(c * CHUNK, CHUNK)
        return pltpu.make_async_copy(
            tend.at[:, part], tend_hbm.at[:, part], out_sems.at[c]
        )

    def bias_columns(layer):
        count = sizes[layer + 1]
        source = biases[layer]
        if count % LANES:
            b_six[0:1, :] = jnp.zeros((1, b_six.shape[1]), F32)
            b_six[0:1, 0:count] = source[...].reshape(1, count)
            row = b_six[0:1, :]
        else:
            row = source[...].reshape(1, count)
        scale = 0.5 if layer < 5 else 1.0
        for n in range(0, count, LANES):
            block = jnp.broadcast_to(row[:, n : n + LANES], (LANES, LANES)).T * scale
            keep = min(LANES, count - n)
            columns[layer][n : n + keep, :] = block[:keep]

    def put_weights(layer, rows, start, block):
        depth = cats[layer].shape[1] // 3
        high, low = split(block)
        size = block.shape[1]
        cats[layer][rows, start : start + size] = high
        cats[layer][rows, depth + start : depth + start + size] = high
        cats[layer][rows, 2 * depth + start : 2 * depth + start + size] = low

    def prepare(layer, part, parts):
        count = sizes[layer + 1]
        if layer == 5:
            step = 16
            for n in range(0, count, step):
                if (n // step) % parts == part:
                    put_weights(
                        layer, slice(n, n + step), 0, weights_in[5][n : n + step, :]
                    )
            return
        for n in range(0, count, LANES):
            if (n // LANES) % parts != part:
                continue
            rows = slice(n, n + LANES)
            for k in range(0, sizes[layer], LANES):
                if layer == 0 and k >= whole:
                    block = w_tail[:, n : n + LANES]
                else:
                    block = weights_in[layer][k : k + LANES, n : n + LANES]
                put_weights(layer, rows, k, block.T * 0.5)

    def put_rows(hold, depth, start, cols, value):
        high, low = split(value)
        size = value.shape[0]
        hold[start : start + size, cols] = high
        hold[depth + start : depth + start + size, cols] = low
        hold[2 * depth + start : 2 * depth + start + size, cols] = high

    w_copy(0).start()
    x_copy(0).start()
    for c in range(1, chunks):
        x_copy(c).start()
    for i in range(10):
        small_copy(i).start()
    w_copy(1).start()
    w_tail[...] = jnp.zeros(w_tail.shape, F32)
    x_tail[...] = jnp.zeros(x_tail.shape, F32)
    w_copy(0).wait()
    w_tail[0 : aligned - whole, :] = weights_in[0][whole:aligned, :]
    w_tail[aligned - whole : depth_in - whole, :] = weights_in[0][aligned:depth_in, :]
    prepare(0, 0, 1)
    depth_pad = cats[0].shape[1] // 3
    for layer in range(2, 6):
        w_copy(layer).start()
    for c in range(chunks):
        x_copy(c).wait()
        cols = slice(c * CHUNK, (c + 1) * CHUNK)
        x_tail[0 : aligned - whole, cols] = x_in[whole:aligned, cols]
        x_tail[aligned - whole : depth_in - whole, cols] = x_in[aligned:depth_in, cols]
        for k in range(0, whole, LANES):
            put_rows(hold_a, depth_pad, k, cols, x_in[k : k + LANES, cols])
        put_rows(hold_a, depth_pad, whole, cols, x_tail[:, cols])

    for i in range(10):
        small_copy(i).wait()
    for layer in range(6):
        bias_columns(layer)
    rows, levels_wide = field.shape[0], field.shape[1]
    for r in range(rows):
        field[r, levels : levels + 1, :] = along[r : r + 1, :]
        field[r, levels + 1 : levels + 2, :] = across[r : r + 1, :]
        field[r, levels + 2 : levels_wide, :] = jnp.zeros(
            (levels_wide - levels - 2, LANES), F32
        )
    held, other = hold_a, hold_b
    for layer in range(6):
        if layer + 1 < 6:
            w_copy(layer + 1).wait()
        count = sizes[layer + 1]
        deep = cats[layer].shape[1]
        for c in range(chunks):
            cols = slice(c * CHUNK, (c + 1) * CHUNK)
            total = jnp.dot(
                cats[layer][...], held[0:deep, cols], preferred_element_type=F32
            )
            if layer + 1 < 6:
                prepare(layer + 1, c, chunks)
            bias = columns[layer][...]
            bias = jnp.concatenate([bias, bias], axis=1)
            value = total + bias
            if layer < 5:
                value = value + value * jnp.tanh(value)
                put_rows(other, count, 0, cols, value)
            else:
                for half in range(CHUNK // LANES):
                    r = c * (CHUNK // LANES) + half
                    day = inverse[r : r + 1, :] >= 0
                    shown = jnp.where(
                        day, value[:, half * LANES : (half + 1) * LANES], 0.0
                    )
                    tend[:, r * LANES : (r + 1) * LANES] = shown
                    field[r, 0:levels, :] = (
                        tracer[pl.ds(r, levels, stride=rows), :] + shown[0:levels]
                    )
                out_copy(c).start()
        held, other = other, held

    odd = lax.rem(lax.axis_index(axis), 2)
    pay_a[...] = field[pl.ds((rows - HALO) * odd, HALO)]
    pay_b[...] = field[pl.ds((rows - HALO) * (1 - odd), HALO)]
    for c in range(chunks):
        out_copy(c).wait()


def network(inverse, tracer, along, across, biases, x, weights, axis):
    sizes = [x.shape[0]] + [b.shape[0] for b in biases]
    width = x.shape[1]
    rows = along.shape[0]
    levels = tracer.shape[0] // rows
    levels_wide = round_up(levels + 2, 8)
    chunks = width // CHUNK
    padded = [round_up(s, LANES) for s in sizes[:6]]
    deepest = 3 * max(padded)
    tail = padded[0] - sizes[0] // LANES * LANES
    vmem, hbm = pl.BlockSpec(memory_space=pltpu.VMEM), pl.BlockSpec(memory_space=pl.ANY)
    total = sum(sizes[i] * sizes[i + 1] for i in range(6)) * width
    return pl.pallas_call(
        functools.partial(network_kernel, sizes=sizes, levels=levels, axis=axis),
        out_shape=(
            jax.ShapeDtypeStruct((sizes[6], width), F32),
            jax.ShapeDtypeStruct((rows, levels_wide, LANES), F32),
            jax.ShapeDtypeStruct((HALO, levels_wide, LANES), F32),
            jax.ShapeDtypeStruct((HALO, levels_wide, LANES), F32),
        ),
        in_specs=[hbm] * 17,
        out_specs=(hbm, vmem, vmem, vmem),
        scratch_shapes=[
            pltpu.VMEM(x.shape, F32),
            *[pltpu.VMEM(w.shape, F32) for w in weights],
            *[pltpu.VMEM((sizes[i + 1], 3 * padded[i]), BF16) for i in range(6)],
            *[pltpu.VMEM((sizes[i + 1], LANES), F32) for i in range(6)],
            pltpu.VMEM(inverse.shape, jnp.int32),
            pltpu.VMEM(tracer.shape, F32),
            pltpu.VMEM(along.shape, F32),
            pltpu.VMEM(across.shape, F32),
            *[pltpu.VMEM(b.shape, F32) for b in biases],
            pltpu.VMEM((deepest, width), BF16),
            pltpu.VMEM((deepest, width), BF16),
            pltpu.VMEM((tail, sizes[1]), F32),
            pltpu.VMEM((tail, width), F32),
            pltpu.VMEM((8, round_up(sizes[6], LANES)), F32),
            pltpu.VMEM((sizes[6], width), F32),
            pltpu.SemaphoreType.DMA((chunks,)),
            pltpu.SemaphoreType.DMA((6,)),
            pltpu.SemaphoreType.DMA((chunks,)),
            pltpu.SemaphoreType.DMA((10,)),
        ],
        compiler_params=pltpu.CompilerParams(vmem_limit_bytes=NETWORK_VMEM),
        cost_estimate=pl.CostEstimate(
            flops=6 * total, bytes_accessed=14_000_000, transcendentals=3_000_000
        ),
        name="column_network",
    )(inverse, tracer, along, across, *biases, x, *weights)


def half_minmod(first, second):
    return 0.5 * (
        jnp.maximum(jnp.minimum(first, second), 0.0)
        + jnp.minimum(jnp.maximum(first, second), 0.0)
    )


def operator(row, along, across):
    step = functools.cache(lambda i: row(i) - row(i - 1))
    slope = functools.cache(lambda i: half_minmod(step(i + 1), step(i)))

    @functools.cache
    def flux(i):
        ahead, behind = along(i)
        return ahead * (row(i - 1) + slope(i - 1)) + behind * (row(i) - slope(i))

    def change(i):
        here = row(i)
        back = here - pltpu.roll(here, 1, 1)
        bend = half_minmod(pltpu.roll(back, LANES - 1, 1), back)
        ahead, behind = across(i)
        side = ahead * pltpu.roll(here + bend, 1, 1) + behind * (here - bend)
        return (flux(i) - flux(i + 1)) + (side - pltpu.roll(side, LANES - 1, 1))

    return change


def advect_kernel(field, got_a, got_b, out, wide, speeds, *, levels, axis):
    rows = field.shape[0]
    odd = lax.rem(lax.axis_index(axis), 2)
    wide[HALO : HALO + rows] = field[...]
    wide[pl.ds((HALO + rows) * odd, HALO)] = got_a[...]
    wide[pl.ds((HALO + rows) * (1 - odd), HALO)] = got_b[...]
    for i in range(rows + 2 * HALO):
        for kind in range(2):
            courant = jnp.broadcast_to(
                wide[i, levels + kind : levels + kind + 1, :], (8, LANES)
            )
            speeds[2 * kind, i] = jnp.maximum(courant, 0.0)
            speeds[2 * kind + 1, i] = jnp.minimum(courant, 0.0)
    for base in range(0, levels, 8):
        along = lambda i: (speeds[0, i + HALO], speeds[1, i + HALO])
        across = lambda i: (speeds[2, i + HALO], speeds[3, i + HALO])

        @functools.cache
        def start(i):
            return wide[i + HALO, base : base + 8, :]

        first = operator(start, along, across)
        one = functools.cache(lambda i: start(i) + first(i))
        second = operator(one, along, across)
        two = functools.cache(
            lambda i: 0.75 * start(i) + 0.25 * (one(i) + second(i))
        )
        third = operator(two, along, across)
        keep = min(8, levels - base)
        for i in range(rows):
            value = 1.0 / 3.0 * start(i) + 2.0 / 3.0 * (two(i) + third(i))
            out[pl.ds(base * rows + i, keep, stride=rows), :] = value[:keep]


def advect(field, got_a, got_b, levels, axis):
    rows, levels_wide, across = field.shape
    vmem = pl.BlockSpec(memory_space=pltpu.VMEM)
    return pl.pallas_call(
        functools.partial(advect_kernel, levels=levels, axis=axis),
        out_shape=jax.ShapeDtypeStruct((levels * rows, across), F32),
        in_specs=[vmem] * 3,
        out_specs=vmem,
        scratch_shapes=[
            pltpu.VMEM((rows + 2 * HALO, levels_wide, across), F32),
            pltpu.VMEM((4, rows + 2 * HALO, 8, across), F32),
        ],
        compiler_params=pltpu.CompilerParams(vmem_limit_bytes=ADVECT_VMEM),
        name="advect_sections",
    )(field, got_a, got_b)


def shards(inputs, tracer, speed_along, speed_across, inverse_list, *params):
    weights, biases = list(params[0::2]), params[1::2]
    weights[5] = weights[5].T
    levels, rows, across = tracer.shape
    tendencies, field, pay_a, pay_b = network(
        inverse_list.reshape(rows, across),
        tracer.reshape(levels * rows, across),
        speed_along,
        speed_across,
        biases,
        inputs.T,
        weights,
        "gx",
    )
    count = lax.axis_size("gx")
    outer = [(i, (i - 1 if i % 2 == 0 else i + 1) % count) for i in range(count)]
    inner = [(i, i + 1 if i % 2 == 0 else i - 1) for i in range(count)]
    got_a = lax.ppermute(pay_a, "gx", outer)
    got_b = lax.ppermute(pay_b, "gx", inner)
    advected = advect(field, got_a, got_b, levels, "gx")
    return tendencies.T, advected.reshape(levels, rows, across)


def solution(mesh):
    placed = (
        P(("member", "gx"), None),
        P(None, ("member", "gx"), None),
        P(("member", "gx"), None),
        P(("member", "gx"), None),
        P(("member", "gx")),
        *[P()] * 12,
    )
    return jax.shard_map(
        shards,
        mesh=mesh,
        in_specs=placed,
        out_specs=(P(("member", "gx"), None), P(None, ("member", "gx"), None)),
        check_vma=False,
    )
```

```python
import functools
import jax
import jax.numpy as jnp
from jax import lax
from jax.experimental import pallas as pl
from jax.experimental.pallas import tpu as pltpu
from jax.sharding import PartitionSpec as P

F32, BF16 = jnp.float32, jnp.bfloat16
LANES = 128
CHUNK = 512
HALO = 6
GROUP = 64
NETWORK_VMEM = 60_000_000
ADVECT_VMEM = 8 * 2**20


def round_up(value, unit):
    return -(-value // unit) * unit


def split(value):
    high = value.astype(BF16)
    low = (value - high.astype(F32)).astype(BF16)
    return high, low


def network_kernel(
    *refs, sizes, levels, axis
):
    small_hbm, rest = refs[:10], refs[10:]
    x_hbm, weights_hbm, rest = rest[0], rest[1:7], rest[7:]
    tend_hbm, field, pay_a, pay_b, rest = rest[0], rest[1], rest[2], rest[3], rest[4:]
    x_in, weights_in, rest = rest[0], rest[1:7], rest[7:]
    cats, columns, rest = rest[:6], rest[6:12], rest[12:]
    inverse, tracer, along, across, *biases = rest[:10]
    hold_a, hold_b, w_tail, x_tail, b_six, tend, x_sems, w_sems, out_sems, small_sems = rest[10:]

    width = x_hbm.shape[1]
    chunks = width // CHUNK
    depth_in = sizes[0]
    aligned = depth_in // 8 * 8
    whole = depth_in // LANES * LANES

    def x_copy(c):
        part = pl.ds(c * CHUNK, CHUNK)
        return pltpu.make_async_copy(x_hbm.at[:, part], x_in.at[:, part], x_sems.at[c])

    def w_copy(layer):
        return pltpu.make_async_copy(
            weights_hbm[layer], weights_in[layer], w_sems.at[layer]
        )

    def small_copy(i):
        target = (inverse, tracer, along, across, *biases)[i]
        return pltpu.make_async_copy(small_hbm[i], target, small_sems.at[i])

    def out_copy(c):
        part = pl.ds(c * CHUNK, CHUNK)
        return pltpu.make_async_copy(
            tend.at[:, part], tend_hbm.at[:, part], out_sems.at[c]
        )

    def bias_columns(layer):
        count = sizes[layer + 1]
        source = biases[layer]
        if count % LANES:
            b_six[0:1, :] = jnp.zeros((1, b_six.shape[1]), F32)
            b_six[0:1, 0:count] = source[...].reshape(1, count)
            row = b_six[0:1, :]
        else:
            row = source[...].reshape(1, count)
        scale = 0.5 if layer < 5 else 1.0
        for n in range(0, count, LANES):
            block = jnp.broadcast_to(row[:, n : n + LANES], (LANES, LANES)).T * scale
            keep = min(LANES, count - n)
            columns[layer][n : n + keep, :] = block[:keep]

    def put_weights(layer, rows, start, block):
        depth = cats[layer].shape[1] // 3
        high, low = split(block)
        size = block.shape[1]
        cats[layer][rows, start : start + size] = high
        cats[layer][rows, depth + start : depth + start + size] = high
        cats[layer][rows, 2 * depth + start : 2 * depth + start + size] = low

    def prepare(layer, part, parts):
        count = sizes[layer + 1]
        if layer == 5:
            step = 16
            for n in range(0, count, step):
                if (n // step) % parts == part:
                    put_weights(
                        layer, slice(n, n + step), 0, weights_in[5][n : n + step, :]
                    )
            return
        for n in range(0, count, LANES):
            if (n // LANES) % parts != part:
                continue
            rows = slice(n, n + LANES)
            for k in range(0, sizes[layer], LANES):
                if layer == 0 and k >= whole:
                    block = w_tail[:, n : n + LANES]
                else:
                    block = weights_in[layer][k : k + LANES, n : n + LANES]
                put_weights(layer, rows, k, block.T * 0.5)

    def put_rows(hold, depth, start, cols, value):
        high, low = split(value)
        size = value.shape[0]
        hold[start : start + size, cols] = high
        hold[depth + start : depth + start + size, cols] = low
        hold[2 * depth + start : 2 * depth + start + size, cols] = high

    w_copy(0).start()
    x_copy(0).start()
    for c in range(1, chunks):
        x_copy(c).start()
    for i in range(10):
        small_copy(i).start()
    w_copy(1).start()
    w_tail[...] = jnp.zeros(w_tail.shape, F32)
    x_tail[...] = jnp.zeros(x_tail.shape, F32)
    w_copy(0).wait()
    w_tail[0 : aligned - whole, :] = weights_in[0][whole:aligned, :]
    w_tail[aligned - whole : depth_in - whole, :] = weights_in[0][aligned:depth_in, :]
    prepare(0, 0, 1)
    depth_pad = cats[0].shape[1] // 3
    for layer in range(2, 6):
        w_copy(layer).start()
    for c in range(chunks):
        x_copy(c).wait()
        cols = slice(c * CHUNK, (c + 1) * CHUNK)
        x_tail[0 : aligned - whole, cols] = x_in[whole:aligned, cols]
        x_tail[aligned - whole : depth_in - whole, cols] = x_in[aligned:depth_in, cols]
        for k in range(0, whole, LANES):
            put_rows(hold_a, depth_pad, k, cols, x_in[k : k + LANES, cols])
        put_rows(hold_a, depth_pad, whole, cols, x_tail[:, cols])

    for i in range(10):
        small_copy(i).wait()
    for layer in range(6):
        bias_columns(layer)
    rows, levels_wide = field.shape[0], field.shape[1]
    for r in range(rows):
        field[r, levels : levels + 1, :] = along[r : r + 1, :]
        field[r, levels + 1 : levels + 2, :] = across[r : r + 1, :]
        field[r, levels + 2 : levels_wide, :] = jnp.zeros(
            (levels_wide - levels - 2, LANES), F32
        )
    held, other = hold_a, hold_b
    for layer in range(6):
        if layer + 1 < 6:
            w_copy(layer + 1).wait()
        count = sizes[layer + 1]
        deep = cats[layer].shape[1]
        for c in range(chunks):
            cols = slice(c * CHUNK, (c + 1) * CHUNK)
            total = jnp.dot(
                cats[layer][...], held[0:deep, cols], preferred_element_type=F32
            )
            if layer + 1 < 6:
                prepare(layer + 1, c, chunks)
            bias = columns[layer][...]
            bias = jnp.concatenate([bias] * (CHUNK // LANES), axis=1)
            value = total + bias
            if layer < 5:
                value = value + value * jnp.tanh(value)
                put_rows(other, count, 0, cols, value)
            else:
                for half in range(CHUNK // LANES):
                    r = c * (CHUNK // LANES) + half
                    day = inverse[r : r + 1, :] >= 0
                    shown = jnp.where(
                        day, value[:, half * LANES : (half + 1) * LANES], 0.0
                    )
                    tend[:, r * LANES : (r + 1) * LANES] = shown
                    field[r, 0:levels, :] = (
                        tracer[pl.ds(r, levels, stride=rows), :] + shown[0:levels]
                    )
                out_copy(c).start()
        held, other = other, held

    odd = lax.rem(lax.axis_index(axis), 2)
    pay_a[...] = field[pl.ds((rows - HALO) * odd, HALO)]
    pay_b[...] = field[pl.ds((rows - HALO) * (1 - odd), HALO)]
    for c in range(chunks):
        out_copy(c).wait()


def network(inverse, tracer, along, across, biases, x, weights, axis):
    sizes = [x.shape[0]] + [b.shape[0] for b in biases]
    width = x.shape[1]
    rows = along.shape[0]
    levels = tracer.shape[0] // rows
    levels_wide = round_up(levels + 2, 8)
    chunks = width // CHUNK
    padded = [round_up(s, LANES) for s in sizes[:6]]
    deepest = 3 * max(padded)
    tail = padded[0] - sizes[0] // LANES * LANES
    vmem, hbm = pl.BlockSpec(memory_space=pltpu.VMEM), pl.BlockSpec(memory_space=pl.ANY)
    total = sum(sizes[i] * sizes[i + 1] for i in range(6)) * width
    return pl.pallas_call(
        functools.partial(network_kernel, sizes=sizes, levels=levels, axis=axis),
        out_shape=(
            jax.ShapeDtypeStruct((sizes[6], width), F32),
            jax.ShapeDtypeStruct((rows, levels_wide, LANES), F32),
            jax.ShapeDtypeStruct((HALO, levels_wide, LANES), F32),
            jax.ShapeDtypeStruct((HALO, levels_wide, LANES), F32),
        ),
        in_specs=[hbm] * 17,
        out_specs=(hbm, vmem, vmem, vmem),
        scratch_shapes=[
            pltpu.VMEM(x.shape, F32),
            *[pltpu.VMEM(w.shape, F32) for w in weights],
            *[pltpu.VMEM((sizes[i + 1], 3 * padded[i]), BF16) for i in range(6)],
            *[pltpu.VMEM((sizes[i + 1], LANES), F32) for i in range(6)],
            pltpu.VMEM(inverse.shape, jnp.int32),
            pltpu.VMEM(tracer.shape, F32),
            pltpu.VMEM(along.shape, F32),
            pltpu.VMEM(across.shape, F32),
            *[pltpu.VMEM(b.shape, F32) for b in biases],
            pltpu.VMEM((deepest, width), BF16),
            pltpu.VMEM((deepest, width), BF16),
            pltpu.VMEM((tail, sizes[1]), F32),
            pltpu.VMEM((tail, width), F32),
            pltpu.VMEM((8, round_up(sizes[6], LANES)), F32),
            pltpu.VMEM((sizes[6], width), F32),
            pltpu.SemaphoreType.DMA((chunks,)),
            pltpu.SemaphoreType.DMA((6,)),
            pltpu.SemaphoreType.DMA((chunks,)),
            pltpu.SemaphoreType.DMA((10,)),
        ],
        compiler_params=pltpu.CompilerParams(vmem_limit_bytes=NETWORK_VMEM),
        cost_estimate=pl.CostEstimate(
            flops=6 * total, bytes_accessed=14_000_000, transcendentals=3_000_000
        ),
        name="column_network",
    )(inverse, tracer, along, across, *biases, x, *weights)


def half_minmod(first, second):
    return 0.5 * (
        jnp.maximum(jnp.minimum(first, second), 0.0)
        + jnp.minimum(jnp.maximum(first, second), 0.0)
    )


def operator(row, along, across):
    step = functools.cache(lambda i: row(i) - row(i - 1))
    slope = functools.cache(lambda i: half_minmod(step(i + 1), step(i)))

    @functools.cache
    def flux(i):
        ahead, behind = along(i)
        return ahead * (row(i - 1) + slope(i - 1)) + behind * (row(i) - slope(i))

    def change(i):
        here = row(i)
        back = here - pltpu.roll(here, 1, 2)
        bend = half_minmod(pltpu.roll(back, LANES - 1, 2), back)
        ahead, behind = across(i)
        side = ahead * pltpu.roll(here + bend, 1, 2) + behind * (here - bend)
        return (flux(i) - flux(i + 1)) + (side - pltpu.roll(side, LANES - 1, 2))

    return change


def advect_kernel(field, got_a, got_b, out, wide, speeds, *, levels, axis):
    rows = field.shape[0]
    odd = lax.rem(lax.axis_index(axis), 2)
    wide[HALO : HALO + rows] = field[...]
    wide[pl.ds((HALO + rows) * odd, HALO)] = got_a[...]
    wide[pl.ds((HALO + rows) * (1 - odd), HALO)] = got_b[...]
    for i in range(rows + 2 * HALO):
        for kind in range(2):
            courant = jnp.broadcast_to(
                wide[i, levels + kind : levels + kind + 1, :], (8, LANES)
            )
            speeds[2 * kind, i] = jnp.maximum(courant, 0.0)
            speeds[2 * kind + 1, i] = jnp.minimum(courant, 0.0)
    for base in range(0, levels, GROUP):
        blocks = -(-min(GROUP, levels - base) // 8)
        along = lambda i: (speeds[0, i + HALO], speeds[1, i + HALO])
        across = lambda i: (speeds[2, i + HALO], speeds[3, i + HALO])

        @functools.cache
        def start(i):
            rows_here = wide[i + HALO, base : base + 8 * blocks, :]
            return rows_here.reshape(blocks, 8, LANES)

        first = operator(start, along, across)
        one = functools.cache(lambda i: start(i) + first(i))
        second = operator(one, along, across)
        two = functools.cache(
            lambda i: 0.75 * start(i) + 0.25 * (one(i) + second(i))
        )
        third = operator(two, along, across)
        keep = min(GROUP, levels - base)
        for i in range(rows):
            value = 1.0 / 3.0 * start(i) + 2.0 / 3.0 * (two(i) + third(i))
            value = value.reshape(8 * blocks, LANES)
            out[pl.ds(base * rows + i, keep, stride=rows), :] = value[:keep]


def advect(field, got_a, got_b, levels, axis):
    rows, levels_wide, across = field.shape
    vmem = pl.BlockSpec(memory_space=pltpu.VMEM)
    return pl.pallas_call(
        functools.partial(advect_kernel, levels=levels, axis=axis),
        out_shape=jax.ShapeDtypeStruct((levels * rows, across), F32),
        in_specs=[vmem] * 3,
        out_specs=vmem,
        scratch_shapes=[
            pltpu.VMEM((rows + 2 * HALO, levels_wide, across), F32),
            pltpu.VMEM((4, rows + 2 * HALO, 8, across), F32),
        ],
        compiler_params=pltpu.CompilerParams(vmem_limit_bytes=ADVECT_VMEM),
        name="advect_sections",
    )(field, got_a, got_b)


def shards(inputs, tracer, speed_along, speed_across, inverse_list, *params):
    weights, biases = list(params[0::2]), params[1::2]
    weights[5] = weights[5].T
    levels, rows, across = tracer.shape
    tendencies, field, pay_a, pay_b = network(
        inverse_list.reshape(rows, across),
        tracer.reshape(levels * rows, across),
        speed_along,
        speed_across,
        biases,
        inputs.T,
        weights,
        "gx",
    )
    count = lax.axis_size("gx")
    outer = [(i, (i - 1 if i % 2 == 0 else i + 1) % count) for i in range(count)]
    inner = [(i, i + 1 if i % 2 == 0 else i - 1) for i in range(count)]
    got_a = lax.ppermute(pay_a, "gx", outer)
    got_b = lax.ppermute(pay_b, "gx", inner)
    advected = advect(field, got_a, got_b, levels, "gx")
    return tendencies.T, advected.reshape(levels, rows, across)


def solution(mesh):
    placed = (
        P(("member", "gx"), None),
        P(None, ("member", "gx"), None),
        P(("member", "gx"), None),
        P(("member", "gx"), None),
        P(("member", "gx")),
        *[P()] * 12,
    )
    return jax.shard_map(
        shards,
        mesh=mesh,
        in_specs=placed,
        out_specs=(P(("member", "gx"), None), P(None, ("member", "gx"), None)),
        check_vma=False,
    )
```

```python
import functools
import jax
import jax.numpy as jnp
from jax import lax
from jax.experimental import pallas as pl
from jax.experimental.pallas import tpu as pltpu
from jax.sharding import PartitionSpec as P

F32, BF16 = jnp.float32, jnp.bfloat16
LANES = 128
CHUNK = 512
HALO = 6
GROUP = 64
FIRST = 256
NETWORK_VMEM = 60_000_000
ADVECT_VMEM = 8 * 2**20


def round_up(value, unit):
    return -(-value // unit) * unit


def split(value):
    high = value.astype(BF16)
    low = (value - high.astype(F32)).astype(BF16)
    return high, low


def network_kernel(
    *refs, sizes, levels, axis
):
    small_hbm, rest = refs[:10], refs[10:]
    x_hbm, weights_hbm, rest = rest[0], rest[1:7], rest[7:]
    tend_hbm, field, pay_a, pay_b, rest = rest[0], rest[1], rest[2], rest[3], rest[4:]
    x_in, weights_in, rest = rest[0], rest[1:7], rest[7:]
    cats, columns, rest = rest[:6], rest[6:12], rest[12:]
    inverse, tracer, along, across, *biases = rest[:10]
    hold_a, hold_b, w_tail, x_tail, b_six, tend, x_sems, w_sems, out_sems, small_sems, first_sems = rest[10:]

    width = x_hbm.shape[1]
    chunks = width // CHUNK
    depth_in = sizes[0]
    aligned = depth_in // 8 * 8
    whole = depth_in // LANES * LANES

    def x_copy(c):
        part = pl.ds(c * CHUNK, CHUNK)
        return pltpu.make_async_copy(x_hbm.at[:, part], x_in.at[:, part], x_sems.at[c])

    def w_copy(layer):
        return pltpu.make_async_copy(
            weights_hbm[layer], weights_in[layer], w_sems.at[layer]
        )

    def small_copy(i):
        target = (inverse, tracer, along, across, *biases)[i]
        return pltpu.make_async_copy(small_hbm[i], target, small_sems.at[i])

    def out_copy(c):
        part = pl.ds(c * CHUNK, CHUNK)
        return pltpu.make_async_copy(
            tend.at[:, part], tend_hbm.at[:, part], out_sems.at[c]
        )

    def bias_columns(layer):
        count = sizes[layer + 1]
        source = biases[layer]
        if count % LANES:
            b_six[0:1, :] = jnp.zeros((1, b_six.shape[1]), F32)
            b_six[0:1, 0:count] = source[...].reshape(1, count)
            row = b_six[0:1, :]
        else:
            row = source[...].reshape(1, count)
        scale = 0.5 if layer < 5 else 1.0
        for n in range(0, count, LANES):
            block = jnp.broadcast_to(row[:, n : n + LANES], (LANES, LANES)).T * scale
            keep = min(LANES, count - n)
            columns[layer][n : n + keep, :] = block[:keep]

    def put_weights(layer, rows, start, block):
        depth = cats[layer].shape[1] // 3
        high, low = split(block)
        size = block.shape[1]
        cats[layer][rows, start : start + size] = high
        cats[layer][rows, depth + start : depth + start + size] = high
        cats[layer][rows, 2 * depth + start : 2 * depth + start + size] = low

    def prepare(layer, part, parts):
        count = sizes[layer + 1]
        if layer == 5:
            step = 16
            for n in range(0, count, step):
                if (n // step) % parts == part:
                    put_weights(
                        layer, slice(n, n + step), 0, weights_in[5][n : n + step, :]
                    )
            return
        for n in range(0, count, LANES):
            if (n // LANES) % parts != part:
                continue
            rows = slice(n, n + LANES)
            for k in range(0, sizes[layer], LANES):
                block = weights_in[layer][k : k + LANES, n : n + LANES]
                put_weights(layer, rows, k, block.T * 0.5)

    def put_rows(hold, depth, start, cols, value):
        high, low = split(value)
        size = value.shape[0]
        hold[start : start + size, cols] = high
        hold[depth + start : depth + start + size, cols] = low
        hold[2 * depth + start : 2 * depth + start + size, cols] = high

    def prepare_inputs(c):
        cols = slice(c * CHUNK, (c + 1) * CHUNK)
        x_tail[0 : aligned - whole, cols] = x_in[whole:aligned, cols]
        x_tail[aligned - whole : depth_in - whole, cols] = x_in[aligned:depth_in, cols]
        for k in range(0, whole, LANES):
            put_rows(hold_a, depth_pad, k, cols, x_in[k : k + LANES, cols])
        put_rows(hold_a, depth_pad, whole, cols, x_tail[:, cols])

    def place_speeds():
        for r in range(rows):
            field[r, levels : levels + 1, :] = along[r : r + 1, :]
            field[r, levels + 1 : levels + 2, :] = across[r : r + 1, :]
            field[r, levels + 2 : levels_wide, :] = jnp.zeros(
                (levels_wide - levels - 2, LANES), F32
            )

    def product(layer, held, c, lines):
        deep = cats[layer].shape[1]
        cols = slice(c * CHUNK, (c + 1) * CHUNK)
        return jnp.dot(
            cats[layer][lines, :], held[0:deep, cols], preferred_element_type=F32
        )

    def finish(layer, other, c, lines, total):
        bias = columns[layer][lines, :]
        value = total + jnp.concatenate([bias] * (CHUNK // LANES), axis=1)
        if layer < 5:
            value = value + value * jnp.tanh(value)
            cols = slice(c * CHUNK, (c + 1) * CHUNK)
            put_rows(other, sizes[layer + 1], lines.start, cols, value)
            return
        for part in range(CHUNK // LANES):
            r = c * (CHUNK // LANES) + part
            day = inverse[r : r + 1, :] >= 0
            shown = jnp.where(day, value[:, part * LANES : (part + 1) * LANES], 0.0)
            tend[:, r * LANES : (r + 1) * LANES] = shown
            field[r, 0:levels, :] = (
                tracer[pl.ds(r, levels, stride=rows), :] + shown[0:levels]
            )
        out_copy(c).start()

    def first_copy(n):
        part = pl.ds(n * FIRST, FIRST)
        return pltpu.make_async_copy(
            weights_hbm[0].at[:, part], weights_in[0].at[:, part], first_sems.at[n]
        )

    def prepare_first(n):
        part = slice(n * FIRST, (n + 1) * FIRST)
        w_tail[0 : aligned - whole, part] = weights_in[0][whole:aligned, part]
        w_tail[aligned - whole : depth_in - whole, part] = weights_in[0][
            aligned:depth_in, part
        ]
        for k in range(0, padded_in, LANES):
            for m in range(n * FIRST, (n + 1) * FIRST, LANES):
                if k >= whole:
                    block = w_tail[:, m : m + LANES]
                else:
                    block = weights_in[0][k : k + LANES, m : m + LANES]
                put_weights(0, slice(m, m + LANES), k, block.T * 0.5)

    rows, levels_wide = field.shape[0], field.shape[1]
    padded_in = cats[0].shape[1] // 3
    depth_pad = padded_in
    first_parts = sizes[1] // FIRST
    x_copy(0).start()
    for n in range(first_parts):
        first_copy(n).start()
    for c in range(1, chunks):
        x_copy(c).start()
    w_tail[...] = jnp.zeros(w_tail.shape, F32)
    x_tail[...] = jnp.zeros(x_tail.shape, F32)
    x_copy(0).wait()
    prepare_inputs(0)
    first_copy(0).wait()
    prepare_first(0)
    for i in range(10):
        small_copy(i).start()
    for layer in range(1, 6):
        w_copy(layer).start()

    pending = None
    held, other = hold_a, hold_b
    for n in range(first_parts):
        lines = slice(n * FIRST, (n + 1) * FIRST)
        for c in range(chunks):
            total = product(0, held, c, lines)
            if n == 0 and c + 1 < chunks:
                x_copy(c + 1).wait()
                prepare_inputs(c + 1)
            elif n == 0:
                for i in range(10):
                    small_copy(i).wait()
                bias_columns(0)
                bias_columns(1)
            if c + 1 == chunks and n + 1 < first_parts:
                first_copy(n + 1).wait()
                prepare_first(n + 1)
            if n + 1 == first_parts:
                if c == 0:
                    w_copy(1).wait()
                prepare(1, c, chunks)
            if pending is not None:
                finish(*pending)
            pending = (0, other, c, lines, total)
    held, other = other, held
    for layer in range(1, 6):
        lines = slice(0, sizes[layer + 1])
        if layer < 5:
            w_copy(layer + 1).wait()
        for c in range(chunks):
            total = product(layer, held, c, lines)
            if layer < 5:
                prepare(layer + 1, c, chunks)
                if c == 0:
                    bias_columns(layer + 1)
            elif c == 0:
                place_speeds()
            finish(*pending)
            pending = (layer, other, c, lines, total)
        held, other = other, held
    finish(*pending)

    odd = lax.rem(lax.axis_index(axis), 2)
    pay_a[...] = field[pl.ds((rows - HALO) * odd, HALO)]
    pay_b[...] = field[pl.ds((rows - HALO) * (1 - odd), HALO)]
    for c in range(chunks):
        out_copy(c).wait()


def network(inverse, tracer, along, across, biases, x, weights, axis):
    sizes = [x.shape[0]] + [b.shape[0] for b in biases]
    width = x.shape[1]
    rows = along.shape[0]
    levels = tracer.shape[0] // rows
    levels_wide = round_up(levels + 2, 8)
    chunks = width // CHUNK
    padded = [round_up(s, LANES) for s in sizes[:6]]
    deepest = 3 * max(padded)
    tail = padded[0] - sizes[0] // LANES * LANES
    vmem, hbm = pl.BlockSpec(memory_space=pltpu.VMEM), pl.BlockSpec(memory_space=pl.ANY)
    total = sum(sizes[i] * sizes[i + 1] for i in range(6)) * width
    return pl.pallas_call(
        functools.partial(network_kernel, sizes=sizes, levels=levels, axis=axis),
        out_shape=(
            jax.ShapeDtypeStruct((sizes[6], width), F32),
            jax.ShapeDtypeStruct((rows, levels_wide, LANES), F32),
            jax.ShapeDtypeStruct((HALO, levels_wide, LANES), F32),
            jax.ShapeDtypeStruct((HALO, levels_wide, LANES), F32),
        ),
        in_specs=[hbm] * 17,
        out_specs=(hbm, vmem, vmem, vmem),
        scratch_shapes=[
            pltpu.VMEM(x.shape, F32),
            *[pltpu.VMEM(w.shape, F32) for w in weights],
            *[pltpu.VMEM((sizes[i + 1], 3 * padded[i]), BF16) for i in range(6)],
            *[pltpu.VMEM((sizes[i + 1], LANES), F32) for i in range(6)],
            pltpu.VMEM(inverse.shape, jnp.int32),
            pltpu.VMEM(tracer.shape, F32),
            pltpu.VMEM(along.shape, F32),
            pltpu.VMEM(across.shape, F32),
            *[pltpu.VMEM(b.shape, F32) for b in biases],
            pltpu.VMEM((deepest, width), BF16),
            pltpu.VMEM((deepest, width), BF16),
            pltpu.VMEM((tail, sizes[1]), F32),
            pltpu.VMEM((tail, width), F32),
            pltpu.VMEM((8, round_up(sizes[6], LANES)), F32),
            pltpu.VMEM((sizes[6], width), F32),
            pltpu.SemaphoreType.DMA((chunks,)),
            pltpu.SemaphoreType.DMA((6,)),
            pltpu.SemaphoreType.DMA((chunks,)),
            pltpu.SemaphoreType.DMA((10,)),
            pltpu.SemaphoreType.DMA((sizes[1] // FIRST,)),
        ],
        compiler_params=pltpu.CompilerParams(vmem_limit_bytes=NETWORK_VMEM),
        cost_estimate=pl.CostEstimate(
            flops=6 * total, bytes_accessed=14_000_000, transcendentals=3_000_000
        ),
        name="column_network",
    )(inverse, tracer, along, across, *biases, x, *weights)


def half_minmod(first, second):
    return 0.5 * (
        jnp.maximum(jnp.minimum(first, second), 0.0)
        + jnp.minimum(jnp.maximum(first, second), 0.0)
    )


def operator(row, along, across):
    step = functools.cache(lambda i: row(i) - row(i - 1))
    slope = functools.cache(lambda i: half_minmod(step(i + 1), step(i)))

    @functools.cache
    def flux(i):
        ahead, behind = along(i)
        return ahead * (row(i - 1) + slope(i - 1)) + behind * (row(i) - slope(i))

    def change(i):
        here = row(i)
        back = here - pltpu.roll(here, 1, 2)
        bend = half_minmod(pltpu.roll(back, LANES - 1, 2), back)
        ahead, behind = across(i)
        side = ahead * pltpu.roll(here + bend, 1, 2) + behind * (here - bend)
        return (flux(i) - flux(i + 1)) + (side - pltpu.roll(side, LANES - 1, 2))

    return change


def advect_kernel(field, got_a, got_b, out, wide, speeds, sem, *, levels, axis):
    rows = field.shape[0]
    odd = lax.rem(lax.axis_index(axis), 2)
    own = pltpu.make_async_copy(field, wide.at[pl.ds(HALO, rows)], sem)
    own.start()
    wide[pl.ds((HALO + rows) * odd, HALO)] = got_a[...]
    wide[pl.ds((HALO + rows) * (1 - odd), HALO)] = got_b[...]

    def place(i):
        for kind in range(2):
            courant = jnp.broadcast_to(
                wide[i, levels + kind : levels + kind + 1, :], (8, LANES)
            )
            speeds[2 * kind, i] = jnp.maximum(courant, 0.0)
            speeds[2 * kind + 1, i] = jnp.minimum(courant, 0.0)

    for i in range(HALO):
        place(i)
        place(HALO + rows + i)
    own.wait()
    for i in range(HALO, HALO + rows):
        place(i)
    done = []
    for base in range(0, levels, GROUP):
        blocks = -(-min(GROUP, levels - base) // 8)
        along = lambda i: (speeds[0, i + HALO], speeds[1, i + HALO])
        across = lambda i: (speeds[2, i + HALO], speeds[3, i + HALO])

        @functools.cache
        def start(i):
            rows_here = wide[i + HALO, base : base + 8 * blocks, :]
            return rows_here.reshape(blocks, 8, LANES)

        first = operator(start, along, across)
        one = functools.cache(lambda i: start(i) + first(i))
        second = operator(one, along, across)
        two = functools.cache(
            lambda i: 0.75 * start(i) + 0.25 * (one(i) + second(i))
        )
        third = operator(two, along, across)
        keep = min(GROUP, levels - base)
        for i in range(rows):
            value = 1.0 / 3.0 * start(i) + 2.0 / 3.0 * (two(i) + third(i))
            value = value.reshape(8 * blocks, LANES)
            done.append((base * rows + i, keep, value))
    for first_line, keep, value in done:
        out[pl.ds(first_line, keep, stride=rows), :] = value[:keep]


def advect(field, got_a, got_b, levels, axis):
    rows, levels_wide, across = field.shape
    vmem = pl.BlockSpec(memory_space=pltpu.VMEM)
    return pl.pallas_call(
        functools.partial(advect_kernel, levels=levels, axis=axis),
        out_shape=jax.ShapeDtypeStruct((levels * rows, across), F32),
        in_specs=[pl.BlockSpec(memory_space=pl.ANY), vmem, vmem],
        out_specs=vmem,
        scratch_shapes=[
            pltpu.VMEM((rows + 2 * HALO, levels_wide, across), F32),
            pltpu.VMEM((4, rows + 2 * HALO, 8, across), F32),
            pltpu.SemaphoreType.DMA,
        ],
        compiler_params=pltpu.CompilerParams(vmem_limit_bytes=ADVECT_VMEM),
        name="advect_sections",
    )(field, got_a, got_b)


def shards(inputs, tracer, speed_along, speed_across, inverse_list, *params):
    weights, biases = list(params[0::2]), params[1::2]
    weights[5] = weights[5].T
    levels, rows, across = tracer.shape
    tendencies, field, pay_a, pay_b = network(
        inverse_list.reshape(rows, across),
        tracer.reshape(levels * rows, across),
        speed_along,
        speed_across,
        biases,
        inputs.T,
        weights,
        "gx",
    )
    count = lax.axis_size("gx")
    outer = [(i, (i - 1 if i % 2 == 0 else i + 1) % count) for i in range(count)]
    inner = [(i, i + 1 if i % 2 == 0 else i - 1) for i in range(count)]
    got_a = lax.ppermute(pay_a, "gx", outer)
    got_b = lax.ppermute(pay_b, "gx", inner)
    advected = advect(field, got_a, got_b, levels, "gx")
    return tendencies.T, advected.reshape(levels, rows, across)


def solution(mesh):
    placed = (
        P(("member", "gx"), None),
        P(None, ("member", "gx"), None),
        P(("member", "gx"), None),
        P(("member", "gx"), None),
        P(("member", "gx")),
        *[P()] * 12,
    )
    return jax.shard_map(
        shards,
        mesh=mesh,
        in_specs=placed,
        out_specs=(P(("member", "gx"), None), P(None, ("member", "gx"), None)),
        check_vma=False,
    )
```

```python
import functools
import jax
import jax.numpy as jnp
from jax import lax
from jax.experimental import pallas as pl
from jax.experimental.pallas import tpu as pltpu
from jax.sharding import PartitionSpec as P

F32, BF16 = jnp.float32, jnp.bfloat16
LANES = 128
CHUNK = 256
HALO = 6
GROUP = 64
FIRST = 256
LINES = 128
NETWORK_VMEM = 60_000_000
ADVECT_VMEM = 8 * 2**20


def round_up(value, unit):
    return -(-value // unit) * unit


def split(value):
    high = value.astype(BF16)
    low = (value - high.astype(F32)).astype(BF16)
    return high, low


def network_kernel(
    *refs, sizes, levels, axis
):
    small_hbm, rest = refs[:10], refs[10:]
    x_hbm, weights_hbm, rest = rest[0], rest[1:7], rest[7:]
    tend_hbm, field, pay_a, pay_b, rest = rest[0], rest[1], rest[2], rest[3], rest[4:]
    x_in, weights_in, rest = rest[0], rest[1:7], rest[7:]
    cats, columns, rest = rest[:6], rest[6:12], rest[12:]
    inverse, tracer, along, across, *biases = rest[:10]
    hold_a, hold_b, w_tail, x_tail, b_six, tend, x_sems, w_sems, out_sems, small_sems, first_sems = rest[10:]

    width = x_hbm.shape[1]
    chunks = width // CHUNK
    depth_in = sizes[0]
    aligned = depth_in // 8 * 8
    whole = depth_in // LANES * LANES

    def x_copy(c):
        part = pl.ds(c * CHUNK, CHUNK)
        return pltpu.make_async_copy(x_hbm.at[:, part], x_in.at[:, part], x_sems.at[c])

    def w_copy(layer):
        return pltpu.make_async_copy(
            weights_hbm[layer], weights_in[layer], w_sems.at[layer]
        )

    def small_copy(i):
        target = (inverse, tracer, along, across, *biases)[i]
        return pltpu.make_async_copy(small_hbm[i], target, small_sems.at[i])

    def out_copy(c):
        part = pl.ds(c * CHUNK, CHUNK)
        return pltpu.make_async_copy(
            tend.at[:, part], tend_hbm.at[:, part], out_sems.at[c]
        )

    def bias_columns(layer):
        count = sizes[layer + 1]
        source = biases[layer]
        if count % LANES:
            b_six[0:1, :] = jnp.zeros((1, b_six.shape[1]), F32)
            b_six[0:1, 0:count] = source[...].reshape(1, count)
            row = b_six[0:1, :]
        else:
            row = source[...].reshape(1, count)
        scale = 0.5 if layer < 5 else 1.0
        for n in range(0, count, LANES):
            block = jnp.broadcast_to(row[:, n : n + LANES], (LANES, LANES)).T * scale
            keep = min(LANES, count - n)
            columns[layer][n : n + keep, :] = block[:keep]

    def put_weights(layer, rows, start, block):
        depth = cats[layer].shape[1] // 3
        high, low = split(block)
        size = block.shape[1]
        cats[layer][rows, start : start + size] = high
        cats[layer][rows, depth + start : depth + start + size] = high
        cats[layer][rows, 2 * depth + start : 2 * depth + start + size] = low

    def prepare(layer, part, parts):
        count = sizes[layer + 1]
        if layer == 5:
            jobs = [(n, 0) for n in range(0, count, 16)]
        else:
            jobs = [
                (n, k)
                for n in range(0, count, LANES)
                for k in range(0, sizes[layer], LANES)
            ]
        for n, k in jobs[part * len(jobs) // parts : (part + 1) * len(jobs) // parts]:
            if layer == 5:
                put_weights(5, slice(n, n + 16), 0, weights_in[5][n : n + 16, :])
            else:
                block = weights_in[layer][k : k + LANES, n : n + LANES]
                put_weights(layer, slice(n, n + LANES), k, block.T * 0.5)

    def put_rows(hold, depth, start, cols, value):
        high, low = split(value)
        size = value.shape[0]
        hold[start : start + size, cols] = high
        hold[depth + start : depth + start + size, cols] = low
        hold[2 * depth + start : 2 * depth + start + size, cols] = high

    def prepare_inputs(c):
        cols = slice(c * CHUNK, (c + 1) * CHUNK)
        x_tail[0 : aligned - whole, cols] = x_in[whole:aligned, cols]
        x_tail[aligned - whole : depth_in - whole, cols] = x_in[aligned:depth_in, cols]
        for k in range(0, whole, LANES):
            put_rows(hold_a, depth_pad, k, cols, x_in[k : k + LANES, cols])
        put_rows(hold_a, depth_pad, whole, cols, x_tail[:, cols])

    def place_speeds():
        for r in range(rows):
            field[r, levels : levels + 1, :] = along[r : r + 1, :]
            field[r, levels + 1 : levels + 2, :] = across[r : r + 1, :]
            field[r, levels + 2 : levels_wide, :] = jnp.zeros(
                (levels_wide - levels - 2, LANES), F32
            )

    def product(layer, held, c, lines):
        deep = cats[layer].shape[1]
        cols = slice(c * CHUNK, (c + 1) * CHUNK)
        return jnp.dot(
            cats[layer][lines, :], held[0:deep, cols], preferred_element_type=F32
        )

    def finish(layer, other, c, lines, total):
        bias = columns[layer][lines, :]
        value = total + jnp.concatenate([bias] * (CHUNK // LANES), axis=1)
        if layer < 5:
            value = value + value * jnp.tanh(value)
            cols = slice(c * CHUNK, (c + 1) * CHUNK)
            put_rows(other, sizes[layer + 1], lines.start, cols, value)
            return
        for part in range(CHUNK // LANES):
            r = c * (CHUNK // LANES) + part
            day = inverse[r : r + 1, :] >= 0
            shown = jnp.where(day, value[:, part * LANES : (part + 1) * LANES], 0.0)
            tend[lines, r * LANES : (r + 1) * LANES] = shown
            if lines.start == 0:
                field[r, 0:levels, :] = (
                    tracer[pl.ds(r, levels, stride=rows), :] + shown[0:levels]
                )
        if lines.stop == sizes[6]:
            out_copy(c).start()

    def first_copy(n):
        part = pl.ds(n * FIRST, FIRST)
        return pltpu.make_async_copy(
            weights_hbm[0].at[:, part], weights_in[0].at[:, part], first_sems.at[n]
        )

    def prepare_first(n):
        part = slice(n, n + LANES)
        w_tail[0 : aligned - whole, part] = weights_in[0][whole:aligned, part]
        w_tail[aligned - whole : depth_in - whole, part] = weights_in[0][
            aligned:depth_in, part
        ]
        for k in range(0, padded_in, LANES):
            if k >= whole:
                block = w_tail[:, part]
            else:
                block = weights_in[0][k : k + LANES, part]
            put_weights(0, part, k, block.T * 0.5)

    rows, levels_wide = field.shape[0], field.shape[1]
    padded_in = cats[0].shape[1] // 3
    depth_pad = padded_in
    first_parts = sizes[1] // FIRST
    x_copy(0).start()
    for n in range(first_parts):
        first_copy(n).start()
    for c in range(1, chunks):
        x_copy(c).start()
    w_tail[...] = jnp.zeros(w_tail.shape, F32)
    x_tail[...] = jnp.zeros(x_tail.shape, F32)
    x_copy(0).wait()
    prepare_inputs(0)
    first_copy(0).wait()
    prepare_first(0)
    for i in range(10):
        small_copy(i).start()
    for layer in range(1, 6):
        w_copy(layer).start()

    pending = None
    held, other = hold_a, hold_b
    for layer in range(6):
        count = sizes[layer + 1]
        blocks = [slice(m, min(m + LINES, count)) for m in range(0, count, LINES)]
        parts = chunks * len(blocks)
        for c in range(chunks):
            for m, lines in enumerate(blocks):
                part = c * len(blocks) + m
                if layer == 0 and c == 0:
                    for n in range(lines.start, lines.stop, LANES):
                        if n and n % FIRST == 0:
                            first_copy(n // FIRST).wait()
                        if n:
                            prepare_first(n)
                if layer == 0 and m == 0 and c > 0:
                    x_copy(c).wait()
                    prepare_inputs(c)
                if layer == 0 and part == 1:
                    for i in range(10):
                        small_copy(i).wait()
                    bias_columns(0)
                total = product(layer, held, c, lines)
                if layer < 5:
                    if layer == 0 and part == parts // 2 or layer and part == 0:
                        w_copy(layer + 1).wait()
                        bias_columns(layer + 1)
                    if layer:
                        prepare(layer + 1, part, parts)
                    elif part >= parts // 2:
                        prepare(layer + 1, part - parts // 2, parts - parts // 2)
                elif part == 0:
                    place_speeds()
                if pending is not None:
                    finish(*pending)
                pending = (layer, other, c, lines, total)
        held, other = other, held
    finish(*pending)

    odd = lax.rem(lax.axis_index(axis), 2)
    pay_a[...] = field[pl.ds((rows - HALO) * odd, HALO)]
    pay_b[...] = field[pl.ds((rows - HALO) * (1 - odd), HALO)]
    for c in range(chunks):
        out_copy(c).wait()


def network(inverse, tracer, along, across, biases, x, weights, axis):
    sizes = [x.shape[0]] + [b.shape[0] for b in biases]
    width = x.shape[1]
    rows = along.shape[0]
    levels = tracer.shape[0] // rows
    levels_wide = round_up(levels + 2, 8)
    chunks = width // CHUNK
    padded = [round_up(s, LANES) for s in sizes[:6]]
    deepest = 3 * max(padded)
    tail = padded[0] - sizes[0] // LANES * LANES
    vmem, hbm = pl.BlockSpec(memory_space=pltpu.VMEM), pl.BlockSpec(memory_space=pl.ANY)
    total = sum(sizes[i] * sizes[i + 1] for i in range(6)) * width
    return pl.pallas_call(
        functools.partial(network_kernel, sizes=sizes, levels=levels, axis=axis),
        out_shape=(
            jax.ShapeDtypeStruct((sizes[6], width), F32),
            jax.ShapeDtypeStruct((rows, levels_wide, LANES), F32),
            jax.ShapeDtypeStruct((HALO, levels_wide, LANES), F32),
            jax.ShapeDtypeStruct((HALO, levels_wide, LANES), F32),
        ),
        in_specs=[hbm] * 17,
        out_specs=(hbm, vmem, vmem, vmem),
        scratch_shapes=[
            pltpu.VMEM(x.shape, F32),
            *[pltpu.VMEM(w.shape, F32) for w in weights],
            *[pltpu.VMEM((sizes[i + 1], 3 * padded[i]), BF16) for i in range(6)],
            *[pltpu.VMEM((sizes[i + 1], LANES), F32) for i in range(6)],
            pltpu.VMEM(inverse.shape, jnp.int32),
            pltpu.VMEM(tracer.shape, F32),
            pltpu.VMEM(along.shape, F32),
            pltpu.VMEM(across.shape, F32),
            *[pltpu.VMEM(b.shape, F32) for b in biases],
            pltpu.VMEM((deepest, width), BF16),
            pltpu.VMEM((deepest, width), BF16),
            pltpu.VMEM((tail, sizes[1]), F32),
            pltpu.VMEM((tail, width), F32),
            pltpu.VMEM((8, round_up(sizes[6], LANES)), F32),
            pltpu.VMEM((sizes[6], width), F32),
            pltpu.SemaphoreType.DMA((chunks,)),
            pltpu.SemaphoreType.DMA((6,)),
            pltpu.SemaphoreType.DMA((chunks,)),
            pltpu.SemaphoreType.DMA((10,)),
            pltpu.SemaphoreType.DMA((sizes[1] // FIRST,)),
        ],
        compiler_params=pltpu.CompilerParams(vmem_limit_bytes=NETWORK_VMEM),
        cost_estimate=pl.CostEstimate(
            flops=6 * total, bytes_accessed=14_000_000, transcendentals=3_000_000
        ),
        name="column_network",
    )(inverse, tracer, along, across, *biases, x, *weights)


def half_minmod(first, second):
    return 0.5 * (
        jnp.maximum(jnp.minimum(first, second), 0.0)
        + jnp.minimum(jnp.maximum(first, second), 0.0)
    )


def cat(values):
    return values[0] if len(values) == 1 else jnp.concatenate(values, axis=0)


def advect_kernel(field, got_a, got_b, out, wide, speeds, sem, *, levels, axis):
    rows = field.shape[0]
    odd = lax.rem(lax.axis_index(axis), 2)
    own = pltpu.make_async_copy(field, wide.at[pl.ds(HALO, rows)], sem)
    own.start()
    wide[pl.ds((HALO + rows) * odd, HALO)] = got_a[...]
    wide[pl.ds((HALO + rows) * (1 - odd), HALO)] = got_b[...]

    def place(i):
        for kind in range(2):
            courant = jnp.broadcast_to(
                wide[i, levels + kind : levels + kind + 1, :], (8, LANES)
            )
            speeds[2 * kind, i] = jnp.maximum(courant, 0.0)
            speeds[2 * kind + 1, i] = jnp.minimum(courant, 0.0)

    for i in range(HALO):
        place(i)
        place(HALO + rows + i)
    own.wait()
    for i in range(HALO, HALO + rows):
        place(i)
    for base in range(0, levels, GROUP):
        blocks = -(-min(GROUP, levels - base) // 8)
        wavefront(base, blocks, min(GROUP, levels - base), out, wide, speeds, rows)


def wavefront(base, blocks, keep, out, wide, speeds, rows):
    fields = [{}, {}, {}]
    steps, slopes, fluxes = [{}, {}, {}], [{}, {}, {}], [{}, {}, {}]
    reach = [(-4, rows + 3), (-2, rows + 1), (0, rows - 1)]
    shape = (blocks, 8, LANES)

    def load(i):
        return wide[i + HALO, base : base + 8 * blocks, :].reshape(shape)

    def courant(kind, at):
        return cat([jnp.broadcast_to(speeds[kind, i + HALO], shape) for i in at])

    def pieces(value, count):
        return [value[n * blocks : (n + 1) * blocks] for n in range(count)]

    def face(active, at):
        ahead, behind = courant(0, at), courant(1, at)
        upper = cat([fields[k][i] - slopes[k][i] for k, i in zip(active, at)])
        lower = cat([fields[k][i - 1] + slopes[k][i - 1] for k, i in zip(active, at)])
        return ahead * lower + behind * upper

    for i in range(-HALO, -2):
        fields[0][i] = load(i)
    for t in range(-4, rows + 6):
        active = [k for k in range(3) if reach[k][0] <= t - 3 * k <= reach[k][1]]
        if t + 2 < rows + HALO:
            fields[0][t + 2] = load(t + 2)
        for k in active:
            c = t - 3 * k
            if c == reach[k][0]:
                f = fields[k]
                for i in (c - 1, c, c + 1):
                    steps[k][i] = f[i] - f[i - 1]
                for i in (c - 1, c):
                    slopes[k][i] = half_minmod(steps[k][i + 1], steps[k][i])
                fluxes[k][c] = face([k], [c])
        at = [t - 3 * k for k in active]
        here = cat([fields[k][i] for k, i in zip(active, at)])
        back = here - pltpu.roll(here, 1, 2)
        new = cat(
            [fields[k][i + 2] - fields[k][i + 1] for k, i in zip(active, at)]
        )
        last = cat([steps[k][i + 1] for k, i in zip(active, at)])
        bend = half_minmod(pltpu.roll(back, LANES - 1, 2), back)
        slope = half_minmod(new, last)
        for k, i, a_step, a_slope in zip(
            active, at, pieces(new, len(at)), pieces(slope, len(at))
        ):
            steps[k][i + 2], slopes[k][i + 1] = a_step, a_slope
        side = courant(2, at) * pltpu.roll(here + bend, 1, 2)
        side = side + courant(3, at) * (here - bend)
        flux = face(active, [i + 1 for i in at])
        for k, i, a_flux in zip(active, at, pieces(flux, len(at))):
            fluxes[k][i + 1] = a_flux
        moved = cat([fluxes[k][i] for k, i in zip(active, at)]) - flux
        moved = here + (moved + (side - pltpu.roll(side, LANES - 1, 2)))
        for k, i, value in zip(active, at, pieces(moved, len(at))):
            if k == 0:
                fields[1][i] = value
            elif k == 1:
                fields[2][i] = 0.75 * fields[0][i] + 0.25 * value
            else:
                value = 1.0 / 3.0 * fields[0][i] + 2.0 / 3.0 * value
                value = value.reshape(8 * blocks, LANES)
                out[pl.ds(base * rows + i, keep, stride=rows), :] = value[:keep]


def advect(field, got_a, got_b, levels, axis):
    rows, levels_wide, across = field.shape
    vmem = pl.BlockSpec(memory_space=pltpu.VMEM)
    return pl.pallas_call(
        functools.partial(advect_kernel, levels=levels, axis=axis),
        out_shape=jax.ShapeDtypeStruct((levels * rows, across), F32),
        in_specs=[pl.BlockSpec(memory_space=pl.ANY), vmem, vmem],
        out_specs=vmem,
        scratch_shapes=[
            pltpu.VMEM((rows + 2 * HALO, levels_wide, across), F32),
            pltpu.VMEM((4, rows + 2 * HALO, 8, across), F32),
            pltpu.SemaphoreType.DMA,
        ],
        compiler_params=pltpu.CompilerParams(vmem_limit_bytes=ADVECT_VMEM),
        name="advect_sections",
    )(field, got_a, got_b)


def shards(inputs, tracer, speed_along, speed_across, inverse_list, *params):
    weights, biases = list(params[0::2]), params[1::2]
    weights[5] = weights[5].T
    levels, rows, across = tracer.shape
    tendencies, field, pay_a, pay_b = network(
        inverse_list.reshape(rows, across),
        tracer.reshape(levels * rows, across),
        speed_along,
        speed_across,
        biases,
        inputs.T,
        weights,
        "gx",
    )
    count = lax.axis_size("gx")
    outer = [(i, (i - 1 if i % 2 == 0 else i + 1) % count) for i in range(count)]
    inner = [(i, i + 1 if i % 2 == 0 else i - 1) for i in range(count)]
    got_a = lax.ppermute(pay_a, "gx", outer)
    got_b = lax.ppermute(pay_b, "gx", inner)
    advected = advect(field, got_a, got_b, levels, "gx")
    return tendencies.T, advected.reshape(levels, rows, across)


def solution(mesh):
    placed = (
        P(("member", "gx"), None),
        P(None, ("member", "gx"), None),
        P(("member", "gx"), None),
        P(("member", "gx"), None),
        P(("member", "gx")),
        *[P()] * 12,
    )
    return jax.shard_map(
        shards,
        mesh=mesh,
        in_specs=placed,
        out_specs=(P(("member", "gx"), None), P(None, ("member", "gx"), None)),
        check_vma=False,
    )
```

```python
import functools
import jax
import jax.numpy as jnp
from jax import lax
from jax.experimental import pallas as pl
from jax.experimental.pallas import tpu as pltpu
from jax.sharding import PartitionSpec as P

F32, BF16 = jnp.float32, jnp.bfloat16
LANES = 128
CHUNK = 256
HALO = 6
GROUP = 32
FIRST = 256
NETWORK_VMEM = 60_000_000
ADVECT_VMEM = 8 * 2**20


def round_up(value, unit):
    return -(-value // unit) * unit


def split(value):
    high = value.astype(BF16)
    low = (value - high.astype(F32)).astype(BF16)
    return high, low


def network_kernel(*refs, sizes, levels, axis):
    small_hbm, x_hbm, weights_hbm, refs = refs[:10], refs[10], refs[11:17], refs[17:]
    (tend_hbm, field, pay_a, pay_b), refs = refs[:4], refs[4:]
    x_in, weights_in, cats, columns, refs = (
        refs[0],
        refs[1:7],
        refs[7:13],
        refs[13:19],
        refs[19:],
    )
    inverse, tracer, along, across, *biases = refs[:10]
    (hold_a, hold_b, w_tail, x_tail, bias_rows, tend) = refs[10:16]
    x_sems, w_sems, out_sems, small_sems, first_sems = refs[16:]

    chunks = x_hbm.shape[1] // CHUNK
    rows, levels_wide = field.shape[0], field.shape[1]
    depth_in = sizes[0]
    aligned = depth_in // 8 * 8
    whole = depth_in // LANES * LANES
    padded_in = cats[0].shape[1] // 3

    def columns_of(c):
        start = c * CHUNK
        if not isinstance(c, int):
            start = pl.multiple_of(start, CHUNK)
        return pl.ds(start, CHUNK)

    def block_of(n, size):
        start = n * size
        if not isinstance(n, int):
            start = pl.multiple_of(start, size)
        return pl.ds(start, size)

    def x_copy(c):
        part = columns_of(c)
        return pltpu.make_async_copy(x_hbm.at[:, part], x_in.at[:, part], x_sems.at[c])

    def first_copy(n):
        part = block_of(n, FIRST)
        return pltpu.make_async_copy(
            weights_hbm[0].at[:, part], weights_in[0].at[:, part], first_sems.at[n]
        )

    def w_copy(layer):
        return pltpu.make_async_copy(
            weights_hbm[layer], weights_in[layer], w_sems.at[layer]
        )

    def small_copy(i):
        target = (inverse, tracer, along, across, *biases)[i]
        return pltpu.make_async_copy(small_hbm[i], target, small_sems.at[i])

    def out_copy(c):
        part = columns_of(c)
        return pltpu.make_async_copy(
            tend.at[:, part], tend_hbm.at[:, part], out_sems.at[c]
        )

    def put_weights(layer, lines, start, block):
        depth = cats[layer].shape[1] // 3
        high, low = split(block)
        size = block.shape[1]
        cats[layer][lines, start : start + size] = high
        cats[layer][lines, depth + start : depth + start + size] = high
        cats[layer][lines, 2 * depth + start : 2 * depth + start + size] = low

    def prepare(layer, n):
        lines = block_of(n, LANES)
        for k in range(0, sizes[layer], LANES):
            block = weights_in[layer][k : k + LANES, lines]
            put_weights(layer, lines, k, block.T * 0.5)
        prepare_bias(layer, n)

    def prepare_bias(layer, n):
        lines = block_of(n, LANES)
        row = bias_rows[layer : layer + 1, lines]
        scale = 0.5 if layer < 5 else 1.0
        columns[layer][lines, :] = jnp.broadcast_to(row, (LANES, LANES)).T * scale

    def prepare_last(start, size):
        put_weights(5, pl.ds(start, size), 0, weights_in[5][pl.ds(start, size), :])

    def prepare_first(n):
        first_copy(n).wait()
        part = block_of(n, FIRST)
        w_tail[0 : aligned - whole, part] = weights_in[0][whole:aligned, part]
        w_tail[aligned - whole : depth_in - whole, part] = weights_in[0][
            aligned:depth_in, part
        ]
        for m in range(FIRST // LANES):
            lines = block_of(n * (FIRST // LANES) + m, LANES)
            for k in range(0, padded_in, LANES):
                if k >= whole:
                    block = w_tail[:, lines]
                else:
                    block = weights_in[0][k : k + LANES, lines]
                put_weights(0, lines, k, block.T * 0.5)
            prepare_bias(0, n * (FIRST // LANES) + m)

    def put_rows(hold, depth, start, cols, value):
        high, low = split(value)
        size = value.shape[0]
        hold[start : start + size, cols] = high
        hold[depth + start : depth + start + size, cols] = low
        hold[2 * depth + start : 2 * depth + start + size, cols] = high

    def prepare_inputs(c):
        cols = columns_of(c)
        x_tail[0 : aligned - whole, :] = x_in[whole:aligned, cols]
        x_tail[aligned - whole : depth_in - whole, :] = x_in[aligned:depth_in, cols]
        for k in range(0, whole, LANES):
            put_rows(hold_a, padded_in, k, cols, x_in[k : k + LANES, cols])
        put_rows(hold_a, padded_in, whole, cols, x_tail[...])

    def product(layer, held, c, lines):
        deep = cats[layer].shape[1]
        return jnp.dot(
            cats[layer][lines, :],
            held[0:deep, columns_of(c)],
            preferred_element_type=F32,
        )

    def finish(layer, other, c, lines, total):
        bias = columns[layer][lines, :]
        value = total + jnp.concatenate([bias] * (CHUNK // LANES), axis=1)
        if layer < 5:
            value = value + value * jnp.tanh(value)
            put_rows(other, sizes[layer + 1], lines.start, columns_of(c), value)
            return
        for part in range(CHUNK // LANES):
            r = c * (CHUNK // LANES) + part
            day = inverse[pl.ds(r, 1), :] >= 0
            shown = jnp.where(day, value[:, part * LANES : (part + 1) * LANES], 0.0)
            tend[lines, block_of(r, LANES)] = shown
            if lines.start == 0:
                field[r, 0:levels, :] = (
                    tracer[pl.ds(r, levels, stride=rows), :] + shown[0:levels]
                )

    def looped(count):
        def wrap(body):
            lax.fori_loop(0, count, lambda i, carry: (body(i), carry)[1], 0)

        return wrap

    x_copy(0).start()
    for n in range(sizes[1] // FIRST):
        first_copy(n).start()
    for i in range(10):
        small_copy(i).start()
    for c in range(1, chunks):
        x_copy(c).start()
    w_tail[...] = jnp.zeros(w_tail.shape, F32)
    x_tail[...] = jnp.zeros(x_tail.shape, F32)
    bias_rows[...] = jnp.zeros(bias_rows.shape, F32)
    x_copy(0).wait()
    prepare_inputs(0)
    for layer in range(1, 6):
        w_copy(layer).start()
    for i in range(10):
        small_copy(i).wait()
    for layer in range(6):
        count = sizes[layer + 1]
        bias_rows[layer : layer + 1, 0:count] = biases[layer][...].reshape(1, count)
    for r in range(rows):
        field[r, levels : levels + 1, :] = along[r : r + 1, :]
        field[r, levels + 1 : levels + 2, :] = across[r : r + 1, :]
        field[r, levels + 2 : levels_wide, :] = jnp.zeros(
            (levels_wide - levels - 2, LANES), F32
        )
    looped(sizes[1] // FIRST)(prepare_first)
    for c in range(1, chunks):
        x_copy(c).wait()

    held, other = hold_a, hold_b
    for layer in range(6):
        count = sizes[layer + 1]
        half = round_up(count, 32) // 2
        blocks = [slice(0, half), slice(half, count)]
        if layer < 5:
            w_copy(layer + 1).wait()
            ahead = sizes[layer + 2]
            if layer == 4:
                share = ahead // chunks // 16 * 16
                if share * chunks < ahead:
                    prepare_last(share * chunks, ahead - share * chunks)
                for n in range(round_up(ahead, LANES) // LANES):
                    prepare_bias(5, n)
            else:
                share = ahead // LANES // chunks
                for n in range(share * chunks, ahead // LANES):
                    prepare(layer + 1, n)

        def body(c, layer=layer, held=held, other=other, blocks=blocks):
            pending = None
            for lines in blocks:
                total = product(layer, held, c, lines)
                if pending is not None:
                    finish(layer, other, c, *pending)
                elif layer == 4:
                    prepare_last(pl.multiple_of(c * share, 16), share)
                elif layer < 4:
                    for n in range(share):
                        prepare(layer + 1, c * share + n)
                    if layer == 0:
                        prepare_inputs(jnp.minimum(c + 1, chunks - 1))
                pending = (lines, total)
            finish(layer, other, c, *pending)
            if layer == 5:
                out_copy(c).start()

        looped(chunks)(body)
        held, other = other, held

    odd = lax.rem(lax.axis_index(axis), 2)
    pay_a[...] = field[pl.ds((rows - HALO) * odd, HALO)]
    pay_b[...] = field[pl.ds((rows - HALO) * (1 - odd), HALO)]
    for c in range(chunks):
        out_copy(c).wait()


def network(inverse, tracer, along, across, biases, x, weights, axis):
    sizes = [x.shape[0]] + [b.shape[0] for b in biases]
    width = x.shape[1]
    rows = along.shape[0]
    levels = tracer.shape[0] // rows
    levels_wide = round_up(levels + 2, 8)
    chunks = width // CHUNK
    padded = [round_up(s, LANES) for s in sizes[:6]]
    deepest = 3 * max(padded)
    tail = padded[0] - sizes[0] // LANES * LANES
    vmem, hbm = pl.BlockSpec(memory_space=pltpu.VMEM), pl.BlockSpec(memory_space=pl.ANY)
    total = sum(sizes[i] * sizes[i + 1] for i in range(6)) * width
    return pl.pallas_call(
        functools.partial(network_kernel, sizes=sizes, levels=levels, axis=axis),
        out_shape=(
            jax.ShapeDtypeStruct((sizes[6], width), F32),
            jax.ShapeDtypeStruct((rows, levels_wide, LANES), F32),
            jax.ShapeDtypeStruct((HALO, levels_wide, LANES), F32),
            jax.ShapeDtypeStruct((HALO, levels_wide, LANES), F32),
        ),
        in_specs=[hbm] * 17,
        out_specs=(hbm, vmem, vmem, vmem),
        scratch_shapes=[
            pltpu.VMEM(x.shape, F32),
            *[pltpu.VMEM(w.shape, F32) for w in weights],
            *[pltpu.VMEM((sizes[i + 1], 3 * padded[i]), BF16) for i in range(6)],
            *[pltpu.VMEM((round_up(sizes[i + 1], LANES), LANES), F32) for i in range(6)],
            pltpu.VMEM(inverse.shape, jnp.int32),
            pltpu.VMEM(tracer.shape, F32),
            pltpu.VMEM(along.shape, F32),
            pltpu.VMEM(across.shape, F32),
            *[pltpu.VMEM(b.shape, F32) for b in biases],
            pltpu.VMEM((deepest, width), BF16),
            pltpu.VMEM((deepest, width), BF16),
            pltpu.VMEM((tail, sizes[1]), F32),
            pltpu.VMEM((tail, CHUNK), F32),
            pltpu.VMEM((8, round_up(max(sizes[1:]), LANES)), F32),
            pltpu.VMEM((sizes[6], width), F32),
            pltpu.SemaphoreType.DMA((chunks,)),
            pltpu.SemaphoreType.DMA((6,)),
            pltpu.SemaphoreType.DMA((chunks,)),
            pltpu.SemaphoreType.DMA((10,)),
            pltpu.SemaphoreType.DMA((sizes[1] // FIRST,)),
        ],
        compiler_params=pltpu.CompilerParams(vmem_limit_bytes=NETWORK_VMEM),
        cost_estimate=pl.CostEstimate(
            flops=6 * total, bytes_accessed=14_000_000, transcendentals=3_000_000
        ),
        name="column_network",
    )(inverse, tracer, along, across, *biases, x, *weights)


def half_minmod(first, second):
    return 0.5 * (
        jnp.maximum(jnp.minimum(first, second), 0.0)
        + jnp.minimum(jnp.maximum(first, second), 0.0)
    )


def cat(values):
    return values[0] if len(values) == 1 else jnp.concatenate(values, axis=0)


def advect_kernel(field, got_a, got_b, out, wide, speeds, sem, *, levels, axis):
    rows = field.shape[0]
    odd = lax.rem(lax.axis_index(axis), 2)
    own = pltpu.make_async_copy(field, wide.at[pl.ds(HALO, rows)], sem)
    own.start()
    wide[pl.ds((HALO + rows) * odd, HALO)] = got_a[...]
    wide[pl.ds((HALO + rows) * (1 - odd), HALO)] = got_b[...]

    def place(i):
        for kind in range(2):
            courant = jnp.broadcast_to(
                wide[i, levels + kind : levels + kind + 1, :], (8, LANES)
            )
            speeds[2 * kind, i] = jnp.maximum(courant, 0.0)
            speeds[2 * kind + 1, i] = jnp.minimum(courant, 0.0)

    for i in range(HALO):
        place(i)
        place(HALO + rows + i)
    own.wait()
    for i in range(HALO, HALO + rows):
        place(i)
    groups = wide.shape[1] // GROUP

    def group(g, carry):
        wavefront(g, groups, levels, out, wide, speeds, rows)
        return carry

    lax.fori_loop(0, groups, group, 0)


def wavefront(g, groups, levels, out, wide, speeds, rows):
    base = pl.multiple_of(g * GROUP, GROUP)
    blocks = GROUP // 8
    keep = levels - (groups - 1) * GROUP
    fields = [{}, {}, {}]
    steps, slopes, fluxes = [{}, {}, {}], [{}, {}, {}], [{}, {}, {}]
    reach = [(-4, rows + 3), (-2, rows + 1), (0, rows - 1)]
    shape = (blocks, 8, LANES)

    def load(i):
        return wide[i + HALO, pl.ds(base, GROUP), :].reshape(shape)

    def courant(kind, at):
        return cat([jnp.broadcast_to(speeds[kind, i + HALO], shape) for i in at])

    def pieces(value, count):
        return [value[n * blocks : (n + 1) * blocks] for n in range(count)]

    def face(active, at):
        ahead, behind = courant(0, at), courant(1, at)
        upper = cat([fields[k][i] - slopes[k][i] for k, i in zip(active, at)])
        lower = cat([fields[k][i - 1] + slopes[k][i - 1] for k, i in zip(active, at)])
        return ahead * lower + behind * upper

    rest = []
    for i in range(-HALO, -2):
        fields[0][i] = load(i)
    for t in range(-4, rows + 6):
        active = [k for k in range(3) if reach[k][0] <= t - 3 * k <= reach[k][1]]
        if t + 2 < rows + HALO:
            fields[0][t + 2] = load(t + 2)
        for k in active:
            c = t - 3 * k
            if c == reach[k][0]:
                f = fields[k]
                for i in (c - 1, c, c + 1):
                    steps[k][i] = f[i] - f[i - 1]
                for i in (c - 1, c):
                    slopes[k][i] = half_minmod(steps[k][i + 1], steps[k][i])
                fluxes[k][c] = face([k], [c])
        at = [t - 3 * k for k in active]
        here = cat([fields[k][i] for k, i in zip(active, at)])
        back = here - pltpu.roll(here, 1, 2)
        new = cat(
            [fields[k][i + 2] - fields[k][i + 1] for k, i in zip(active, at)]
        )
        last = cat([steps[k][i + 1] for k, i in zip(active, at)])
        bend = half_minmod(pltpu.roll(back, LANES - 1, 2), back)
        slope = half_minmod(new, last)
        for k, i, a_step, a_slope in zip(
            active, at, pieces(new, len(at)), pieces(slope, len(at))
        ):
            steps[k][i + 2], slopes[k][i + 1] = a_step, a_slope
        side = courant(2, at) * pltpu.roll(here + bend, 1, 2)
        side = side + courant(3, at) * (here - bend)
        flux = face(active, [i + 1 for i in at])
        for k, i, a_flux in zip(active, at, pieces(flux, len(at))):
            fluxes[k][i + 1] = a_flux
        moved = cat([fluxes[k][i] for k, i in zip(active, at)]) - flux
        moved = here + (moved + (side - pltpu.roll(side, LANES - 1, 2)))
        for k, i, value in zip(active, at, pieces(moved, len(at))):
            if k == 0:
                fields[1][i] = value
            elif k == 1:
                fields[2][i] = 0.75 * fields[0][i] + 0.25 * value
            else:
                value = 1.0 / 3.0 * fields[0][i] + 2.0 / 3.0 * value
                value = value.reshape(GROUP, LANES)
                out[pl.ds(base * rows + i, keep, stride=rows), :] = value[:keep]
                rest.append((i, value[keep:]))
    if keep < GROUP:

        @pl.when(g < groups - 1)
        def _():
            for i, value in rest:
                lines = pl.ds((base + keep) * rows + i, GROUP - keep, stride=rows)
                out[lines, :] = value


def advect(field, got_a, got_b, levels, axis):
    rows, levels_wide, across = field.shape
    vmem = pl.BlockSpec(memory_space=pltpu.VMEM)
    return pl.pallas_call(
        functools.partial(advect_kernel, levels=levels, axis=axis),
        out_shape=jax.ShapeDtypeStruct((levels * rows, across), F32),
        in_specs=[pl.BlockSpec(memory_space=pl.ANY), vmem, vmem],
        out_specs=vmem,
        scratch_shapes=[
            pltpu.VMEM((rows + 2 * HALO, levels_wide, across), F32),
            pltpu.VMEM((4, rows + 2 * HALO, 8, across), F32),
            pltpu.SemaphoreType.DMA,
        ],
        compiler_params=pltpu.CompilerParams(vmem_limit_bytes=ADVECT_VMEM),
        name="advect_sections",
    )(field, got_a, got_b)


def shards(inputs, tracer, speed_along, speed_across, inverse_list, *params):
    weights, biases = list(params[0::2]), params[1::2]
    weights[5] = weights[5].T
    levels, rows, across = tracer.shape
    tendencies, field, pay_a, pay_b = network(
        inverse_list.reshape(rows, across),
        tracer.reshape(levels * rows, across),
        speed_along,
        speed_across,
        biases,
        inputs.T,
        weights,
        "gx",
    )
    count = lax.axis_size("gx")
    outer = [(i, (i - 1 if i % 2 == 0 else i + 1) % count) for i in range(count)]
    inner = [(i, i + 1 if i % 2 == 0 else i - 1) for i in range(count)]
    got_a = lax.ppermute(pay_a, "gx", outer)
    got_b = lax.ppermute(pay_b, "gx", inner)
    advected = advect(field, got_a, got_b, levels, "gx")
    return tendencies.T, advected.reshape(levels, rows, across)


def solution(mesh):
    placed = (
        P(("member", "gx"), None),
        P(None, ("member", "gx"), None),
        P(("member", "gx"), None),
        P(("member", "gx"), None),
        P(("member", "gx")),
        *[P()] * 12,
    )
    return jax.shard_map(
        shards,
        mesh=mesh,
        in_specs=placed,
        out_specs=(P(("member", "gx"), None), P(None, ("member", "gx"), None)),
        check_vma=False,
    )
```

```python
import functools
import jax
import jax.numpy as jnp
from jax import lax
from jax.experimental import pallas as pl
from jax.experimental.pallas import tpu as pltpu
from jax.sharding import PartitionSpec as P

F32, BF16 = jnp.float32, jnp.bfloat16
LANES = 128
CHUNK = 512
HALO = 6
GROUP = 32
TILE = 256
NETWORK_VMEM = 60_000_000
ADVECT_VMEM = 8 * 2**20


def round_up(value, unit):
    return -(-value // unit) * unit


def split(value):
    high = value.astype(BF16)
    low = (value - high.astype(F32)).astype(BF16)
    return high, low


def network_kernel(*refs, sizes, levels, axis):
    small_hbm, x_hbm, weights_hbm, refs = refs[:10], refs[10], refs[11:17], refs[17:]
    (tend_hbm, field, pay_a, pay_b), refs = refs[:4], refs[4:]
    x_in, weights_in, cats, refs = refs[0], refs[1:7], refs[7:13], refs[13:]
    inverse, tracer, along, across, *biases = refs[:10]
    hold_a, hold_b, w_tail, x_tail, bias_rows, tend = refs[10:16]
    x_sems, w_sems, out_sems, small_sems, first_sems = refs[16:]

    chunks = x_hbm.shape[1] // CHUNK
    rows, levels_wide = field.shape[0], field.shape[1]
    depth_in = sizes[0]
    aligned = depth_in // 8 * 8
    whole = depth_in // LANES * LANES
    padded = [cats[layer].shape[0] // 3 for layer in range(6)]

    def x_copy(c):
        part = pl.ds(c * CHUNK, CHUNK)
        return pltpu.make_async_copy(x_hbm.at[:, part], x_in.at[:, part], x_sems.at[c])

    def first_copy(n):
        part = pl.ds(n * TILE, TILE)
        return pltpu.make_async_copy(
            weights_hbm[0].at[:, part], weights_in[0].at[:, part], first_sems.at[n]
        )

    def w_copy(layer):
        target = weights_in[layer]
        if layer == 5:
            target = target.at[pl.ds(0, sizes[6])]
        return pltpu.make_async_copy(weights_hbm[layer], target, w_sems.at[layer])

    def small_copy(i):
        target = (inverse, tracer, along, across, *biases)[i]
        return pltpu.make_async_copy(small_hbm[i], target, small_sems.at[i])

    def out_copy(c):
        part = pl.ds(c * CHUNK, CHUNK)
        return pltpu.make_async_copy(
            tend.at[:, part], tend_hbm.at[:, part], out_sems.at[c]
        )

    def put_weights(layer, k, lanes, block):
        depth = padded[layer]
        high, low = split(block)
        size = block.shape[0]
        cats[layer][k : k + size, lanes] = high
        cats[layer][depth + k : depth + k + size, lanes] = high
        cats[layer][2 * depth + k : 2 * depth + k + size, lanes] = low

    def jobs(layer):
        if layer == 5:
            return [
                (k, slice(n, n + LANES))
                for n in range(0, cats[5].shape[1], LANES)
                for k in range(0, padded[5], LANES)
            ]
        return [(k, slice(0, sizes[layer + 1])) for k in range(0, sizes[layer], 32)]

    def prepare(layer, part, parts):
        work = jobs(layer)
        for k, lanes in work[part * len(work) // parts : (part + 1) * len(work) // parts]:
            if layer == 5:
                put_weights(5, k, lanes, weights_in[5][lanes, k : k + LANES].T)
            else:
                put_weights(layer, k, lanes, weights_in[layer][k : k + 32, lanes] * 0.5)

    def prepare_first(n):
        lanes = slice(n * TILE, (n + 1) * TILE)
        w_tail[0 : aligned - whole, lanes] = weights_in[0][whole:aligned, lanes]
        w_tail[aligned - whole : depth_in - whole, lanes] = weights_in[0][
            aligned:depth_in, lanes
        ]
        for k in range(0, padded[0], LANES):
            source = w_tail[:, lanes] if k >= whole else weights_in[0][k : k + LANES, lanes]
            put_weights(0, k, lanes, source * 0.5)

    def put_units(hold, depth, start, columns, value):
        high, low = split(value)
        size = value.shape[1]
        hold[columns, start : start + size] = high
        hold[columns, depth + start : depth + start + size] = low
        hold[columns, 2 * depth + start : 2 * depth + start + size] = high

    def prepare_inputs(c):
        columns = slice(c * CHUNK, (c + 1) * CHUNK)
        x_tail[0 : aligned - whole, columns] = x_in[whole:aligned, columns]
        x_tail[aligned - whole : depth_in - whole, columns] = x_in[
            aligned:depth_in, columns
        ]
        for m in range(c * CHUNK, (c + 1) * CHUNK, LANES):
            part = slice(m, m + LANES)
            for k in range(0, padded[0], LANES):
                source = x_tail[:, part] if k >= whole else x_in[k : k + LANES, part]
                put_units(hold_a, padded[0], k, part, source.T)

    def product(layer, held, c, units):
        return jnp.dot(
            held[c * CHUNK : (c + 1) * CHUNK, 0 : 3 * padded[layer]],
            cats[layer][:, units],
            preferred_element_type=F32,
        )

    def finish(layer, other, c, units, total):
        value = total + bias_rows[layer : layer + 1, units]
        if layer < 5:
            value = value + value * jnp.tanh(value)
            columns = slice(c * CHUNK, (c + 1) * CHUNK)
            put_units(other, sizes[layer + 1], units.start, columns, value)
            return
        for part in range(CHUNK // LANES):
            r = c * (CHUNK // LANES) + part
            day = inverse[r : r + 1, :] >= 0
            for n in range(units.start, units.stop, LANES):
                block = value[
                    part * LANES : (part + 1) * LANES, n - units.start : n - units.start + LANES
                ].T
                keep = min(LANES, sizes[6] - n)
                shown = jnp.where(day, block[:keep], 0.0)
                tend[n : n + keep, r * LANES : (r + 1) * LANES] = shown
                if n == 0:
                    field[r, 0:levels, :] = (
                        tracer[pl.ds(r, levels, stride=rows), :] + shown[0:levels]
                    )
        if units.stop >= sizes[6]:
            out_copy(c).start()

    x_copy(0).start()
    for n in range(sizes[1] // TILE):
        first_copy(n).start()
    for i in range(10):
        small_copy(i).start()
    for c in range(1, chunks):
        x_copy(c).start()
    w_tail[...] = jnp.zeros(w_tail.shape, F32)
    x_tail[...] = jnp.zeros(x_tail.shape, F32)
    bias_rows[...] = jnp.zeros(bias_rows.shape, F32)
    weights_in[5][sizes[6] :, :] = jnp.zeros(
        (weights_in[5].shape[0] - sizes[6], sizes[5]), F32
    )
    x_copy(0).wait()
    prepare_inputs(0)
    first_copy(0).wait()
    prepare_first(0)
    for layer in range(1, 6):
        w_copy(layer).start()

    pending = None
    held, other = hold_a, hold_b
    for layer in range(6):
        count = cats[layer].shape[1]
        tiles = [slice(n, min(n + TILE, count)) for n in range(0, count, TILE)]
        parts = chunks * len(tiles)
        for c in range(chunks):
            for n, units in enumerate(tiles):
                part = c * len(tiles) + n
                total = product(layer, held, c, units)
                if layer == 0 and c == 0 and n + 1 < len(tiles):
                    first_copy(n + 1).wait()
                    prepare_first(n + 1)
                if layer == 0 and c == 0 and n + 1 == len(tiles):
                    for i in range(1, chunks):
                        x_copy(i).wait()
                        prepare_inputs(i)
                if part == 0 and layer == 0:
                    for i in range(10):
                        small_copy(i).wait()
                    for i in range(6):
                        bias_rows[i : i + 1, 0 : sizes[i + 1]] = biases[i][...].reshape(
                            1, sizes[i + 1]
                        ) * (0.5 if i < 5 else 1.0)
                    for r in range(rows):
                        field[r, levels : levels + 1, :] = along[r : r + 1, :]
                        field[r, levels + 1 : levels + 2, :] = across[r : r + 1, :]
                        field[r, levels + 2 : levels_wide, :] = jnp.zeros(
                            (levels_wide - levels - 2, LANES), F32
                        )
                finish(layer, other, c, units, total)
                if layer == 0 and part >= parts // 2:
                    if part == parts // 2:
                        w_copy(1).wait()
                    prepare(1, part - parts // 2, parts - parts // 2)
                elif 0 < layer < 5:
                    if part == 0:
                        w_copy(layer + 1).wait()
                    prepare(layer + 1, part, parts)
        held, other = other, held

    odd = lax.rem(lax.axis_index(axis), 2)
    pay_a[...] = field[pl.ds((rows - HALO) * odd, HALO)]
    pay_b[...] = field[pl.ds((rows - HALO) * (1 - odd), HALO)]
    for c in range(chunks):
        out_copy(c).wait()


def network(inverse, tracer, along, across, biases, x, weights, axis):
    sizes = [x.shape[0]] + [b.shape[0] for b in biases]
    width = x.shape[1]
    rows = along.shape[0]
    levels = tracer.shape[0] // rows
    levels_wide = round_up(levels + 2, 8)
    chunks = width // CHUNK
    padded = [round_up(s, LANES) for s in sizes[:6]]
    deepest = 3 * max(padded)
    outs = round_up(sizes[6], LANES)
    tail = padded[0] - sizes[0] // LANES * LANES
    vmem, hbm = pl.BlockSpec(memory_space=pltpu.VMEM), pl.BlockSpec(memory_space=pl.ANY)
    total = sum(sizes[i] * sizes[i + 1] for i in range(6)) * width
    return pl.pallas_call(
        functools.partial(network_kernel, sizes=sizes, levels=levels, axis=axis),
        out_shape=(
            jax.ShapeDtypeStruct((sizes[6], width), F32),
            jax.ShapeDtypeStruct((rows, levels_wide, LANES), F32),
            jax.ShapeDtypeStruct((HALO, levels_wide, LANES), F32),
            jax.ShapeDtypeStruct((HALO, levels_wide, LANES), F32),
        ),
        in_specs=[hbm] * 17,
        out_specs=(hbm, vmem, vmem, vmem),
        scratch_shapes=[
            pltpu.VMEM(x.shape, F32),
            *[pltpu.VMEM(w.shape, F32) for w in weights[:5]],
            pltpu.VMEM((outs, sizes[5]), F32),
            *[pltpu.VMEM((3 * padded[i], (sizes[1:6] + [outs])[i]), BF16) for i in range(6)],
            pltpu.VMEM(inverse.shape, jnp.int32),
            pltpu.VMEM(tracer.shape, F32),
            pltpu.VMEM(along.shape, F32),
            pltpu.VMEM(across.shape, F32),
            *[pltpu.VMEM(b.shape, F32) for b in biases],
            pltpu.VMEM((width, deepest), BF16),
            pltpu.VMEM((width, deepest), BF16),
            pltpu.VMEM((tail, sizes[1]), F32),
            pltpu.VMEM((tail, width), F32),
            pltpu.VMEM((8, round_up(max(sizes[1:]), LANES)), F32),
            pltpu.VMEM((sizes[6], width), F32),
            pltpu.SemaphoreType.DMA((chunks,)),
            pltpu.SemaphoreType.DMA((6,)),
            pltpu.SemaphoreType.DMA((chunks,)),
            pltpu.SemaphoreType.DMA((10,)),
            pltpu.SemaphoreType.DMA((sizes[1] // TILE,)),
        ],
        compiler_params=pltpu.CompilerParams(vmem_limit_bytes=NETWORK_VMEM),
        cost_estimate=pl.CostEstimate(
            flops=6 * total, bytes_accessed=14_000_000, transcendentals=3_000_000
        ),
        name="column_network",
    )(inverse, tracer, along, across, *biases, x, *weights)


def half_minmod(first, second):
    return 0.5 * (
        jnp.maximum(jnp.minimum(first, second), 0.0)
        + jnp.minimum(jnp.maximum(first, second), 0.0)
    )


def cat(values):
    return values[0] if len(values) == 1 else jnp.concatenate(values, axis=0)


def advect_kernel(field, got_a, got_b, out, wide, speeds, sem, *, levels, axis):
    rows = field.shape[0]
    odd = lax.rem(lax.axis_index(axis), 2)
    own = pltpu.make_async_copy(field, wide.at[pl.ds(HALO, rows)], sem)
    own.start()
    wide[pl.ds((HALO + rows) * odd, HALO)] = got_a[...]
    wide[pl.ds((HALO + rows) * (1 - odd), HALO)] = got_b[...]

    def place(i):
        for kind in range(2):
            courant = jnp.broadcast_to(
                wide[i, levels + kind : levels + kind + 1, :], (8, LANES)
            )
            speeds[2 * kind, i] = jnp.maximum(courant, 0.0)
            speeds[2 * kind + 1, i] = jnp.minimum(courant, 0.0)

    for i in range(HALO):
        place(i)
        place(HALO + rows + i)
    own.wait()
    for i in range(HALO, HALO + rows):
        place(i)
    groups = wide.shape[1] // GROUP

    def group(g, carry):
        wavefront(g, groups, levels, out, wide, speeds, rows)
        return carry

    lax.fori_loop(0, groups, group, 0)


def wavefront(g, groups, levels, out, wide, speeds, rows):
    base = pl.multiple_of(g * GROUP, GROUP)
    blocks = GROUP // 8
    keep = levels - (groups - 1) * GROUP
    fields = [{}, {}, {}]
    steps, slopes, fluxes = [{}, {}, {}], [{}, {}, {}], [{}, {}, {}]
    reach = [(-4, rows + 3), (-2, rows + 1), (0, rows - 1)]
    shape = (blocks, 8, LANES)

    def load(i):
        return wide[i + HALO, pl.ds(base, GROUP), :].reshape(shape)

    def courant(kind, at):
        return cat([jnp.broadcast_to(speeds[kind, i + HALO], shape) for i in at])

    def pieces(value, count):
        return [value[n * blocks : (n + 1) * blocks] for n in range(count)]

    def face(active, at):
        ahead, behind = courant(0, at), courant(1, at)
        upper = cat([fields[k][i] - slopes[k][i] for k, i in zip(active, at)])
        lower = cat([fields[k][i - 1] + slopes[k][i - 1] for k, i in zip(active, at)])
        return ahead * lower + behind * upper

    rest = []
    for i in range(-HALO, -2):
        fields[0][i] = load(i)
    for t in range(-4, rows + 6):
        active = [k for k in range(3) if reach[k][0] <= t - 3 * k <= reach[k][1]]
        if t + 2 < rows + HALO:
            fields[0][t + 2] = load(t + 2)
        for k in active:
            c = t - 3 * k
            if c == reach[k][0]:
                f = fields[k]
                for i in (c - 1, c, c + 1):
                    steps[k][i] = f[i] - f[i - 1]
                for i in (c - 1, c):
                    slopes[k][i] = half_minmod(steps[k][i + 1], steps[k][i])
                fluxes[k][c] = face([k], [c])
        at = [t - 3 * k for k in active]
        here = cat([fields[k][i] for k, i in zip(active, at)])
        back = here - pltpu.roll(here, 1, 2)
        new = cat(
            [fields[k][i + 2] - fields[k][i + 1] for k, i in zip(active, at)]
        )
        last = cat([steps[k][i + 1] for k, i in zip(active, at)])
        bend = half_minmod(pltpu.roll(back, LANES - 1, 2), back)
        slope = half_minmod(new, last)
        for k, i, a_step, a_slope in zip(
            active, at, pieces(new, len(at)), pieces(slope, len(at))
        ):
            steps[k][i + 2], slopes[k][i + 1] = a_step, a_slope
        side = courant(2, at) * pltpu.roll(here + bend, 1, 2)
        side = side + courant(3, at) * (here - bend)
        flux = face(active, [i + 1 for i in at])
        for k, i, a_flux in zip(active, at, pieces(flux, len(at))):
            fluxes[k][i + 1] = a_flux
        moved = cat([fluxes[k][i] for k, i in zip(active, at)]) - flux
        moved = here + (moved + (side - pltpu.roll(side, LANES - 1, 2)))
        for k, i, value in zip(active, at, pieces(moved, len(at))):
            if k == 0:
                fields[1][i] = value
            elif k == 1:
                fields[2][i] = 0.75 * fields[0][i] + 0.25 * value
            else:
                value = 1.0 / 3.0 * fields[0][i] + 2.0 / 3.0 * value
                value = value.reshape(GROUP, LANES)
                out[pl.ds(base * rows + i, keep, stride=rows), :] = value[:keep]
                rest.append((i, value[keep:]))
    if keep < GROUP:

        @pl.when(g < groups - 1)
        def _():
            for i, value in rest:
                lines = pl.ds((base + keep) * rows + i, GROUP - keep, stride=rows)
                out[lines, :] = value


def advect(field, got_a, got_b, levels, axis):
    rows, levels_wide, across = field.shape
    vmem = pl.BlockSpec(memory_space=pltpu.VMEM)
    return pl.pallas_call(
        functools.partial(advect_kernel, levels=levels, axis=axis),
        out_shape=jax.ShapeDtypeStruct((levels * rows, across), F32),
        in_specs=[pl.BlockSpec(memory_space=pl.ANY), vmem, vmem],
        out_specs=vmem,
        scratch_shapes=[
            pltpu.VMEM((rows + 2 * HALO, levels_wide, across), F32),
            pltpu.VMEM((4, rows + 2 * HALO, 8, across), F32),
            pltpu.SemaphoreType.DMA,
        ],
        compiler_params=pltpu.CompilerParams(vmem_limit_bytes=ADVECT_VMEM),
        name="advect_sections",
    )(field, got_a, got_b)


def shards(inputs, tracer, speed_along, speed_across, inverse_list, *params):
    weights, biases = list(params[0::2]), params[1::2]
    weights[5] = weights[5].T
    levels, rows, across = tracer.shape
    tendencies, field, pay_a, pay_b = network(
        inverse_list.reshape(rows, across),
        tracer.reshape(levels * rows, across),
        speed_along,
        speed_across,
        biases,
        inputs.T,
        weights,
        "gx",
    )
    count = lax.axis_size("gx")
    outer = [(i, (i - 1 if i % 2 == 0 else i + 1) % count) for i in range(count)]
    inner = [(i, i + 1 if i % 2 == 0 else i - 1) for i in range(count)]
    got_a = lax.ppermute(pay_a, "gx", outer)
    got_b = lax.ppermute(pay_b, "gx", inner)
    advected = advect(field, got_a, got_b, levels, "gx")
    return tendencies.T, advected.reshape(levels, rows, across)


def solution(mesh):
    placed = (
        P(("member", "gx"), None),
        P(None, ("member", "gx"), None),
        P(("member", "gx"), None),
        P(("member", "gx"), None),
        P(("member", "gx")),
        *[P()] * 12,
    )
    return jax.shard_map(
        shards,
        mesh=mesh,
        in_specs=placed,
        out_specs=(P(("member", "gx"), None), P(None, ("member", "gx"), None)),
        check_vma=False,
    )
```

```python
import functools
import jax
import jax.numpy as jnp
from jax import lax
from jax.experimental import pallas as pl
from jax.experimental.pallas import tpu as pltpu
from jax.sharding import PartitionSpec as P

F32, BF16, F8 = jnp.float32, jnp.bfloat16, jnp.float8_e4m3fn
LANES = 128
CHUNK = 512
HALO = 6
GROUP = 16
WEIGHT_MAX = (0.25, 0.3125, 0.3125, 0.375, 0.3125, 0.3125)
BIAS_MAX = 3.0
INPUT_MAX = 6.0
SILU_DIP = 0.28
TOP = 440.0
WEIGHT_STEP = 2.0**10
LOW_STEP = 2.0**8
NETWORK_VMEM = 60_000_000
ADVECT_VMEM = 8 * 2**20


def round_up(value, unit):
    return -(-value // unit) * unit


def network_kernel(*refs, sizes, levels, axis):
    small_hbm, x_hbm, weights_hbm, refs = refs[:10], refs[10], refs[11:17], refs[17:]
    (tend_hbm, field, pay_a, pay_b), refs = refs[:4], refs[4:]
    x_in, weights_in, refs = refs[0], refs[1:7], refs[7:]
    cats, cats8, columns, refs = refs[:6], refs[6:12], refs[12:18], refs[18:]
    inverse, tracer, along, across, *biases = refs[:10]
    holds, holds8, refs = refs[10:12], refs[12:14], refs[14:]
    w_tail, x_tail, b_six, tend, peaks, shrinks, *sems = refs
    x_sems, w_sems, out_sems, small_sems = sems

    chunks = x_hbm.shape[1] // CHUNK
    rows, levels_wide = field.shape[0], field.shape[1]
    depth_in = sizes[0]
    aligned = depth_in // 8 * 8
    whole = depth_in // LANES * LANES
    padded = [cats[layer].shape[1] for layer in range(6)]

    def x_copy(c):
        part = pl.ds(c * CHUNK, CHUNK)
        return pltpu.make_async_copy(x_hbm.at[:, part], x_in.at[:, part], x_sems.at[c])

    def w_copy(layer):
        target = weights_in[layer]
        if layer == 5:
            target = target.at[pl.ds(0, sizes[6])]
        return pltpu.make_async_copy(weights_hbm[layer], target, w_sems.at[layer])

    def small_copy(i):
        target = (inverse, tracer, along, across, *biases)[i]
        return pltpu.make_async_copy(small_hbm[i], target, small_sems.at[i])

    def out_copy(c):
        part = pl.ds(c * CHUNK, CHUNK)
        return pltpu.make_async_copy(
            tend.at[:, part], tend_hbm.at[:, part], out_sems.at[c]
        )

    def bias_columns(layer):
        count = sizes[layer + 1]
        source = biases[layer]
        if count % LANES:
            b_six[0:1, :] = jnp.zeros((1, b_six.shape[1]), F32)
            b_six[0:1, 0:count] = source[...].reshape(1, count)
            row = b_six[0:1, :]
        else:
            row = source[...].reshape(1, count)
        scale = 0.5 if layer < 5 else 1.0
        for n in range(0, count, LANES):
            block = jnp.broadcast_to(row[:, n : n + LANES], (LANES, LANES)).T * scale
            columns[layer][n : n + LANES, :] = block

    def put_weights(layer, lines, k, block):
        depth = padded[layer]
        if layer < 5:
            block = block * 0.5
        high = block.astype(BF16)
        low = block - high.astype(F32)
        step = WEIGHT_STEP * (2.0 if layer < 5 else 1.0)
        lanes, far = slice(k, k + LANES), slice(depth + k, depth + k + LANES)
        cats[layer][lines, lanes] = high
        cats8[layer][lines, lanes] = (block * step).astype(F8)
        cats8[layer][lines, far] = (low * (step * LOW_STEP)).astype(F8)

    def prepare(layer, part, parts):
        work = [
            (n, k)
            for n in range(0, round_up(sizes[layer + 1], LANES), LANES)
            for k in range(0, padded[layer], LANES)
        ]
        for n, k in work[part * len(work) // parts : (part + 1) * len(work) // parts]:
            lines, lanes = slice(n, n + LANES), slice(k, k + LANES)
            if layer == 5:
                block = weights_in[5][lines, lanes]
            elif layer == 0 and k >= whole:
                block = w_tail[:, lines].T
            else:
                block = weights_in[layer][lanes, lines].T
            put_weights(layer, lines, k, block)

    def put_rows(layer, start, cols, value, scale):
        depth = padded[layer]
        high = value.astype(BF16)
        low = value - high.astype(F32)
        size = value.shape[0]
        holds[layer % 2][start : start + size, cols] = high
        hold8 = holds8[layer % 2]
        hold8[start : start + size, cols] = (low * (scale * LOW_STEP)).astype(F8)
        hold8[depth + start : depth + start + size, cols] = (value * scale).astype(F8)

    def prepare_inputs(c):
        cols = slice(c * CHUNK, (c + 1) * CHUNK)
        x_tail[0 : aligned - whole, cols] = x_in[whole:aligned, cols]
        x_tail[aligned - whole : depth_in - whole, cols] = x_in[aligned:depth_in, cols]
        for k in range(0, whole, LANES):
            put_rows(0, k, cols, x_in[k : k + LANES, cols], TOP / INPUT_MAX)
        put_rows(0, whole, cols, x_tail[:, cols], TOP / INPUT_MAX)

    def product(layer, c):
        depth = padded[layer]
        cols = slice(c * CHUNK, (c + 1) * CHUNK)
        main = jnp.dot(
            cats[layer][...],
            holds[layer % 2][0:depth, cols],
            preferred_element_type=F32,
        )
        rest = jnp.dot(
            cats8[layer][...],
            holds8[layer % 2][0 : 2 * depth, cols],
            preferred_element_type=F32,
        )
        return main, rest

    def finish(layer, c, main, rest):
        cols = slice(c * CHUNK, (c + 1) * CHUNK)
        unit = 1.0 / (WEIGHT_STEP * LOW_STEP * (2.0 if layer < 5 else 1.0))
        if layer == 0:
            shrink, peak = jnp.full((1, CHUNK), INPUT_MAX / TOP, F32), INPUT_MAX
        else:
            shrink, peak = shrinks[layer : layer + 1, cols], peaks[layer : layer + 1, cols]
        bias = columns[layer][...]
        value = main + rest * (shrink * unit)
        value = value + jnp.concatenate([bias] * (CHUNK // LANES), axis=1)
        if layer < 5:
            value = value + value * jnp.tanh(value)
            limit = (sizes[layer] * WEIGHT_MAX[layer]) * peak + BIAS_MAX
            limit = jnp.broadcast_to(jnp.asarray(limit, F32), (1, CHUNK))
            put_rows(layer + 1, 0, cols, value, TOP / limit)
            shrinks[layer + 1 : layer + 2, cols] = limit / TOP
            highest = jnp.max(value, axis=0, keepdims=True)
            peaks[layer + 1 : layer + 2, cols] = jnp.maximum(highest, SILU_DIP)
            return
        for part in range(CHUNK // LANES):
            r = c * (CHUNK // LANES) + part
            day = inverse[r : r + 1, :] >= 0
            shown = jnp.where(
                day, value[: sizes[6], part * LANES : (part + 1) * LANES], 0.0
            )
            tend[:, r * LANES : (r + 1) * LANES] = shown
            field[r, 0:levels, :] = (
                tracer[pl.ds(r, levels, stride=rows), :] + shown[0:levels]
            )
        out_copy(c).start()

    w_copy(0).start()
    for c in range(chunks):
        x_copy(c).start()
    for i in range(10):
        small_copy(i).start()
    w_copy(1).start()
    w_tail[...] = jnp.zeros(w_tail.shape, F32)
    x_tail[...] = jnp.zeros(x_tail.shape, F32)
    weights_in[5][sizes[6] :, :] = jnp.zeros(
        (weights_in[5].shape[0] - sizes[6], sizes[5]), F32
    )
    w_copy(0).wait()
    w_tail[0 : aligned - whole, :] = weights_in[0][whole:aligned, :]
    w_tail[aligned - whole : depth_in - whole, :] = weights_in[0][aligned:depth_in, :]
    prepare(0, 0, 1)
    for layer in range(2, 6):
        w_copy(layer).start()
    for c in range(chunks):
        x_copy(c).wait()
        prepare_inputs(c)
    for i in range(10):
        small_copy(i).wait()
    for layer in range(6):
        bias_columns(layer)
    for r in range(rows):
        field[r, levels : levels + 1, :] = along[r : r + 1, :]
        field[r, levels + 1 : levels + 2, :] = across[r : r + 1, :]
        field[r, levels + 2 : levels_wide, :] = jnp.zeros(
            (levels_wide - levels - 2, LANES), F32
        )

    for layer in range(6):
        if layer < 5:
            w_copy(layer + 1).wait()
        for c in range(chunks):
            main, rest = product(layer, c)
            if layer < 5:
                prepare(layer + 1, c, chunks)
            finish(layer, c, main, rest)

    odd = lax.rem(lax.axis_index(axis), 2)
    pay_a[...] = field[pl.ds((rows - HALO) * odd, HALO)]
    pay_b[...] = field[pl.ds((rows - HALO) * (1 - odd), HALO)]
    for c in range(chunks):
        out_copy(c).wait()


def network(inverse, tracer, along, across, biases, x, weights, axis):
    sizes = [x.shape[0]] + [b.shape[0] for b in biases]
    width = x.shape[1]
    rows = along.shape[0]
    levels = tracer.shape[0] // rows
    levels_wide = round_up(levels + 2, 8)
    chunks = width // CHUNK
    padded = [round_up(s, LANES) for s in sizes]
    deepest = max(padded[:6])
    tail = padded[0] - sizes[0] // LANES * LANES
    vmem, hbm = pl.BlockSpec(memory_space=pltpu.VMEM), pl.BlockSpec(memory_space=pl.ANY)
    total = sum(sizes[i] * sizes[i + 1] for i in range(6)) * width
    return pl.pallas_call(
        functools.partial(network_kernel, sizes=sizes, levels=levels, axis=axis),
        out_shape=(
            jax.ShapeDtypeStruct((sizes[6], width), F32),
            jax.ShapeDtypeStruct((rows, levels_wide, LANES), F32),
            jax.ShapeDtypeStruct((HALO, levels_wide, LANES), F32),
            jax.ShapeDtypeStruct((HALO, levels_wide, LANES), F32),
        ),
        in_specs=[hbm] * 17,
        out_specs=(hbm, vmem, vmem, vmem),
        scratch_shapes=[
            pltpu.VMEM(x.shape, F32),
            *[pltpu.VMEM(w.shape, F32) for w in weights[:5]],
            pltpu.VMEM((padded[6], sizes[5]), F32),
            *[pltpu.VMEM((padded[i + 1], padded[i]), BF16) for i in range(6)],
            *[pltpu.VMEM((padded[i + 1], 2 * padded[i]), F8) for i in range(6)],
            *[pltpu.VMEM((padded[i + 1], LANES), F32) for i in range(6)],
            pltpu.VMEM(inverse.shape, jnp.int32),
            pltpu.VMEM(tracer.shape, F32),
            pltpu.VMEM(along.shape, F32),
            pltpu.VMEM(across.shape, F32),
            *[pltpu.VMEM(b.shape, F32) for b in biases],
            *[pltpu.VMEM((deepest, width), BF16)] * 2,
            *[pltpu.VMEM((2 * deepest, width), F8)] * 2,
            pltpu.VMEM((tail, sizes[1]), F32),
            pltpu.VMEM((tail, width), F32),
            pltpu.VMEM((8, padded[6]), F32),
            pltpu.VMEM((sizes[6], width), F32),
            pltpu.VMEM((8, width), F32),
            pltpu.VMEM((8, width), F32),
            pltpu.SemaphoreType.DMA((chunks,)),
            pltpu.SemaphoreType.DMA((6,)),
            pltpu.SemaphoreType.DMA((chunks,)),
            pltpu.SemaphoreType.DMA((10,)),
        ],
        compiler_params=pltpu.CompilerParams(vmem_limit_bytes=NETWORK_VMEM),
        cost_estimate=pl.CostEstimate(
            flops=4 * total, bytes_accessed=14_000_000, transcendentals=3_000_000
        ),
        name="column_network",
    )(inverse, tracer, along, across, *biases, x, *weights)


def half_minmod(first, second):
    return 0.5 * (
        jnp.maximum(jnp.minimum(first, second), 0.0)
        + jnp.minimum(jnp.maximum(first, second), 0.0)
    )


def cat(values):
    return values[0] if len(values) == 1 else jnp.concatenate(values, axis=0)


def advect_kernel(field, got_a, got_b, out, wide, speeds, sem, *, levels, axis):
    rows = field.shape[0]
    odd = lax.rem(lax.axis_index(axis), 2)
    own = pltpu.make_async_copy(field, wide.at[pl.ds(HALO, rows)], sem)
    own.start()
    wide[pl.ds((HALO + rows) * odd, HALO)] = got_a[...]
    wide[pl.ds((HALO + rows) * (1 - odd), HALO)] = got_b[...]

    def place(i):
        for kind in range(2):
            courant = jnp.broadcast_to(
                wide[i, levels + kind : levels + kind + 1, :], (8, LANES)
            )
            speeds[2 * kind, i] = jnp.maximum(courant, 0.0)
            speeds[2 * kind + 1, i] = jnp.minimum(courant, 0.0)

    for i in range(HALO):
        place(i)
        place(HALO + rows + i)
    own.wait()
    for i in range(HALO, HALO + rows):
        place(i)
    groups = wide.shape[1] // GROUP

    def group(g, carry):
        wavefront(g, groups, levels, out, wide, speeds, rows)
        return carry

    lax.fori_loop(0, groups, group, 0)


def wavefront(g, groups, levels, out, wide, speeds, rows):
    base = pl.multiple_of(g * GROUP, GROUP)
    blocks = GROUP // 8
    keep = levels - (groups - 1) * GROUP
    fields = [{}, {}, {}]
    steps, slopes, fluxes = [{}, {}, {}], [{}, {}, {}], [{}, {}, {}]
    reach = [(-4, rows + 3), (-2, rows + 1), (0, rows - 1)]
    shape = (blocks, 8, LANES)

    def load(i):
        return wide[i + HALO, pl.ds(base, GROUP), :].reshape(shape)

    def courant(kind, at):
        return cat([jnp.broadcast_to(speeds[kind, i + HALO], shape) for i in at])

    def pieces(value, count):
        return [value[n * blocks : (n + 1) * blocks] for n in range(count)]

    def face(active, at):
        ahead, behind = courant(0, at), courant(1, at)
        upper = cat([fields[k][i] - slopes[k][i] for k, i in zip(active, at)])
        lower = cat([fields[k][i - 1] + slopes[k][i - 1] for k, i in zip(active, at)])
        return ahead * lower + behind * upper

    rest = []
    for i in range(-HALO, -2):
        fields[0][i] = load(i)
    for t in range(-4, rows + 6):
        active = [k for k in range(3) if reach[k][0] <= t - 3 * k <= reach[k][1]]
        if t + 2 < rows + HALO:
            fields[0][t + 2] = load(t + 2)
        for k in active:
            c = t - 3 * k
            if c == reach[k][0]:
                f = fields[k]
                for i in (c - 1, c, c + 1):
                    steps[k][i] = f[i] - f[i - 1]
                for i in (c - 1, c):
                    slopes[k][i] = half_minmod(steps[k][i + 1], steps[k][i])
                fluxes[k][c] = face([k], [c])
        at = [t - 3 * k for k in active]
        here = cat([fields[k][i] for k, i in zip(active, at)])
        back = here - pltpu.roll(here, 1, 2)
        new = cat(
            [fields[k][i + 2] - fields[k][i + 1] for k, i in zip(active, at)]
        )
        last = cat([steps[k][i + 1] for k, i in zip(active, at)])
        bend = half_minmod(pltpu.roll(back, LANES - 1, 2), back)
        slope = half_minmod(new, last)
        for k, i, a_step, a_slope in zip(
            active, at, pieces(new, len(at)), pieces(slope, len(at))
        ):
            steps[k][i + 2], slopes[k][i + 1] = a_step, a_slope
        side = courant(2, at) * pltpu.roll(here + bend, 1, 2)
        side = side + courant(3, at) * (here - bend)
        flux = face(active, [i + 1 for i in at])
        for k, i, a_flux in zip(active, at, pieces(flux, len(at))):
            fluxes[k][i + 1] = a_flux
        moved = cat([fluxes[k][i] for k, i in zip(active, at)]) - flux
        moved = here + (moved + (side - pltpu.roll(side, LANES - 1, 2)))
        for k, i, value in zip(active, at, pieces(moved, len(at))):
            if k == 0:
                fields[1][i] = value
            elif k == 1:
                fields[2][i] = 0.75 * fields[0][i] + 0.25 * value
            else:
                value = 1.0 / 3.0 * fields[0][i] + 2.0 / 3.0 * value
                value = value.reshape(GROUP, LANES)
                out[pl.ds(base * rows + i, keep, stride=rows), :] = value[:keep]
                rest.append((i, value[keep:]))
    if keep < GROUP:

        @pl.when(g < groups - 1)
        def _():
            for i, value in rest:
                lines = pl.ds((base + keep) * rows + i, GROUP - keep, stride=rows)
                out[lines, :] = value


def advect(field, got_a, got_b, levels, axis):
    rows, levels_wide, across = field.shape
    vmem = pl.BlockSpec(memory_space=pltpu.VMEM)
    return pl.pallas_call(
        functools.partial(advect_kernel, levels=levels, axis=axis),
        out_shape=jax.ShapeDtypeStruct((levels * rows, across), F32),
        in_specs=[pl.BlockSpec(memory_space=pl.ANY), vmem, vmem],
        out_specs=vmem,
        scratch_shapes=[
            pltpu.VMEM((rows + 2 * HALO, levels_wide, across), F32),
            pltpu.VMEM((4, rows + 2 * HALO, 8, across), F32),
            pltpu.SemaphoreType.DMA,
        ],
        compiler_params=pltpu.CompilerParams(vmem_limit_bytes=ADVECT_VMEM),
        name="advect_sections",
    )(field, got_a, got_b)


def shards(inputs, tracer, speed_along, speed_across, inverse_list, *params):
    weights, biases = list(params[0::2]), params[1::2]
    weights[5] = weights[5].T
    levels, rows, across = tracer.shape
    tendencies, field, pay_a, pay_b = network(
        inverse_list.reshape(rows, across),
        tracer.reshape(levels * rows, across),
        speed_along,
        speed_across,
        biases,
        inputs.T,
        weights,
        "gx",
    )
    count = lax.axis_size("gx")
    outer = [(i, (i - 1 if i % 2 == 0 else i + 1) % count) for i in range(count)]
    inner = [(i, i + 1 if i % 2 == 0 else i - 1) for i in range(count)]
    got_a = lax.ppermute(pay_a, "gx", outer)
    got_b = lax.ppermute(pay_b, "gx", inner)
    advected = advect(field, got_a, got_b, levels, "gx")
    return tendencies.T, advected.reshape(levels, rows, across)


def solution(mesh):
    placed = (
        P(("member", "gx"), None),
        P(None, ("member", "gx"), None),
        P(("member", "gx"), None),
        P(("member", "gx"), None),
        P(("member", "gx")),
        *[P()] * 12,
    )
    return jax.shard_map(
        shards,
        mesh=mesh,
        in_specs=placed,
        out_specs=(P(("member", "gx"), None), P(None, ("member", "gx"), None)),
        check_vma=False,
    )
```

```python
import functools
import jax
import jax.numpy as jnp
from jax import lax
from jax.experimental import pallas as pl
from jax.experimental.pallas import tpu as pltpu
from jax.sharding import PartitionSpec as P

F32, BF16, F8 = jnp.float32, jnp.bfloat16, jnp.float8_e4m3fn
LANES = 128
CHUNK = 512
HALO = 6
GROUP = 32
WEIGHT_MAX = (0.25, 0.3125, 0.3125, 0.375, 0.3125, 0.3125)
BIAS_MAX = 3.0
INPUT_MAX = 6.0
SILU_DIP = 0.28
TOP = 440.0
WEIGHT_STEP = 2.0**10
LOW_STEP = 2.0**8
NETWORK_VMEM = 60_000_000
ADVECT_VMEM = 8 * 2**20


def round_up(value, unit):
    return -(-value // unit) * unit


def network_kernel(*refs, sizes, levels, axis):
    small_hbm, x_hbm, weights_hbm, refs = refs[:10], refs[10], refs[11:17], refs[17:]
    (tend_hbm, field_hbm, pay_a, pay_b), refs = refs[:4], refs[4:]
    x_in, weights_in, refs = refs[0], refs[1:7], refs[7:]
    cats, cats8, columns, refs = refs[:6], refs[6:12], refs[12:18], refs[18:]
    inverse, tracer, along, across, *biases = refs[:10]
    holds, holds8, refs = refs[10:12], refs[12:14], refs[14:]
    w_tail, x_tail, b_six, tend, peaks, shrinks, field, *sems = refs
    x_sems, w_sems, out_sems, small_sems, field_sems = sems

    chunks = x_hbm.shape[1] // CHUNK
    rows, levels_wide = field.shape[0], field.shape[1]
    depth_in = sizes[0]
    aligned = depth_in // 8 * 8
    whole = depth_in // LANES * LANES
    padded = [cats[layer].shape[1] for layer in range(6)]

    def x_copy(c):
        part = pl.ds(c * CHUNK, CHUNK)
        return pltpu.make_async_copy(x_hbm.at[:, part], x_in.at[:, part], x_sems.at[c])

    def w_copy(layer):
        target = weights_in[layer]
        if layer == 5:
            target = target.at[pl.ds(0, sizes[6])]
        return pltpu.make_async_copy(weights_hbm[layer], target, w_sems.at[layer])

    def small_copy(i):
        target = (inverse, tracer, along, across, *biases)[i]
        return pltpu.make_async_copy(small_hbm[i], target, small_sems.at[i])

    def out_copy(c):
        part = pl.ds(c * CHUNK, CHUNK)
        return pltpu.make_async_copy(
            tend.at[:, part], tend_hbm.at[:, part], out_sems.at[c]
        )

    def bias_columns(layer):
        count = sizes[layer + 1]
        source = biases[layer]
        if count % LANES:
            b_six[0:1, :] = jnp.zeros((1, b_six.shape[1]), F32)
            b_six[0:1, 0:count] = source[...].reshape(1, count)
            row = b_six[0:1, :]
        else:
            row = source[...].reshape(1, count)
        scale = 0.5 if layer < 5 else 1.0
        for n in range(0, count, LANES):
            block = jnp.broadcast_to(row[:, n : n + LANES], (LANES, LANES)).T * scale
            columns[layer][n : n + LANES, :] = block

    def put_weights(layer, lines, k, block):
        depth = padded[layer]
        if layer < 5:
            block = block * 0.5
        high = block.astype(BF16)
        low = block - high.astype(F32)
        step = WEIGHT_STEP * (2.0 if layer < 5 else 1.0)
        lanes, far = slice(k, k + LANES), slice(depth + k, depth + k + LANES)
        cats[layer][lines, lanes] = high
        cats8[layer][lines, lanes] = (block * step).astype(F8)
        cats8[layer][lines, far] = (low * (step * LOW_STEP)).astype(F8)

    def prepare(layer, part, parts):
        work = [
            (n, k)
            for n in range(0, round_up(sizes[layer + 1], LANES), LANES)
            for k in range(0, padded[layer], LANES)
        ]
        for n, k in work[part * len(work) // parts : (part + 1) * len(work) // parts]:
            lines, lanes = slice(n, n + LANES), slice(k, k + LANES)
            if layer == 5:
                block = weights_in[5][lines, lanes]
            elif layer == 0 and k >= whole:
                block = w_tail[:, lines].T
            else:
                block = weights_in[layer][lanes, lines].T
            put_weights(layer, lines, k, block)

    def put_rows(layer, start, cols, value, scale):
        depth = padded[layer]
        high = value.astype(BF16)
        low = value - high.astype(F32)
        size = value.shape[0]
        holds[layer % 2][start : start + size, cols] = high
        hold8 = holds8[layer % 2]
        hold8[start : start + size, cols] = (low * (scale * LOW_STEP)).astype(F8)
        hold8[depth + start : depth + start + size, cols] = (value * scale).astype(F8)

    def prepare_inputs(c):
        cols = slice(c * CHUNK, (c + 1) * CHUNK)
        x_tail[0 : aligned - whole, cols] = x_in[whole:aligned, cols]
        x_tail[aligned - whole : depth_in - whole, cols] = x_in[aligned:depth_in, cols]
        for k in range(0, whole, LANES):
            put_rows(0, k, cols, x_in[k : k + LANES, cols], TOP / INPUT_MAX)
        put_rows(0, whole, cols, x_tail[:, cols], TOP / INPUT_MAX)

    def product(layer, c):
        depth = padded[layer]
        cols = slice(c * CHUNK, (c + 1) * CHUNK)
        main = jnp.dot(
            cats[layer][...],
            holds[layer % 2][0:depth, cols],
            preferred_element_type=F32,
        )
        rest = jnp.dot(
            cats8[layer][...],
            holds8[layer % 2][0 : 2 * depth, cols],
            preferred_element_type=F32,
        )
        return main, rest

    def finish(layer, c, main, rest):
        cols = slice(c * CHUNK, (c + 1) * CHUNK)
        unit = 1.0 / (WEIGHT_STEP * LOW_STEP * (2.0 if layer < 5 else 1.0))
        if layer == 0:
            shrink, peak = jnp.full((1, CHUNK), INPUT_MAX / TOP, F32), INPUT_MAX
        else:
            shrink, peak = shrinks[layer : layer + 1, cols], peaks[layer : layer + 1, cols]
        bias = columns[layer][...]
        value = main + rest * (shrink * unit)
        value = value + jnp.concatenate([bias] * (CHUNK // LANES), axis=1)
        if layer < 5:
            value = value + value * jnp.tanh(value)
            limit = (sizes[layer] * WEIGHT_MAX[layer]) * peak + BIAS_MAX
            limit = jnp.broadcast_to(jnp.asarray(limit, F32), (1, CHUNK))
            put_rows(layer + 1, 0, cols, value, TOP / limit)
            shrinks[layer + 1 : layer + 2, cols] = limit / TOP
            highest = jnp.max(value, axis=0, keepdims=True)
            peaks[layer + 1 : layer + 2, cols] = jnp.maximum(highest, SILU_DIP)
            return
        for part in range(CHUNK // LANES):
            r = c * (CHUNK // LANES) + part
            day = inverse[r : r + 1, :] >= 0
            shown = jnp.where(
                day, value[: sizes[6], part * LANES : (part + 1) * LANES], 0.0
            )
            tend[:, r * LANES : (r + 1) * LANES] = shown
            field[r, 0:levels, :] = (
                tracer[pl.ds(r, levels, stride=rows), :] + shown[0:levels]
            )
        out_copy(c).start()

    w_copy(0).start()
    for c in range(chunks):
        x_copy(c).start()
    for i in range(10):
        small_copy(i).start()
    w_copy(1).start()
    w_tail[...] = jnp.zeros(w_tail.shape, F32)
    x_tail[...] = jnp.zeros(x_tail.shape, F32)
    weights_in[5][sizes[6] :, :] = jnp.zeros(
        (weights_in[5].shape[0] - sizes[6], sizes[5]), F32
    )
    w_copy(0).wait()
    w_tail[0 : aligned - whole, :] = weights_in[0][whole:aligned, :]
    w_tail[aligned - whole : depth_in - whole, :] = weights_in[0][aligned:depth_in, :]
    prepare(0, 0, 1)
    for layer in range(2, 6):
        w_copy(layer).start()
    x_copy(0).wait()
    prepare_inputs(0)

    for layer in range(6):
        if 0 < layer < 5:
            w_copy(layer + 1).wait()
        for c in range(chunks):
            main, rest = product(layer, c)
            if layer == 0 and c == 0:
                for i in range(10):
                    small_copy(i).wait()
                bias_columns(0)
                for i in range(1, chunks):
                    x_copy(i).wait()
                    prepare_inputs(i)
                w_copy(1).wait()
            if layer < 5:
                prepare(layer + 1, c, chunks)
                if c == chunks - 1:
                    bias_columns(layer + 1)
            if layer == 4 and c == 0:
                for r in range(rows):
                    field[r, levels : levels + 1, :] = along[r : r + 1, :]
                    field[r, levels + 1 : levels + 2, :] = across[r : r + 1, :]
                    field[r, levels + 2 : levels_wide, :] = jnp.zeros(
                        (levels_wide - levels - 2, LANES), F32
                    )
            finish(layer, c, main, rest)

    odd = lax.rem(lax.axis_index(axis), 2)
    leaving = [
        pltpu.make_async_copy(
            field.at[pl.ds((rows - HALO) * odd, HALO)], pay_a, field_sems.at[0]
        ),
        pltpu.make_async_copy(
            field.at[pl.ds((rows - HALO) * (1 - odd), HALO)], pay_b, field_sems.at[1]
        ),
        pltpu.make_async_copy(field, field_hbm, field_sems.at[2]),
    ]
    for copy in leaving:
        copy.start()
    for copy in leaving:
        copy.wait()
    for c in range(chunks):
        out_copy(c).wait()


def network(inverse, tracer, along, across, biases, x, weights, axis):
    sizes = [x.shape[0]] + [b.shape[0] for b in biases]
    width = x.shape[1]
    rows = along.shape[0]
    levels = tracer.shape[0] // rows
    levels_wide = round_up(levels + 2, 8)
    chunks = width // CHUNK
    padded = [round_up(s, LANES) for s in sizes]
    deepest = max(padded[:6])
    tail = padded[0] - sizes[0] // LANES * LANES
    hbm = pl.BlockSpec(memory_space=pl.ANY)
    total = sum(sizes[i] * sizes[i + 1] for i in range(6)) * width
    return pl.pallas_call(
        functools.partial(network_kernel, sizes=sizes, levels=levels, axis=axis),
        out_shape=(
            jax.ShapeDtypeStruct((sizes[6], width), F32),
            jax.ShapeDtypeStruct((rows, levels_wide, LANES), F32),
            jax.ShapeDtypeStruct((HALO, levels_wide, LANES), F32),
            jax.ShapeDtypeStruct((HALO, levels_wide, LANES), F32),
        ),
        in_specs=[hbm] * 17,
        out_specs=(hbm,) * 4,
        scratch_shapes=[
            pltpu.VMEM(x.shape, F32),
            *[pltpu.VMEM(w.shape, F32) for w in weights[:5]],
            pltpu.VMEM((padded[6], sizes[5]), F32),
            *[pltpu.VMEM((padded[i + 1], padded[i]), BF16) for i in range(6)],
            *[pltpu.VMEM((padded[i + 1], 2 * padded[i]), F8) for i in range(6)],
            *[pltpu.VMEM((padded[i + 1], LANES), F32) for i in range(6)],
            pltpu.VMEM(inverse.shape, jnp.int32),
            pltpu.VMEM(tracer.shape, F32),
            pltpu.VMEM(along.shape, F32),
            pltpu.VMEM(across.shape, F32),
            *[pltpu.VMEM(b.shape, F32) for b in biases],
            *[pltpu.VMEM((deepest, width), BF16)] * 2,
            *[pltpu.VMEM((2 * deepest, width), F8)] * 2,
            pltpu.VMEM((tail, sizes[1]), F32),
            pltpu.VMEM((tail, width), F32),
            pltpu.VMEM((8, padded[6]), F32),
            pltpu.VMEM((sizes[6], width), F32),
            pltpu.VMEM((8, width), F32),
            pltpu.VMEM((8, width), F32),
            pltpu.VMEM((rows, levels_wide, LANES), F32),
            pltpu.SemaphoreType.DMA((chunks,)),
            pltpu.SemaphoreType.DMA((6,)),
            pltpu.SemaphoreType.DMA((chunks,)),
            pltpu.SemaphoreType.DMA((10,)),
            pltpu.SemaphoreType.DMA((3,)),
        ],
        compiler_params=pltpu.CompilerParams(vmem_limit_bytes=NETWORK_VMEM),
        cost_estimate=pl.CostEstimate(
            flops=4 * total, bytes_accessed=14_000_000, transcendentals=3_000_000
        ),
        name="column_network",
    )(inverse, tracer, along, across, *biases, x, *weights)


def half_minmod(first, second):
    return 0.5 * (
        jnp.maximum(jnp.minimum(first, second), 0.0)
        + jnp.minimum(jnp.maximum(first, second), 0.0)
    )


def cat(values):
    return values[0] if len(values) == 1 else jnp.concatenate(values, axis=0)


def advect_kernel(field, got_a, got_b, out, wide, speeds, sem, *, levels, axis):
    rows = field.shape[0]
    odd = lax.rem(lax.axis_index(axis), 2)
    own = pltpu.make_async_copy(field, wide.at[pl.ds(HALO, rows)], sem)
    own.start()
    wide[pl.ds((HALO + rows) * odd, HALO)] = got_a[...]
    wide[pl.ds((HALO + rows) * (1 - odd), HALO)] = got_b[...]

    def place(i):
        for kind in range(2):
            courant = jnp.broadcast_to(
                wide[i, levels + kind : levels + kind + 1, :], (8, LANES)
            )
            speeds[2 * kind, i] = jnp.maximum(courant, 0.0)
            speeds[2 * kind + 1, i] = jnp.minimum(courant, 0.0)

    for i in range(HALO):
        place(i)
        place(HALO + rows + i)
    own.wait()
    for i in range(HALO, HALO + rows):
        place(i)
    groups = wide.shape[1] // GROUP

    def group(g, carry):
        wavefront(g, groups, levels, out, wide, speeds, rows)
        return carry

    lax.fori_loop(0, groups, group, 0)


def wavefront(g, groups, levels, out, wide, speeds, rows):
    base = pl.multiple_of(g * GROUP, GROUP)
    blocks = GROUP // 8
    keep = levels - (groups - 1) * GROUP
    fields = [{}, {}, {}]
    steps, slopes, fluxes = [{}, {}, {}], [{}, {}, {}], [{}, {}, {}]
    reach = [(-4, rows + 3), (-2, rows + 1), (0, rows - 1)]
    shape = (blocks, 8, LANES)

    def load(i):
        return wide[i + HALO, pl.ds(base, GROUP), :].reshape(shape)

    def courant(kind, at):
        return cat([jnp.broadcast_to(speeds[kind, i + HALO], shape) for i in at])

    def pieces(value, count):
        return [value[n * blocks : (n + 1) * blocks] for n in range(count)]

    def face(active, at):
        ahead, behind = courant(0, at), courant(1, at)
        upper = cat([fields[k][i] - slopes[k][i] for k, i in zip(active, at)])
        lower = cat([fields[k][i - 1] + slopes[k][i - 1] for k, i in zip(active, at)])
        return ahead * lower + behind * upper

    rest = []
    for i in range(-HALO, -2):
        fields[0][i] = load(i)
    for t in range(-4, rows + 6):
        active = [k for k in range(3) if reach[k][0] <= t - 3 * k <= reach[k][1]]
        if t + 2 < rows + HALO:
            fields[0][t + 2] = load(t + 2)
        for k in active:
            c = t - 3 * k
            if c == reach[k][0]:
                f = fields[k]
                for i in (c - 1, c, c + 1):
                    steps[k][i] = f[i] - f[i - 1]
                for i in (c - 1, c):
                    slopes[k][i] = half_minmod(steps[k][i + 1], steps[k][i])
                fluxes[k][c] = face([k], [c])
        at = [t - 3 * k for k in active]
        here = cat([fields[k][i] for k, i in zip(active, at)])
        back = here - pltpu.roll(here, 1, 2)
        new = cat(
            [fields[k][i + 2] - fields[k][i + 1] for k, i in zip(active, at)]
        )
        last = cat([steps[k][i + 1] for k, i in zip(active, at)])
        bend = half_minmod(pltpu.roll(back, LANES - 1, 2), back)
        slope = half_minmod(new, last)
        for k, i, a_step, a_slope in zip(
            active, at, pieces(new, len(at)), pieces(slope, len(at))
        ):
            steps[k][i + 2], slopes[k][i + 1] = a_step, a_slope
        side = courant(2, at) * pltpu.roll(here + bend, 1, 2)
        side = side + courant(3, at) * (here - bend)
        flux = face(active, [i + 1 for i in at])
        for k, i, a_flux in zip(active, at, pieces(flux, len(at))):
            fluxes[k][i + 1] = a_flux
        moved = cat([fluxes[k][i] for k, i in zip(active, at)]) - flux
        moved = here + (moved + (side - pltpu.roll(side, LANES - 1, 2)))
        for k, i, value in zip(active, at, pieces(moved, len(at))):
            if k == 0:
                fields[1][i] = value
            elif k == 1:
                fields[2][i] = 0.75 * fields[0][i] + 0.25 * value
            else:
                value = 1.0 / 3.0 * fields[0][i] + 2.0 / 3.0 * value
                value = value.reshape(GROUP, LANES)
                out[pl.ds(base * rows + i, keep, stride=rows), :] = value[:keep]
                rest.append((i, value[keep:]))
    if keep < GROUP:

        @pl.when(g < groups - 1)
        def _():
            for i, value in rest:
                lines = pl.ds((base + keep) * rows + i, GROUP - keep, stride=rows)
                out[lines, :] = value


def advect(field, got_a, got_b, levels, axis):
    rows, levels_wide, across = field.shape
    vmem = pl.BlockSpec(memory_space=pltpu.VMEM)
    return pl.pallas_call(
        functools.partial(advect_kernel, levels=levels, axis=axis),
        out_shape=jax.ShapeDtypeStruct((levels * rows, across), F32),
        in_specs=[pl.BlockSpec(memory_space=pl.ANY), vmem, vmem],
        out_specs=vmem,
        scratch_shapes=[
            pltpu.VMEM((rows + 2 * HALO, levels_wide, across), F32),
            pltpu.VMEM((4, rows + 2 * HALO, 8, across), F32),
            pltpu.SemaphoreType.DMA,
        ],
        compiler_params=pltpu.CompilerParams(vmem_limit_bytes=ADVECT_VMEM),
        name="advect_sections",
    )(field, got_a, got_b)


def shards(inputs, tracer, speed_along, speed_across, inverse_list, *params):
    weights, biases = list(params[0::2]), params[1::2]
    weights[5] = weights[5].T
    levels, rows, across = tracer.shape
    tendencies, field, pay_a, pay_b = network(
        inverse_list.reshape(rows, across),
        tracer.reshape(levels * rows, across),
        speed_along,
        speed_across,
        biases,
        inputs.T,
        weights,
        "gx",
    )
    count = lax.axis_size("gx")
    outer = [(i, (i - 1 if i % 2 == 0 else i + 1) % count) for i in range(count)]
    inner = [(i, i + 1 if i % 2 == 0 else i - 1) for i in range(count)]
    got_a = lax.ppermute(pay_a, "gx", outer)
    got_b = lax.ppermute(pay_b, "gx", inner)
    advected = advect(field, got_a, got_b, levels, "gx")
    return tendencies.T, advected.reshape(levels, rows, across)


def solution(mesh):
    placed = (
        P(("member", "gx"), None),
        P(None, ("member", "gx"), None),
        P(("member", "gx"), None),
        P(("member", "gx"), None),
        P(("member", "gx")),
        *[P()] * 12,
    )
    return jax.shard_map(
        shards,
        mesh=mesh,
        in_specs=placed,
        out_specs=(P(("member", "gx"), None), P(None, ("member", "gx"), None)),
        check_vma=False,
    )
```

```python
import functools
import jax
import jax.numpy as jnp
from jax import lax
from jax.experimental import pallas as pl
from jax.experimental.pallas import tpu as pltpu
from jax.sharding import PartitionSpec as P

F32, BF16, F8 = jnp.float32, jnp.bfloat16, jnp.float8_e4m3fn
LANES = 128
CHUNK = 512
HALO = 6
GROUP = 32
FIRST = 256
WEIGHT_MAX = (0.25, 0.3125, 0.3125, 0.375, 0.3125, 0.3125)
BIAS_MAX = 3.0
INPUT_MAX = 6.0
SILU_DIP = 0.28
TOP = 440.0
WEIGHT_STEP = 2.0**10
LOW_STEP = 2.0**8
NETWORK_VMEM = 60_000_000
ADVECT_VMEM = 54_000_000
ROOM = 128


def round_up(value, unit):
    return -(-value // unit) * unit


def network_kernel(*refs, sizes, levels, axis):
    small_hbm, x_hbm, weights_hbm, refs = refs[:10], refs[10], refs[11:17], refs[17:]
    (tend_hbm, field_hbm, pay_a, pay_b), refs = refs[:4], refs[4:]
    x_in, weights_in, refs = refs[0], refs[1:7], refs[7:]
    cats, cats8, columns, refs = refs[:6], refs[6:12], refs[12:18], refs[18:]
    inverse, tracer, along, across, *biases = refs[:10]
    holds, holds8, refs = refs[10:12], refs[12:14], refs[14:]
    w_tail, x_tail, b_six, tend, peaks, shrinks, field, *sems = refs
    x_sems, w_sems, out_sems, small_sems, field_sems, first_sems = sems

    chunks = x_hbm.shape[1] // CHUNK
    rows, levels_wide = field.shape[0], field.shape[1]
    depth_in = sizes[0]
    aligned = depth_in // 8 * 8
    whole = depth_in // LANES * LANES
    padded = [cats[layer].shape[1] for layer in range(6)] + [cats[5].shape[0]]

    def x_copy(c):
        part = pl.ds(c * CHUNK, CHUNK)
        return pltpu.make_async_copy(x_hbm.at[:, part], x_in.at[:, part], x_sems.at[c])

    def first_copy(n):
        part = pl.ds(n * FIRST, FIRST)
        return pltpu.make_async_copy(
            weights_hbm[0].at[:, part], weights_in[0].at[:, part], first_sems.at[n]
        )

    def w_copy(layer):
        target = weights_in[layer]
        if layer == 5:
            target = target.at[pl.ds(0, sizes[6])]
        return pltpu.make_async_copy(weights_hbm[layer], target, w_sems.at[layer])

    def small_copy(i):
        target = (inverse, tracer, along, across, *biases)[i]
        return pltpu.make_async_copy(small_hbm[i], target, small_sems.at[i])

    def out_copy(c):
        part = pl.ds(c * CHUNK, CHUNK)
        return pltpu.make_async_copy(
            tend.at[:, part], tend_hbm.at[:, part], out_sems.at[c]
        )

    def bias_columns(layer):
        count = sizes[layer + 1]
        source = biases[layer]
        if count % LANES:
            b_six[0:1, :] = jnp.zeros((1, b_six.shape[1]), F32)
            b_six[0:1, 0:count] = source[...].reshape(1, count)
            row = b_six[0:1, :]
        else:
            row = source[...].reshape(1, count)
        scale = 0.5 if layer < 5 else 1.0
        for n in range(0, count, LANES):
            block = jnp.broadcast_to(row[:, n : n + LANES], (LANES, LANES)).T * scale
            columns[layer][n : n + LANES, :] = block

    def put_weights(layer, lines, k, block):
        depth = padded[layer]
        if layer < 5:
            block = block * 0.5
        high = block.astype(BF16)
        low = block - high.astype(F32)
        step = WEIGHT_STEP * (2.0 if layer < 5 else 1.0)
        lanes, far = slice(k, k + LANES), slice(depth + k, depth + k + LANES)
        cats[layer][lines, lanes] = high
        cats8[layer][lines, lanes] = (block * step).astype(F8)
        cats8[layer][lines, far] = (low * (step * LOW_STEP)).astype(F8)

    def prepare(layer, part, parts):
        work = [
            (n, k)
            for n in range(0, round_up(sizes[layer + 1], LANES), LANES)
            for k in range(0, padded[layer], LANES)
        ]
        for n, k in work[part * len(work) // parts : (part + 1) * len(work) // parts]:
            lines, lanes = slice(n, n + LANES), slice(k, k + LANES)
            if layer == 5:
                block = weights_in[5][lines, lanes]
            elif layer == 0 and k >= whole:
                block = w_tail[:, lines].T
            else:
                block = weights_in[layer][lanes, lines].T
            put_weights(layer, lines, k, block)

    def put_rows(layer, start, cols, value, scale):
        depth = padded[layer]
        high = value.astype(BF16)
        low = value - high.astype(F32)
        size = value.shape[0]
        holds[layer % 2][start : start + size, cols] = high
        hold8 = holds8[layer % 2]
        hold8[start : start + size, cols] = (low * (scale * LOW_STEP)).astype(F8)
        hold8[depth + start : depth + start + size, cols] = (value * scale).astype(F8)

    def prepare_inputs(c):
        cols = slice(c * CHUNK, (c + 1) * CHUNK)
        x_tail[0 : aligned - whole, cols] = x_in[whole:aligned, cols]
        x_tail[aligned - whole : depth_in - whole, cols] = x_in[aligned:depth_in, cols]
        for k in range(0, whole, LANES):
            put_rows(0, k, cols, x_in[k : k + LANES, cols], TOP / INPUT_MAX)
        put_rows(0, whole, cols, x_tail[:, cols], TOP / INPUT_MAX)

    def product(layer, c, lines):
        depth = padded[layer]
        cols = slice(c * CHUNK, (c + 1) * CHUNK)
        main = jnp.dot(
            cats[layer][lines, :],
            holds[layer % 2][0:depth, cols],
            preferred_element_type=F32,
        )
        rest = jnp.dot(
            cats8[layer][lines, :],
            holds8[layer % 2][0 : 2 * depth, cols],
            preferred_element_type=F32,
        )
        return main, rest

    def finish(layer, c, lines, main, rest):
        cols = slice(c * CHUNK, (c + 1) * CHUNK)
        unit = 1.0 / (WEIGHT_STEP * LOW_STEP * (2.0 if layer < 5 else 1.0))
        if layer == 0:
            shrink, peak = jnp.full((1, CHUNK), INPUT_MAX / TOP, F32), INPUT_MAX
        else:
            shrink, peak = shrinks[layer : layer + 1, cols], peaks[layer : layer + 1, cols]
        bias = columns[layer][lines, :]
        value = main + rest * (shrink * unit)
        value = value + jnp.concatenate([bias] * (CHUNK // LANES), axis=1)
        if layer < 5:
            value = value + value * jnp.tanh(value)
            limit = (sizes[layer] * WEIGHT_MAX[layer]) * peak + BIAS_MAX
            limit = jnp.broadcast_to(jnp.asarray(limit, F32), (1, CHUNK))
            put_rows(layer + 1, lines.start, cols, value, TOP / limit)
            shrinks[layer + 1 : layer + 2, cols] = limit / TOP
            highest = jnp.max(value, axis=0, keepdims=True)
            if lines.start:
                highest = jnp.maximum(highest, peaks[layer + 1 : layer + 2, cols])
            peaks[layer + 1 : layer + 2, cols] = jnp.maximum(highest, SILU_DIP)
            return
        for part in range(CHUNK // LANES):
            r = c * (CHUNK // LANES) + part
            day = inverse[r : r + 1, :] >= 0
            shown = jnp.where(
                day, value[: sizes[6], part * LANES : (part + 1) * LANES], 0.0
            )
            tend[:, r * LANES : (r + 1) * LANES] = shown
            field[r, 0:levels, :] = (
                tracer[pl.ds(r, levels, stride=rows), :] + shown[0:levels]
            )
        out_copy(c).start()

    def prepare_first(n):
        first_copy(n).wait()
        lines = slice(n * FIRST, (n + 1) * FIRST)
        w_tail[0 : aligned - whole, lines] = weights_in[0][whole:aligned, lines]
        w_tail[aligned - whole : depth_in - whole, lines] = weights_in[0][
            aligned:depth_in, lines
        ]
        prepare(0, n, sizes[1] // FIRST)

    first_copy(0).start()
    x_copy(0).start()
    for n in range(1, sizes[1] // FIRST):
        first_copy(n).start()
    w_tail[...] = jnp.zeros(w_tail.shape, F32)
    x_tail[...] = jnp.zeros(x_tail.shape, F32)
    weights_in[5][sizes[6] :, :] = jnp.zeros(
        (weights_in[5].shape[0] - sizes[6], sizes[5]), F32
    )
    prepare_first(0)
    for c in range(1, chunks):
        x_copy(c).start()
    for i in range(10):
        small_copy(i).start()
    for layer in range(1, 6):
        w_copy(layer).start()
    x_copy(0).wait()
    prepare_inputs(0)

    for layer in range(6):
        if 0 < layer < 5:
            w_copy(layer + 1).wait()
        span = FIRST if layer == 0 else padded[layer + 1]
        for n in range(0, padded[layer + 1], span):
            lines = slice(n, n + span)
            for c in range(chunks):
                main, rest = product(layer, c, lines)
                if layer == 0 and n == 0 and c == 0:
                    for i in range(10):
                        small_copy(i).wait()
                    bias_columns(0)
                    for i in range(1, chunks):
                        x_copy(i).wait()
                        prepare_inputs(i)
                elif layer == 0 and c == chunks - 1 and n + span < sizes[1]:
                    prepare_first(n // FIRST + 1)
                if layer == 0 and n + span == sizes[1] or 0 < layer < 5:
                    if layer == 0 and c == 0:
                        w_copy(1).wait()
                    prepare(layer + 1, c, chunks)
                    if c == chunks - 1:
                        bias_columns(layer + 1)
                if layer == 4 and c == 0:
                    for r in range(rows):
                        field[r, levels : levels + 1, :] = along[r : r + 1, :]
                        field[r, levels + 1 : levels + 2, :] = across[r : r + 1, :]
                        field[r, levels + 2 : levels_wide, :] = jnp.zeros(
                            (levels_wide - levels - 2, LANES), F32
                        )
                finish(layer, c, lines, main, rest)

    odd = lax.rem(lax.axis_index(axis), 2)
    leaving = [
        pltpu.make_async_copy(
            field.at[pl.ds((rows - HALO) * odd, HALO)], pay_a, field_sems.at[0]
        ),
        pltpu.make_async_copy(
            field.at[pl.ds((rows - HALO) * (1 - odd), HALO)], pay_b, field_sems.at[1]
        ),
        pltpu.make_async_copy(field, field_hbm.at[pl.ds(0, rows)], field_sems.at[2]),
    ]
    for copy in leaving:
        copy.start()
    for copy in leaving:
        copy.wait()
    for c in range(chunks):
        out_copy(c).wait()


def network(inverse, tracer, along, across, biases, x, weights, axis):
    sizes = [x.shape[0]] + [b.shape[0] for b in biases]
    width = x.shape[1]
    rows = along.shape[0]
    levels = tracer.shape[0] // rows
    levels_wide = round_up(levels + 2, 8)
    chunks = width // CHUNK
    padded = [round_up(s, LANES) for s in sizes]
    deepest = max(padded[:6])
    tail = padded[0] - sizes[0] // LANES * LANES
    hbm = pl.BlockSpec(memory_space=pl.ANY)
    total = sum(sizes[i] * sizes[i + 1] for i in range(6)) * width
    return pl.pallas_call(
        functools.partial(network_kernel, sizes=sizes, levels=levels, axis=axis),
        out_shape=(
            jax.ShapeDtypeStruct((sizes[6], width), F32),
            jax.ShapeDtypeStruct((ROOM, levels_wide, LANES), F32),
            jax.ShapeDtypeStruct((HALO, levels_wide, LANES), F32),
            jax.ShapeDtypeStruct((HALO, levels_wide, LANES), F32),
        ),
        in_specs=[hbm] * 17,
        out_specs=(hbm,) * 4,
        scratch_shapes=[
            pltpu.VMEM(x.shape, F32),
            *[pltpu.VMEM(w.shape, F32) for w in weights[:5]],
            pltpu.VMEM((padded[6], sizes[5]), F32),
            *[pltpu.VMEM((padded[i + 1], padded[i]), BF16) for i in range(6)],
            *[pltpu.VMEM((padded[i + 1], 2 * padded[i]), F8) for i in range(6)],
            *[pltpu.VMEM((padded[i + 1], LANES), F32) for i in range(6)],
            pltpu.VMEM(inverse.shape, jnp.int32),
            pltpu.VMEM(tracer.shape, F32),
            pltpu.VMEM(along.shape, F32),
            pltpu.VMEM(across.shape, F32),
            *[pltpu.VMEM(b.shape, F32) for b in biases],
            *[pltpu.VMEM((deepest, width), BF16)] * 2,
            *[pltpu.VMEM((2 * deepest, width), F8)] * 2,
            pltpu.VMEM((tail, sizes[1]), F32),
            pltpu.VMEM((tail, width), F32),
            pltpu.VMEM((8, padded[6]), F32),
            pltpu.VMEM((sizes[6], width), F32),
            pltpu.VMEM((8, width), F32),
            pltpu.VMEM((8, width), F32),
            pltpu.VMEM((rows, levels_wide, LANES), F32),
            pltpu.SemaphoreType.DMA((chunks,)),
            pltpu.SemaphoreType.DMA((6,)),
            pltpu.SemaphoreType.DMA((chunks,)),
            pltpu.SemaphoreType.DMA((10,)),
            pltpu.SemaphoreType.DMA((3,)),
            pltpu.SemaphoreType.DMA((sizes[1] // FIRST,)),
        ],
        compiler_params=pltpu.CompilerParams(vmem_limit_bytes=NETWORK_VMEM),
        cost_estimate=pl.CostEstimate(
            flops=4 * total, bytes_accessed=14_000_000, transcendentals=3_000_000
        ),
        name="column_network",
    )(inverse, tracer, along, across, *biases, x, *weights)


def half_minmod(first, second):
    return 0.5 * (
        jnp.maximum(jnp.minimum(first, second), 0.0)
        + jnp.minimum(jnp.maximum(first, second), 0.0)
    )


def cat(values):
    return values[0] if len(values) == 1 else jnp.concatenate(values, axis=0)


def advect_kernel(
    field, got_a, got_b, out, wide, speeds, held, in_sems, out_sems, *, levels, axis
):
    rows = wide.shape[0] - 2 * HALO
    odd = lax.rem(lax.axis_index(axis), 2)
    arriving = [
        pltpu.make_async_copy(source, wide.at[pl.ds(start, source.shape[0])], in_sems.at[n])
        for n, (source, start) in enumerate(
            [
                (field.at[pl.ds(0, rows)], HALO),
                (got_a, (HALO + rows) * odd),
                (got_b, (HALO + rows) * (1 - odd)),
            ]
        )
    ]
    for copy in arriving:
        copy.start()

    def place(i):
        for kind in range(2):
            courant = jnp.broadcast_to(
                wide[i, levels + kind : levels + kind + 1, :], (8, LANES)
            )
            speeds[2 * kind, i] = jnp.maximum(courant, 0.0)
            speeds[2 * kind + 1, i] = jnp.minimum(courant, 0.0)

    for copy in arriving:
        copy.wait()
    for i in range(rows + 2 * HALO):
        place(i)
    groups = wide.shape[1] // GROUP
    span = GROUP * rows

    def leaving(g, start, size):
        return pltpu.make_async_copy(
            held.at[pl.ds(start, size)], out.at[pl.ds(start, size)], out_sems.at[g]
        )

    last = out.shape[0] - (groups - 1) * span

    def group(g, carry):
        wavefront(g, groups, levels, held, wide, speeds, rows)

        @pl.when(g < groups - 1)
        def _():
            leaving(g, pl.multiple_of(g * span, span), span).start()

        return carry

    lax.fori_loop(0, groups, group, 0)
    leaving(groups - 1, (groups - 1) * span, last).start()
    for g in range(groups - 1):
        leaving(g, g * span, span).wait()
    leaving(groups - 1, (groups - 1) * span, last).wait()


def wavefront(g, groups, levels, out, wide, speeds, rows):
    base = pl.multiple_of(g * GROUP, GROUP)
    blocks = GROUP // 8
    keep = levels - (groups - 1) * GROUP
    fields = [{}, {}, {}]
    steps, slopes, fluxes = [{}, {}, {}], [{}, {}, {}], [{}, {}, {}]
    reach = [(-4, rows + 3), (-2, rows + 1), (0, rows - 1)]
    shape = (blocks, 8, LANES)

    def load(i):
        return wide[i + HALO, pl.ds(base, GROUP), :].reshape(shape)

    def courant(kind, at):
        return cat([jnp.broadcast_to(speeds[kind, i + HALO], shape) for i in at])

    def pieces(value, count):
        return [value[n * blocks : (n + 1) * blocks] for n in range(count)]

    def face(active, at):
        ahead, behind = courant(0, at), courant(1, at)
        upper = cat([fields[k][i] - slopes[k][i] for k, i in zip(active, at)])
        lower = cat([fields[k][i - 1] + slopes[k][i - 1] for k, i in zip(active, at)])
        return ahead * lower + behind * upper

    rest = []
    for i in range(-HALO, -2):
        fields[0][i] = load(i)
    for t in range(-4, rows + 6):
        active = [k for k in range(3) if reach[k][0] <= t - 3 * k <= reach[k][1]]
        if t + 2 < rows + HALO:
            fields[0][t + 2] = load(t + 2)
        for k in active:
            c = t - 3 * k
            if c == reach[k][0]:
                f = fields[k]
                for i in (c - 1, c, c + 1):
                    steps[k][i] = f[i] - f[i - 1]
                for i in (c - 1, c):
                    slopes[k][i] = half_minmod(steps[k][i + 1], steps[k][i])
                fluxes[k][c] = face([k], [c])
        at = [t - 3 * k for k in active]
        here = cat([fields[k][i] for k, i in zip(active, at)])
        back = here - pltpu.roll(here, 1, 2)
        new = cat(
            [fields[k][i + 2] - fields[k][i + 1] for k, i in zip(active, at)]
        )
        last = cat([steps[k][i + 1] for k, i in zip(active, at)])
        bend = half_minmod(pltpu.roll(back, LANES - 1, 2), back)
        slope = half_minmod(new, last)
        for k, i, a_step, a_slope in zip(
            active, at, pieces(new, len(at)), pieces(slope, len(at))
        ):
            steps[k][i + 2], slopes[k][i + 1] = a_step, a_slope
        side = courant(2, at) * pltpu.roll(here + bend, 1, 2)
        side = side + courant(3, at) * (here - bend)
        flux = face(active, [i + 1 for i in at])
        for k, i, a_flux in zip(active, at, pieces(flux, len(at))):
            fluxes[k][i + 1] = a_flux
        moved = cat([fluxes[k][i] for k, i in zip(active, at)]) - flux
        moved = here + (moved + (side - pltpu.roll(side, LANES - 1, 2)))
        for k, i, value in zip(active, at, pieces(moved, len(at))):
            if k == 0:
                fields[1][i] = value
            elif k == 1:
                fields[2][i] = 0.75 * fields[0][i] + 0.25 * value
            else:
                value = 1.0 / 3.0 * fields[0][i] + 2.0 / 3.0 * value
                value = value.reshape(GROUP, LANES)
                out[pl.ds(base * rows + i, keep, stride=rows), :] = value[:keep]
                rest.append((i, value[keep:]))
    if keep < GROUP:

        @pl.when(g < groups - 1)
        def _():
            for i, value in rest:
                lines = pl.ds((base + keep) * rows + i, GROUP - keep, stride=rows)
                out[lines, :] = value


def advect(field, got_a, got_b, rows, levels, axis):
    _, levels_wide, across = field.shape
    hbm = pl.BlockSpec(memory_space=pl.ANY)
    return pl.pallas_call(
        functools.partial(advect_kernel, levels=levels, axis=axis),
        out_shape=jax.ShapeDtypeStruct((levels * rows, across), F32),
        in_specs=[hbm] * 3,
        out_specs=hbm,
        scratch_shapes=[
            pltpu.VMEM((rows + 2 * HALO, levels_wide, across), F32),
            pltpu.VMEM((4, rows + 2 * HALO, 8, across), F32),
            pltpu.VMEM((levels * rows, across), F32),
            pltpu.SemaphoreType.DMA((3,)),
            pltpu.SemaphoreType.DMA((levels_wide // GROUP,)),
        ],
        compiler_params=pltpu.CompilerParams(vmem_limit_bytes=ADVECT_VMEM),
        name="advect_sections",
    )(field, got_a, got_b)


def shards(inputs, tracer, speed_along, speed_across, inverse_list, *params):
    weights, biases = list(params[0::2]), params[1::2]
    weights[5] = weights[5].T
    levels, rows, across = tracer.shape
    tendencies, field, pay_a, pay_b = network(
        inverse_list.reshape(rows, across),
        tracer.reshape(levels * rows, across),
        speed_along,
        speed_across,
        biases,
        inputs.T,
        weights,
        "gx",
    )
    count = lax.axis_size("gx")
    outer = [(i, (i - 1 if i % 2 == 0 else i + 1) % count) for i in range(count)]
    inner = [(i, i + 1 if i % 2 == 0 else i - 1) for i in range(count)]
    got_a = lax.ppermute(pay_a, "gx", outer)
    got_b = lax.ppermute(pay_b, "gx", inner)
    advected = advect(field, got_a, got_b, rows, levels, "gx")
    return tendencies.T, advected.reshape(levels, rows, across)


def solution(mesh):
    placed = (
        P(("member", "gx"), None),
        P(None, ("member", "gx"), None),
        P(("member", "gx"), None),
        P(("member", "gx"), None),
        P(("member", "gx")),
        *[P()] * 12,
    )
    return jax.shard_map(
        shards,
        mesh=mesh,
        in_specs=placed,
        out_specs=(P(("member", "gx"), None), P(None, ("member", "gx"), None)),
        check_vma=False,
    )
```

```python
import functools
import jax
import jax.numpy as jnp
from jax import lax
from jax.experimental import pallas as pl
from jax.experimental.pallas import tpu as pltpu
from jax.sharding import PartitionSpec as P

F32, BF16, F8 = jnp.float32, jnp.bfloat16, jnp.float8_e4m3fn
LANES = 128
CHUNK = 512
HALO = 6
GROUP = 32
FIRST = 256
WEIGHT_MAX = (0.25, 0.3125, 0.3125, 0.375, 0.3125, 0.3125)
BIAS_MAX = 3.0
INPUT_MAX = 6.0
SILU_DIP = 0.28
TOP = 440.0
WEIGHT_STEP = 2.0**10
LOW_STEP = 2.0**8
NETWORK_VMEM = 60_000_000
ADVECT_VMEM = 8 * 2**20


def round_up(value, unit):
    return -(-value // unit) * unit


def network_kernel(*refs, sizes, levels, axis):
    small_hbm, x_hbm, weights_hbm, refs = refs[:10], refs[10], refs[11:17], refs[17:]
    (tend_hbm, field_hbm, pay_a, pay_b), refs = refs[:4], refs[4:]
    x_in, weights_in, refs = refs[0], refs[1:7], refs[7:]
    cats, cats8, columns, refs = refs[:6], refs[6:12], refs[12:18], refs[18:]
    inverse, tracer, along, across, *biases = refs[:10]
    holds, holds8, refs = refs[10:12], refs[12:14], refs[14:]
    w_tail, x_tail, b_six, tend, peaks, shrinks, field, *sems = refs
    x_sems, w_sems, out_sems, small_sems, field_sems, first_sems = sems

    chunks = x_hbm.shape[1] // CHUNK
    rows, levels_wide = field.shape[0], field.shape[1]
    depth_in = sizes[0]
    aligned = depth_in // 8 * 8
    whole = depth_in // LANES * LANES
    padded = [cats[layer].shape[1] for layer in range(6)] + [cats[5].shape[0]]

    def x_copy(c):
        part = pl.ds(c * CHUNK, CHUNK)
        return pltpu.make_async_copy(x_hbm.at[:, part], x_in.at[:, part], x_sems.at[c])

    def first_copy(n):
        part = pl.ds(n * FIRST, FIRST)
        return pltpu.make_async_copy(
            weights_hbm[0].at[:, part], weights_in[0].at[:, part], first_sems.at[n]
        )

    def w_copy(layer):
        target = weights_in[layer]
        if layer == 5:
            target = target.at[pl.ds(0, sizes[6])]
        return pltpu.make_async_copy(weights_hbm[layer], target, w_sems.at[layer])

    def small_copy(i):
        target = (inverse, tracer, along, across, *biases)[i]
        return pltpu.make_async_copy(small_hbm[i], target, small_sems.at[i])

    def out_copy(c):
        part = pl.ds(c * CHUNK, CHUNK)
        return pltpu.make_async_copy(
            tend.at[:, part], tend_hbm.at[:, part], out_sems.at[c]
        )

    def bias_columns(layer):
        count = sizes[layer + 1]
        source = biases[layer]
        if count % LANES:
            b_six[0:1, :] = jnp.zeros((1, b_six.shape[1]), F32)
            b_six[0:1, 0:count] = source[...].reshape(1, count)
            row = b_six[0:1, :]
        else:
            row = source[...].reshape(1, count)
        scale = 0.5 if layer < 5 else 1.0
        for n in range(0, count, LANES):
            block = jnp.broadcast_to(row[:, n : n + LANES], (LANES, LANES)).T * scale
            columns[layer][n : n + LANES, :] = block

    def put_weights(layer, lines, k, block):
        depth = padded[layer]
        if layer < 5:
            block = block * 0.5
        high = block.astype(BF16)
        low = block - high.astype(F32)
        step = WEIGHT_STEP * (2.0 if layer < 5 else 1.0)
        lanes, far = slice(k, k + LANES), slice(depth + k, depth + k + LANES)
        cats[layer][lines, lanes] = high
        cats8[layer][lines, lanes] = (block * step).astype(F8)
        cats8[layer][lines, far] = (low * (step * LOW_STEP)).astype(F8)

    def prepare(layer, part, parts):
        work = [
            (n, k)
            for n in range(0, round_up(sizes[layer + 1], LANES), LANES)
            for k in range(0, padded[layer], LANES)
        ]
        for n, k in work[part * len(work) // parts : (part + 1) * len(work) // parts]:
            lines, lanes = slice(n, n + LANES), slice(k, k + LANES)
            if layer == 5:
                block = weights_in[5][lines, lanes]
            elif layer == 0 and k >= whole:
                block = w_tail[:, lines].T
            else:
                block = weights_in[layer][lanes, lines].T
            put_weights(layer, lines, k, block)

    def put_rows(layer, start, cols, value, scale):
        depth = padded[layer]
        high = value.astype(BF16)
        low = value - high.astype(F32)
        size = value.shape[0]
        holds[layer % 2][start : start + size, cols] = high
        hold8 = holds8[layer % 2]
        hold8[start : start + size, cols] = (low * (scale * LOW_STEP)).astype(F8)
        hold8[depth + start : depth + start + size, cols] = (value * scale).astype(F8)

    def prepare_inputs(c):
        cols = slice(c * CHUNK, (c + 1) * CHUNK)
        x_tail[0 : aligned - whole, cols] = x_in[whole:aligned, cols]
        x_tail[aligned - whole : depth_in - whole, cols] = x_in[aligned:depth_in, cols]
        for k in range(0, whole, LANES):
            put_rows(0, k, cols, x_in[k : k + LANES, cols], TOP / INPUT_MAX)
        put_rows(0, whole, cols, x_tail[:, cols], TOP / INPUT_MAX)

    def product(layer, c, lines):
        depth = padded[layer]
        cols = slice(c * CHUNK, (c + 1) * CHUNK)
        main = jnp.dot(
            cats[layer][lines, :],
            holds[layer % 2][0:depth, cols],
            preferred_element_type=F32,
        )
        rest = jnp.dot(
            cats8[layer][lines, :],
            holds8[layer % 2][0 : 2 * depth, cols],
            preferred_element_type=F32,
        )
        return main, rest

    def finish(layer, c, lines, main, rest):
        cols = slice(c * CHUNK, (c + 1) * CHUNK)
        unit = 1.0 / (WEIGHT_STEP * LOW_STEP * (2.0 if layer < 5 else 1.0))
        if layer == 0:
            shrink, peak = jnp.full((1, CHUNK), INPUT_MAX / TOP, F32), INPUT_MAX
        else:
            shrink, peak = shrinks[layer : layer + 1, cols], peaks[layer : layer + 1, cols]
        bias = columns[layer][lines, :]
        value = main + rest * (shrink * unit)
        value = value + jnp.concatenate([bias] * (CHUNK // LANES), axis=1)
        if layer < 5:
            value = value + value * jnp.tanh(value)
            limit = (sizes[layer] * WEIGHT_MAX[layer]) * peak + BIAS_MAX
            limit = jnp.broadcast_to(jnp.asarray(limit, F32), (1, CHUNK))
            put_rows(layer + 1, lines.start, cols, value, TOP / limit)
            shrinks[layer + 1 : layer + 2, cols] = limit / TOP
            highest = jnp.max(value, axis=0, keepdims=True)
            if lines.start:
                highest = jnp.maximum(highest, peaks[layer + 1 : layer + 2, cols])
            peaks[layer + 1 : layer + 2, cols] = jnp.maximum(highest, SILU_DIP)
            return
        keep = min(lines.stop, sizes[6]) - lines.start
        for part in range(CHUNK // LANES):
            r = c * (CHUNK // LANES) + part
            day = inverse[r : r + 1, :] >= 0
            shown = jnp.where(day, value[:keep, part * LANES : (part + 1) * LANES], 0.0)
            tend[lines.start : lines.start + keep, r * LANES : (r + 1) * LANES] = shown
            if lines.start == 0:
                field[r, 0:levels, :] = (
                    tracer[pl.ds(r, levels, stride=rows), :] + shown[0:levels]
                )
        if lines.stop >= sizes[6]:
            out_copy(c).start()

    def prepare_first(n):
        first_copy(n).wait()
        lines = slice(n * FIRST, (n + 1) * FIRST)
        w_tail[0 : aligned - whole, lines] = weights_in[0][whole:aligned, lines]
        w_tail[aligned - whole : depth_in - whole, lines] = weights_in[0][
            aligned:depth_in, lines
        ]
        prepare(0, n, sizes[1] // FIRST)

    first_parts = sizes[1] // FIRST
    first_copy(0).start()
    x_copy(0).start()
    for n in range(1, first_parts):
        first_copy(n).start()
    for i in range(10):
        small_copy(i).start()
    for c in range(1, chunks):
        x_copy(c).start()
    w_tail[...] = jnp.zeros(w_tail.shape, F32)
    x_tail[...] = jnp.zeros(x_tail.shape, F32)
    weights_in[5][sizes[6] :, :] = jnp.zeros(
        (weights_in[5].shape[0] - sizes[6], sizes[5]), F32
    )
    prepare_first(0)
    x_copy(0).wait()
    prepare_inputs(0)
    for n in range(1, first_parts):
        prepare_first(n)
    w_copy(1).start()

    for layer in range(6):
        if 0 < layer < 5:
            w_copy(layer + 1).wait()
        if 0 < layer < 4:
            w_copy(layer + 2).start()
        count = padded[layer + 1]
        blocks = [slice(0, count)]
        parts = chunks * len(blocks)
        for c in range(chunks):
            for lines in blocks:
                part = c
                main, rest = product(layer, c, lines)
                if layer == 0 and part == 0:
                    for i in range(10):
                        small_copy(i).wait()
                    bias_columns(0)
                if layer == 0 and c + 1 < chunks:
                    x_copy(c + 1).wait()
                    prepare_inputs(c + 1)
                    if c + 2 == chunks:
                        w_copy(2).start()
                if layer == 0 and part >= parts // 2:
                    if part == parts // 2:
                        w_copy(1).wait()
                    prepare(1, part - parts // 2, parts - parts // 2)
                elif 0 < layer < 5:
                    prepare(layer + 1, part, parts)
                if layer < 5 and part == parts - 1:
                    bias_columns(layer + 1)
                if layer == 4 and part == 0:
                    for r in range(rows):
                        field[r, levels : levels + 1, :] = along[r : r + 1, :]
                        field[r, levels + 1 : levels + 2, :] = across[r : r + 1, :]
                        field[r, levels + 2 : levels_wide, :] = jnp.zeros(
                            (levels_wide - levels - 2, LANES), F32
                        )
                finish(layer, c, lines, main, rest)

    odd = lax.rem(lax.axis_index(axis), 2)
    leaving = [
        pltpu.make_async_copy(
            field.at[pl.ds((rows - HALO) * odd, HALO)], pay_a, field_sems.at[0]
        ),
        pltpu.make_async_copy(
            field.at[pl.ds((rows - HALO) * (1 - odd), HALO)], pay_b, field_sems.at[1]
        ),
        pltpu.make_async_copy(field, field_hbm, field_sems.at[2]),
    ]
    for copy in leaving:
        copy.start()
    for copy in leaving:
        copy.wait()
    for c in range(chunks):
        out_copy(c).wait()


def network(inverse, tracer, along, across, biases, x, weights, axis):
    sizes = [x.shape[0]] + [b.shape[0] for b in biases]
    width = x.shape[1]
    rows = along.shape[0]
    levels = tracer.shape[0] // rows
    levels_wide = round_up(levels + 2, 8)
    chunks = width // CHUNK
    padded = [round_up(s, LANES) for s in sizes]
    deepest = max(padded[:6])
    tail = padded[0] - sizes[0] // LANES * LANES
    hbm = pl.BlockSpec(memory_space=pl.ANY)
    total = sum(sizes[i] * sizes[i + 1] for i in range(6)) * width
    return pl.pallas_call(
        functools.partial(network_kernel, sizes=sizes, levels=levels, axis=axis),
        out_shape=(
            jax.ShapeDtypeStruct((sizes[6], width), F32),
            jax.ShapeDtypeStruct((rows, levels_wide, LANES), F32),
            jax.ShapeDtypeStruct((HALO, levels_wide, LANES), F32),
            jax.ShapeDtypeStruct((HALO, levels_wide, LANES), F32),
        ),
        in_specs=[hbm] * 17,
        out_specs=(hbm,) * 4,
        scratch_shapes=[
            pltpu.VMEM(x.shape, F32),
            *[pltpu.VMEM(w.shape, F32) for w in weights[:5]],
            pltpu.VMEM((padded[6], sizes[5]), F32),
            *[pltpu.VMEM((padded[i + 1], padded[i]), BF16) for i in range(6)],
            *[pltpu.VMEM((padded[i + 1], 2 * padded[i]), F8) for i in range(6)],
            *[pltpu.VMEM((padded[i + 1], LANES), F32) for i in range(6)],
            pltpu.VMEM(inverse.shape, jnp.int32),
            pltpu.VMEM(tracer.shape, F32),
            pltpu.VMEM(along.shape, F32),
            pltpu.VMEM(across.shape, F32),
            *[pltpu.VMEM(b.shape, F32) for b in biases],
            *[pltpu.VMEM((deepest, width), BF16)] * 2,
            *[pltpu.VMEM((2 * deepest, width), F8)] * 2,
            pltpu.VMEM((tail, sizes[1]), F32),
            pltpu.VMEM((tail, width), F32),
            pltpu.VMEM((8, padded[6]), F32),
            pltpu.VMEM((sizes[6], width), F32),
            pltpu.VMEM((8, width), F32),
            pltpu.VMEM((8, width), F32),
            pltpu.VMEM((rows, levels_wide, LANES), F32),
            pltpu.SemaphoreType.DMA((chunks,)),
            pltpu.SemaphoreType.DMA((6,)),
            pltpu.SemaphoreType.DMA((chunks,)),
            pltpu.SemaphoreType.DMA((10,)),
            pltpu.SemaphoreType.DMA((3,)),
            pltpu.SemaphoreType.DMA((sizes[1] // FIRST,)),
        ],
        compiler_params=pltpu.CompilerParams(vmem_limit_bytes=NETWORK_VMEM),
        cost_estimate=pl.CostEstimate(
            flops=4 * total, bytes_accessed=14_000_000, transcendentals=3_000_000
        ),
        name="column_network",
    )(inverse, tracer, along, across, *biases, x, *weights)


def half_minmod(first, second):
    return 0.5 * (
        jnp.maximum(jnp.minimum(first, second), 0.0)
        + jnp.minimum(jnp.maximum(first, second), 0.0)
    )


def cat(values):
    return values[0] if len(values) == 1 else jnp.concatenate(values, axis=0)


def advect_kernel(field, got_a, got_b, out, wide, speeds, sem, *, levels, axis):
    rows = field.shape[0]
    odd = lax.rem(lax.axis_index(axis), 2)
    own = pltpu.make_async_copy(field, wide.at[pl.ds(HALO, rows)], sem)
    own.start()
    wide[pl.ds((HALO + rows) * odd, HALO)] = got_a[...]
    wide[pl.ds((HALO + rows) * (1 - odd), HALO)] = got_b[...]

    def place(i):
        for kind in range(2):
            courant = jnp.broadcast_to(
                wide[i, levels + kind : levels + kind + 1, :], (8, LANES)
            )
            speeds[2 * kind, i] = jnp.maximum(courant, 0.0)
            speeds[2 * kind + 1, i] = jnp.minimum(courant, 0.0)

    for i in range(HALO):
        place(i)
        place(HALO + rows + i)
    own.wait()
    for i in range(HALO, HALO + rows):
        place(i)
    groups = wide.shape[1] // GROUP

    def group(g, carry):
        wavefront(g, groups, levels, out, wide, speeds, rows)
        return carry

    lax.fori_loop(0, groups, group, 0)


def wavefront(g, groups, levels, out, wide, speeds, rows):
    base = pl.multiple_of(g * GROUP, GROUP)
    blocks = GROUP // 8
    keep = levels - (groups - 1) * GROUP
    fields = [{}, {}, {}]
    steps, slopes, fluxes = [{}, {}, {}], [{}, {}, {}], [{}, {}, {}]
    reach = [(-4, rows + 3), (-2, rows + 1), (0, rows - 1)]
    shape = (blocks, 8, LANES)

    def load(i):
        return wide[i + HALO, pl.ds(base, GROUP), :].reshape(shape)

    def courant(kind, at):
        return cat([jnp.broadcast_to(speeds[kind, i + HALO], shape) for i in at])

    def pieces(value, count):
        return [value[n * blocks : (n + 1) * blocks] for n in range(count)]

    def face(active, at):
        ahead, behind = courant(0, at), courant(1, at)
        upper = cat([fields[k][i] - slopes[k][i] for k, i in zip(active, at)])
        lower = cat([fields[k][i - 1] + slopes[k][i - 1] for k, i in zip(active, at)])
        return ahead * lower + behind * upper

    rest = []
    for i in range(-HALO, -2):
        fields[0][i] = load(i)
    for t in range(-4, rows + 6):
        active = [k for k in range(3) if reach[k][0] <= t - 3 * k <= reach[k][1]]
        if t + 2 < rows + HALO:
            fields[0][t + 2] = load(t + 2)
        for k in active:
            c = t - 3 * k
            if c == reach[k][0]:
                f = fields[k]
                for i in (c - 1, c, c + 1):
                    steps[k][i] = f[i] - f[i - 1]
                for i in (c - 1, c):
                    slopes[k][i] = half_minmod(steps[k][i + 1], steps[k][i])
                fluxes[k][c] = face([k], [c])
        at = [t - 3 * k for k in active]
        here = cat([fields[k][i] for k, i in zip(active, at)])
        back = here - pltpu.roll(here, 1, 2)
        new = cat(
            [fields[k][i + 2] - fields[k][i + 1] for k, i in zip(active, at)]
        )
        last = cat([steps[k][i + 1] for k, i in zip(active, at)])
        bend = half_minmod(pltpu.roll(back, LANES - 1, 2), back)
        slope = half_minmod(new, last)
        for k, i, a_step, a_slope in zip(
            active, at, pieces(new, len(at)), pieces(slope, len(at))
        ):
            steps[k][i + 2], slopes[k][i + 1] = a_step, a_slope
        side = courant(2, at) * pltpu.roll(here + bend, 1, 2)
        side = side + courant(3, at) * (here - bend)
        flux = face(active, [i + 1 for i in at])
        for k, i, a_flux in zip(active, at, pieces(flux, len(at))):
            fluxes[k][i + 1] = a_flux
        moved = cat([fluxes[k][i] for k, i in zip(active, at)]) - flux
        moved = here + (moved + (side - pltpu.roll(side, LANES - 1, 2)))
        for k, i, value in zip(active, at, pieces(moved, len(at))):
            if k == 0:
                fields[1][i] = value
            elif k == 1:
                fields[2][i] = 0.75 * fields[0][i] + 0.25 * value
            else:
                value = 1.0 / 3.0 * fields[0][i] + 2.0 / 3.0 * value
                value = value.reshape(GROUP, LANES)
                out[pl.ds(base * rows + i, keep, stride=rows), :] = value[:keep]
                rest.append((i, value[keep:]))
    if keep < GROUP:

        @pl.when(g < groups - 1)
        def _():
            for i, value in rest:
                lines = pl.ds((base + keep) * rows + i, GROUP - keep, stride=rows)
                out[lines, :] = value


def advect(field, got_a, got_b, levels, axis):
    rows, levels_wide, across = field.shape
    vmem = pl.BlockSpec(memory_space=pltpu.VMEM)
    return pl.pallas_call(
        functools.partial(advect_kernel, levels=levels, axis=axis),
        out_shape=jax.ShapeDtypeStruct((levels * rows, across), F32),
        in_specs=[pl.BlockSpec(memory_space=pl.ANY), vmem, vmem],
        out_specs=vmem,
        scratch_shapes=[
            pltpu.VMEM((rows + 2 * HALO, levels_wide, across), F32),
            pltpu.VMEM((4, rows + 2 * HALO, 8, across), F32),
            pltpu.SemaphoreType.DMA,
        ],
        compiler_params=pltpu.CompilerParams(vmem_limit_bytes=ADVECT_VMEM),
        name="advect_sections",
    )(field, got_a, got_b)


def shards(inputs, tracer, speed_along, speed_across, inverse_list, *params):
    weights, biases = list(params[0::2]), params[1::2]
    weights[5] = weights[5].T
    levels, rows, across = tracer.shape
    tendencies, field, pay_a, pay_b = network(
        inverse_list.reshape(rows, across),
        tracer.reshape(levels * rows, across),
        speed_along,
        speed_across,
        biases,
        inputs.T,
        weights,
        "gx",
    )
    count = lax.axis_size("gx")
    outer = [(i, (i - 1 if i % 2 == 0 else i + 1) % count) for i in range(count)]
    inner = [(i, i + 1 if i % 2 == 0 else i - 1) for i in range(count)]
    got_a = lax.ppermute(pay_a, "gx", outer)
    got_b = lax.ppermute(pay_b, "gx", inner)
    advected = advect(field, got_a, got_b, levels, "gx")
    return tendencies.T, advected.reshape(levels, rows, across)


def solution(mesh):
    placed = (
        P(("member", "gx"), None),
        P(None, ("member", "gx"), None),
        P(("member", "gx"), None),
        P(("member", "gx"), None),
        P(("member", "gx")),
        *[P()] * 12,
    )
    return jax.shard_map(
        shards,
        mesh=mesh,
        in_specs=placed,
        out_specs=(P(("member", "gx"), None), P(None, ("member", "gx"), None)),
        check_vma=False,
    )
```

```python
import functools
import jax
import jax.numpy as jnp
from jax import lax
from jax.experimental import pallas as pl
from jax.experimental.pallas import tpu as pltpu
from jax.sharding import PartitionSpec as P

F32, BF16 = jnp.float32, jnp.bfloat16
LANES = 128
CHUNK = 256
HALO = 6
GROUP = 32
FIRST = 256
NETWORK_VMEM = 60_000_000
ADVECT_VMEM = 8 * 2**20


def round_up(value, unit):
    return -(-value // unit) * unit


def split(value):
    high = value.astype(BF16)
    low = (value - high.astype(F32)).astype(BF16)
    return high, low


def network_kernel(*refs, sizes, levels, axis):
    small_hbm, x_hbm, weights_hbm, refs = refs[:10], refs[10], refs[11:17], refs[17:]
    (tend_hbm, field_hbm, pay_a, pay_b), refs = refs[:4], refs[4:]
    x_in, weights_in, refs = refs[0], refs[1:7], refs[7:]
    cats, columns, refs = refs[:6], refs[6:12], refs[12:]
    inverse, tracer, along, across, *biases = refs[:10]
    holds, refs = refs[10:12], refs[12:]
    w_tail, x_tail, b_six, tend, field, *sems = refs
    x_sems, w_sems, out_sems, small_sems, field_sems, first_sems = sems

    chunks = x_hbm.shape[1] // CHUNK
    rows, levels_wide = field.shape[0], field.shape[1]
    depth_in = sizes[0]
    aligned = depth_in // 8 * 8
    whole = depth_in // LANES * LANES
    padded = [cats[layer].shape[1] // 3 for layer in range(6)] + [cats[5].shape[0]]

    def x_copy(c):
        part = pl.ds(c * CHUNK, CHUNK)
        return pltpu.make_async_copy(x_hbm.at[:, part], x_in.at[:, part], x_sems.at[c])

    def first_copy(n):
        part = pl.ds(n * FIRST, FIRST)
        return pltpu.make_async_copy(
            weights_hbm[0].at[:, part], weights_in[0].at[:, part], first_sems.at[n]
        )

    def w_copy(layer):
        target = weights_in[layer]
        if layer == 5:
            target = target.at[pl.ds(0, sizes[6])]
        return pltpu.make_async_copy(weights_hbm[layer], target, w_sems.at[layer])

    def small_copy(i):
        target = (inverse, tracer, along, across, *biases)[i]
        return pltpu.make_async_copy(small_hbm[i], target, small_sems.at[i])

    def out_copy(c):
        part = pl.ds(c * CHUNK, CHUNK)
        return pltpu.make_async_copy(
            tend.at[:, part], tend_hbm.at[:, part], out_sems.at[c]
        )

    def bias_columns(layer):
        count = sizes[layer + 1]
        source = biases[layer]
        if count % LANES:
            b_six[0:1, :] = jnp.zeros((1, b_six.shape[1]), F32)
            b_six[0:1, 0:count] = source[...].reshape(1, count)
            row = b_six[0:1, :]
        else:
            row = source[...].reshape(1, count)
        scale = 0.5 if layer < 5 else 1.0
        for n in range(0, count, LANES):
            block = jnp.broadcast_to(row[:, n : n + LANES], (LANES, LANES)).T * scale
            columns[layer][n : n + LANES, :] = block

    def put_weights(layer, lines, k, block):
        depth = padded[layer]
        if layer < 5:
            block = block * 0.5
        high, low = split(block)
        for n, piece in enumerate((high, high, low)):
            cats[layer][lines, n * depth + k : n * depth + k + LANES] = piece

    def prepare(layer, part, parts):
        work = [
            (n, k)
            for n in range(0, round_up(sizes[layer + 1], LANES), LANES)
            for k in range(0, padded[layer], LANES)
        ]
        for n, k in work[part * len(work) // parts : (part + 1) * len(work) // parts]:
            lines, lanes = slice(n, n + LANES), slice(k, k + LANES)
            if layer == 5:
                block = weights_in[5][lines, lanes]
            elif layer == 0 and k >= whole:
                block = w_tail[:, lines].T
            else:
                block = weights_in[layer][lanes, lines].T
            put_weights(layer, lines, k, block)

    def put_rows(layer, start, cols, value):
        depth = padded[layer]
        high, low = split(value)
        size = value.shape[0]
        for n, piece in enumerate((high, low, high)):
            holds[layer % 2][n * depth + start : n * depth + start + size, cols] = piece

    def prepare_inputs(c):
        cols = slice(c * CHUNK, (c + 1) * CHUNK)
        x_tail[0 : aligned - whole, cols] = x_in[whole:aligned, cols]
        x_tail[aligned - whole : depth_in - whole, cols] = x_in[aligned:depth_in, cols]
        for k in range(0, whole, LANES):
            put_rows(0, k, cols, x_in[k : k + LANES, cols])
        put_rows(0, whole, cols, x_tail[:, cols])

    def product(layer, c, lines):
        cols = slice(c * CHUNK, (c + 1) * CHUNK)
        return jnp.dot(
            cats[layer][lines, :],
            holds[layer % 2][0 : 3 * padded[layer], cols],
            preferred_element_type=F32,
        )

    def finish(layer, c, lines, total):
        cols = slice(c * CHUNK, (c + 1) * CHUNK)
        bias = columns[layer][lines, :]
        value = total + jnp.concatenate([bias] * (CHUNK // LANES), axis=1)
        if layer < 5:
            value = value + value * jnp.tanh(value)
            put_rows(layer + 1, lines.start, cols, value)
            return
        keep = min(lines.stop, sizes[6]) - lines.start
        for part in range(CHUNK // LANES):
            r = c * (CHUNK // LANES) + part
            day = inverse[r : r + 1, :] >= 0
            shown = jnp.where(day, value[:keep, part * LANES : (part + 1) * LANES], 0.0)
            tend[lines.start : lines.start + keep, r * LANES : (r + 1) * LANES] = shown
            if lines.start == 0:
                field[r, 0:levels, :] = (
                    tracer[pl.ds(r, levels, stride=rows), :] + shown[0:levels]
                )
        if lines.stop >= sizes[6]:
            out_copy(c).start()

    def prepare_first(n):
        first_copy(n).wait()
        lines = slice(n * FIRST, (n + 1) * FIRST)
        w_tail[0 : aligned - whole, lines] = weights_in[0][whole:aligned, lines]
        w_tail[aligned - whole : depth_in - whole, lines] = weights_in[0][
            aligned:depth_in, lines
        ]
        prepare(0, n, sizes[1] // FIRST)

    first_parts = sizes[1] // FIRST
    first_copy(0).start()
    x_copy(0).start()
    for n in range(1, first_parts):
        first_copy(n).start()
    for i in range(10):
        small_copy(i).start()
    for c in range(1, chunks):
        x_copy(c).start()
    w_tail[...] = jnp.zeros(w_tail.shape, F32)
    x_tail[...] = jnp.zeros(x_tail.shape, F32)
    weights_in[5][sizes[6] :, :] = jnp.zeros(
        (weights_in[5].shape[0] - sizes[6], sizes[5]), F32
    )
    prepare_first(0)
    x_copy(0).wait()
    prepare_inputs(0)
    for n in range(1, first_parts):
        prepare_first(n)
    w_copy(1).start()

    pending = None
    for layer in range(6):
        if 0 < layer < 5:
            w_copy(layer + 1).wait()
        if 0 < layer < 4:
            w_copy(layer + 2).start()
        count = padded[layer + 1]
        blocks = [slice(0, count // 2), slice(count // 2, count)]
        parts = chunks * len(blocks)
        for c in range(chunks):
            for m, lines in enumerate(blocks):
                part = c * len(blocks) + m
                total = product(layer, c, lines)
                if layer == 0 and part == 0:
                    for i in range(10):
                        small_copy(i).wait()
                    bias_columns(0)
                if layer == 0 and m == 1 and c + 1 < chunks:
                    x_copy(c + 1).wait()
                    prepare_inputs(c + 1)
                    if c + 2 == chunks:
                        w_copy(2).start()
                if layer == 0 and part >= parts // 2:
                    if part == parts // 2:
                        w_copy(1).wait()
                    prepare(1, part - parts // 2, parts - parts // 2)
                elif 0 < layer < 5:
                    prepare(layer + 1, part, parts)
                if layer < 5 and part == parts - 1:
                    bias_columns(layer + 1)
                if layer == 4 and part == 0:
                    for r in range(rows):
                        field[r, levels : levels + 1, :] = along[r : r + 1, :]
                        field[r, levels + 1 : levels + 2, :] = across[r : r + 1, :]
                        field[r, levels + 2 : levels_wide, :] = jnp.zeros(
                            (levels_wide - levels - 2, LANES), F32
                        )
                if pending is not None:
                    finish(*pending)
                pending = (layer, c, lines, total)
    finish(*pending)

    odd = lax.rem(lax.axis_index(axis), 2)
    leaving = [
        pltpu.make_async_copy(
            field.at[pl.ds((rows - HALO) * odd, HALO)], pay_a, field_sems.at[0]
        ),
        pltpu.make_async_copy(
            field.at[pl.ds((rows - HALO) * (1 - odd), HALO)], pay_b, field_sems.at[1]
        ),
        pltpu.make_async_copy(field, field_hbm, field_sems.at[2]),
    ]
    for copy in leaving:
        copy.start()
    for copy in leaving:
        copy.wait()
    for c in range(chunks):
        out_copy(c).wait()


def network(inverse, tracer, along, across, biases, x, weights, axis):
    sizes = [x.shape[0]] + [b.shape[0] for b in biases]
    width = x.shape[1]
    rows = along.shape[0]
    levels = tracer.shape[0] // rows
    levels_wide = round_up(levels + 2, 8)
    chunks = width // CHUNK
    padded = [round_up(s, LANES) for s in sizes]
    deepest = max(padded[:6])
    tail = padded[0] - sizes[0] // LANES * LANES
    hbm = pl.BlockSpec(memory_space=pl.ANY)
    total = sum(sizes[i] * sizes[i + 1] for i in range(6)) * width
    return pl.pallas_call(
        functools.partial(network_kernel, sizes=sizes, levels=levels, axis=axis),
        out_shape=(
            jax.ShapeDtypeStruct((sizes[6], width), F32),
            jax.ShapeDtypeStruct((rows, levels_wide, LANES), F32),
            jax.ShapeDtypeStruct((HALO, levels_wide, LANES), F32),
            jax.ShapeDtypeStruct((HALO, levels_wide, LANES), F32),
        ),
        in_specs=[hbm] * 17,
        out_specs=(hbm,) * 4,
        scratch_shapes=[
            pltpu.VMEM(x.shape, F32),
            *[pltpu.VMEM(w.shape, F32) for w in weights[:5]],
            pltpu.VMEM((padded[6], sizes[5]), F32),
            *[pltpu.VMEM((padded[i + 1], 3 * padded[i]), BF16) for i in range(6)],
            *[pltpu.VMEM((padded[i + 1], LANES), F32) for i in range(6)],
            pltpu.VMEM(inverse.shape, jnp.int32),
            pltpu.VMEM(tracer.shape, F32),
            pltpu.VMEM(along.shape, F32),
            pltpu.VMEM(across.shape, F32),
            *[pltpu.VMEM(b.shape, F32) for b in biases],
            *[pltpu.VMEM((3 * deepest, width), BF16)] * 2,
            pltpu.VMEM((tail, sizes[1]), F32),
            pltpu.VMEM((tail, width), F32),
            pltpu.VMEM((8, padded[6]), F32),
            pltpu.VMEM((sizes[6], width), F32),
            pltpu.VMEM((rows, levels_wide, LANES), F32),
            pltpu.SemaphoreType.DMA((chunks,)),
            pltpu.SemaphoreType.DMA((6,)),
            pltpu.SemaphoreType.DMA((chunks,)),
            pltpu.SemaphoreType.DMA((10,)),
            pltpu.SemaphoreType.DMA((3,)),
            pltpu.SemaphoreType.DMA((sizes[1] // FIRST,)),
        ],
        compiler_params=pltpu.CompilerParams(vmem_limit_bytes=NETWORK_VMEM),
        cost_estimate=pl.CostEstimate(
            flops=4 * total, bytes_accessed=14_000_000, transcendentals=3_000_000
        ),
        name="column_network",
    )(inverse, tracer, along, across, *biases, x, *weights)


def half_minmod(first, second):
    return 0.5 * (
        jnp.maximum(jnp.minimum(first, second), 0.0)
        + jnp.minimum(jnp.maximum(first, second), 0.0)
    )


def cat(values):
    return values[0] if len(values) == 1 else jnp.concatenate(values, axis=0)


def advect_kernel(field, got_a, got_b, out, wide, speeds, sem, *, levels, axis):
    rows = field.shape[0]
    odd = lax.rem(lax.axis_index(axis), 2)
    own = pltpu.make_async_copy(field, wide.at[pl.ds(HALO, rows)], sem)
    own.start()
    wide[pl.ds((HALO + rows) * odd, HALO)] = got_a[...]
    wide[pl.ds((HALO + rows) * (1 - odd), HALO)] = got_b[...]

    def place(i):
        for kind in range(2):
            courant = jnp.broadcast_to(
                wide[i, levels + kind : levels + kind + 1, :], (8, LANES)
            )
            speeds[2 * kind, i] = jnp.maximum(courant, 0.0)
            speeds[2 * kind + 1, i] = jnp.minimum(courant, 0.0)

    for i in range(HALO):
        place(i)
        place(HALO + rows + i)
    own.wait()
    for i in range(HALO, HALO + rows):
        place(i)
    groups = wide.shape[1] // GROUP

    def group(g, carry):
        wavefront(g, groups, levels, out, wide, speeds, rows)
        return carry

    lax.fori_loop(0, groups, group, 0)


def wavefront(g, groups, levels, out, wide, speeds, rows):
    base = pl.multiple_of(g * GROUP, GROUP)
    blocks = GROUP // 8
    keep = levels - (groups - 1) * GROUP
    fields = [{}, {}, {}]
    steps, slopes, fluxes = [{}, {}, {}], [{}, {}, {}], [{}, {}, {}]
    reach = [(-4, rows + 3), (-2, rows + 1), (0, rows - 1)]
    shape = (blocks, 8, LANES)

    def load(i):
        return wide[i + HALO, pl.ds(base, GROUP), :].reshape(shape)

    def courant(kind, at):
        return cat([jnp.broadcast_to(speeds[kind, i + HALO], shape) for i in at])

    def pieces(value, count):
        return [value[n * blocks : (n + 1) * blocks] for n in range(count)]

    def face(active, at):
        ahead, behind = courant(0, at), courant(1, at)
        upper = cat([fields[k][i] - slopes[k][i] for k, i in zip(active, at)])
        lower = cat([fields[k][i - 1] + slopes[k][i - 1] for k, i in zip(active, at)])
        return ahead * lower + behind * upper

    rest = []
    for i in range(-HALO, -2):
        fields[0][i] = load(i)
    for t in range(-4, rows + 6):
        active = [k for k in range(3) if reach[k][0] <= t - 3 * k <= reach[k][1]]
        if t + 2 < rows + HALO:
            fields[0][t + 2] = load(t + 2)
        for k in active:
            c = t - 3 * k
            if c == reach[k][0]:
                f = fields[k]
                for i in (c - 1, c, c + 1):
                    steps[k][i] = f[i] - f[i - 1]
                for i in (c - 1, c):
                    slopes[k][i] = half_minmod(steps[k][i + 1], steps[k][i])
                fluxes[k][c] = face([k], [c])
        at = [t - 3 * k for k in active]
        here = cat([fields[k][i] for k, i in zip(active, at)])
        back = here - pltpu.roll(here, 1, 2)
        new = cat(
            [fields[k][i + 2] - fields[k][i + 1] for k, i in zip(active, at)]
        )
        last = cat([steps[k][i + 1] for k, i in zip(active, at)])
        bend = half_minmod(pltpu.roll(back, LANES - 1, 2), back)
        slope = half_minmod(new, last)
        for k, i, a_step, a_slope in zip(
            active, at, pieces(new, len(at)), pieces(slope, len(at))
        ):
            steps[k][i + 2], slopes[k][i + 1] = a_step, a_slope
        side = courant(2, at) * pltpu.roll(here + bend, 1, 2)
        side = side + courant(3, at) * (here - bend)
        flux = face(active, [i + 1 for i in at])
        for k, i, a_flux in zip(active, at, pieces(flux, len(at))):
            fluxes[k][i + 1] = a_flux
        moved = cat([fluxes[k][i] for k, i in zip(active, at)]) - flux
        moved = here + (moved + (side - pltpu.roll(side, LANES - 1, 2)))
        for k, i, value in zip(active, at, pieces(moved, len(at))):
            if k == 0:
                fields[1][i] = value
            elif k == 1:
                fields[2][i] = 0.75 * fields[0][i] + 0.25 * value
            else:
                value = 1.0 / 3.0 * fields[0][i] + 2.0 / 3.0 * value
                value = value.reshape(GROUP, LANES)
                out[pl.ds(base * rows + i, keep, stride=rows), :] = value[:keep]
                rest.append((i, value[keep:]))
    if keep < GROUP:

        @pl.when(g < groups - 1)
        def _():
            for i, value in rest:
                lines = pl.ds((base + keep) * rows + i, GROUP - keep, stride=rows)
                out[lines, :] = value


def advect(field, got_a, got_b, levels, axis):
    rows, levels_wide, across = field.shape
    vmem = pl.BlockSpec(memory_space=pltpu.VMEM)
    return pl.pallas_call(
        functools.partial(advect_kernel, levels=levels, axis=axis),
        out_shape=jax.ShapeDtypeStruct((levels * rows, across), F32),
        in_specs=[pl.BlockSpec(memory_space=pl.ANY), vmem, vmem],
        out_specs=vmem,
        scratch_shapes=[
            pltpu.VMEM((rows + 2 * HALO, levels_wide, across), F32),
            pltpu.VMEM((4, rows + 2 * HALO, 8, across), F32),
            pltpu.SemaphoreType.DMA,
        ],
        compiler_params=pltpu.CompilerParams(vmem_limit_bytes=ADVECT_VMEM),
        name="advect_sections",
    )(field, got_a, got_b)


def shards(inputs, tracer, speed_along, speed_across, inverse_list, *params):
    weights, biases = list(params[0::2]), params[1::2]
    weights[5] = weights[5].T
    levels, rows, across = tracer.shape
    tendencies, field, pay_a, pay_b = network(
        inverse_list.reshape(rows, across),
        tracer.reshape(levels * rows, across),
        speed_along,
        speed_across,
        biases,
        inputs.T,
        weights,
        "gx",
    )
    count = lax.axis_size("gx")
    outer = [(i, (i - 1 if i % 2 == 0 else i + 1) % count) for i in range(count)]
    inner = [(i, i + 1 if i % 2 == 0 else i - 1) for i in range(count)]
    got_a = lax.ppermute(pay_a, "gx", outer)
    got_b = lax.ppermute(pay_b, "gx", inner)
    advected = advect(field, got_a, got_b, levels, "gx")
    return tendencies.T, advected.reshape(levels, rows, across)


def solution(mesh):
    placed = (
        P(("member", "gx"), None),
        P(None, ("member", "gx"), None),
        P(("member", "gx"), None),
        P(("member", "gx"), None),
        P(("member", "gx")),
        *[P()] * 12,
    )
    return jax.shard_map(
        shards,
        mesh=mesh,
        in_specs=placed,
        out_specs=(P(("member", "gx"), None), P(None, ("member", "gx"), None)),
        check_vma=False,
    )
```

```python
import functools
import jax
import jax.numpy as jnp
from jax import lax
from jax.experimental import pallas as pl
from jax.experimental.pallas import tpu as pltpu
from jax.sharding import PartitionSpec as P

F32, BF16, F8 = jnp.float32, jnp.bfloat16, jnp.float8_e4m3fn
LANES = 128
CHUNK = 512
HALO = 6
GROUP = 32
WEIGHT_MAX = (0.25, 0.3125, 0.3125, 0.375, 0.3125, 0.3125)
BIAS_MAX = 3.0
INPUT_MAX = 6.0
SILU_DIP = 0.28
TOP = 440.0
WEIGHT_STEP = 2.0**10
LOW_STEP = 2.0**8
NETWORK_VMEM = 60_000_000
ADVECT_VMEM = 54_000_000
ROOM = 128


def round_up(value, unit):
    return -(-value // unit) * unit


def network_kernel(*refs, sizes, levels, axis):
    small_hbm, x_hbm, weights_hbm, refs = refs[:10], refs[10], refs[11:17], refs[17:]
    (tend_hbm, field_hbm, pay_a, pay_b), refs = refs[:4], refs[4:]
    x_in, weights_in, refs = refs[0], refs[1:7], refs[7:]
    cats, cats8, columns, refs = refs[:6], refs[6:12], refs[12:18], refs[18:]
    inverse, tracer, along, across, *biases = refs[:10]
    holds, holds8, refs = refs[10:12], refs[12:14], refs[14:]
    w_tail, x_tail, b_six, tend, peaks, shrinks, field, *sems = refs
    x_sems, w_sems, out_sems, small_sems, field_sems = sems

    chunks = x_hbm.shape[1] // CHUNK
    rows, levels_wide = field.shape[0], field.shape[1]
    depth_in = sizes[0]
    aligned = depth_in // 8 * 8
    whole = depth_in // LANES * LANES
    padded = [cats[layer].shape[1] for layer in range(6)]

    def x_copy(c):
        part = pl.ds(c * CHUNK, CHUNK)
        return pltpu.make_async_copy(x_hbm.at[:, part], x_in.at[:, part], x_sems.at[c])

    def w_copy(layer):
        target = weights_in[layer]
        if layer == 5:
            target = target.at[pl.ds(0, sizes[6])]
        return pltpu.make_async_copy(weights_hbm[layer], target, w_sems.at[layer])

    def small_copy(i):
        target = (inverse, tracer, along, across, *biases)[i]
        return pltpu.make_async_copy(small_hbm[i], target, small_sems.at[i])

    def out_copy(c):
        part = pl.ds(c * CHUNK, CHUNK)
        return pltpu.make_async_copy(
            tend.at[:, part], tend_hbm.at[:, part], out_sems.at[c]
        )

    def bias_columns(layer):
        count = sizes[layer + 1]
        source = biases[layer]
        if count % LANES:
            b_six[0:1, :] = jnp.zeros((1, b_six.shape[1]), F32)
            b_six[0:1, 0:count] = source[...].reshape(1, count)
            row = b_six[0:1, :]
        else:
            row = source[...].reshape(1, count)
        scale = 0.5 if layer < 5 else 1.0
        for n in range(0, count, LANES):
            block = jnp.broadcast_to(row[:, n : n + LANES], (LANES, LANES)).T * scale
            columns[layer][n : n + LANES, :] = block

    def put_weights(layer, lines, k, block):
        depth = padded[layer]
        if layer < 5:
            block = block * 0.5
        high = block.astype(BF16)
        low = block - high.astype(F32)
        step = WEIGHT_STEP * (2.0 if layer < 5 else 1.0)
        lanes, far = slice(k, k + LANES), slice(depth + k, depth + k + LANES)
        cats[layer][lines, lanes] = high
        cats8[layer][lines, lanes] = (block * step).astype(F8)
        cats8[layer][lines, far] = (low * (step * LOW_STEP)).astype(F8)

    def prepare(layer, part, parts):
        work = [
            (n, k)
            for n in range(0, round_up(sizes[layer + 1], LANES), LANES)
            for k in range(0, padded[layer], LANES)
        ]
        for n, k in work[part * len(work) // parts : (part + 1) * len(work) // parts]:
            lines, lanes = slice(n, n + LANES), slice(k, k + LANES)
            if layer == 5:
                block = weights_in[5][lines, lanes]
            elif layer == 0 and k >= whole:
                block = w_tail[:, lines].T
            else:
                block = weights_in[layer][lanes, lines].T
            put_weights(layer, lines, k, block)

    def put_rows(layer, start, cols, value, scale):
        depth = padded[layer]
        high = value.astype(BF16)
        low = value - high.astype(F32)
        size = value.shape[0]
        holds[layer % 2][start : start + size, cols] = high
        hold8 = holds8[layer % 2]
        hold8[start : start + size, cols] = (low * (scale * LOW_STEP)).astype(F8)
        hold8[depth + start : depth + start + size, cols] = (value * scale).astype(F8)

    def prepare_inputs(c):
        cols = slice(c * CHUNK, (c + 1) * CHUNK)
        x_tail[0 : aligned - whole, cols] = x_in[whole:aligned, cols]
        x_tail[aligned - whole : depth_in - whole, cols] = x_in[aligned:depth_in, cols]
        for k in range(0, whole, LANES):
            put_rows(0, k, cols, x_in[k : k + LANES, cols], TOP / INPUT_MAX)
        put_rows(0, whole, cols, x_tail[:, cols], TOP / INPUT_MAX)

    def main_product(layer, c):
        cols = slice(c * CHUNK, (c + 1) * CHUNK)
        return jnp.dot(
            cats[layer][...],
            holds[layer % 2][0 : padded[layer], cols],
            preferred_element_type=F32,
        )

    def rest_product(layer, c):
        cols = slice(c * CHUNK, (c + 1) * CHUNK)
        return jnp.dot(
            cats8[layer][...],
            holds8[layer % 2][0 : 2 * padded[layer], cols],
            preferred_element_type=F32,
        )

    def finish(layer, c, main, rest):
        cols = slice(c * CHUNK, (c + 1) * CHUNK)
        unit = 1.0 / (WEIGHT_STEP * LOW_STEP * (2.0 if layer < 5 else 1.0))
        if layer == 0:
            shrink, peak = jnp.full((1, CHUNK), INPUT_MAX / TOP, F32), INPUT_MAX
        else:
            shrink, peak = shrinks[layer : layer + 1, cols], peaks[layer : layer + 1, cols]
        bias = columns[layer][...]
        value = main + rest * (shrink * unit)
        value = value + jnp.concatenate([bias] * (CHUNK // LANES), axis=1)
        if layer < 5:
            value = value + value * jnp.tanh(value)
            limit = (sizes[layer] * WEIGHT_MAX[layer]) * peak + BIAS_MAX
            limit = jnp.broadcast_to(jnp.asarray(limit, F32), (1, CHUNK))
            put_rows(layer + 1, 0, cols, value, TOP / limit)
            shrinks[layer + 1 : layer + 2, cols] = limit / TOP
            highest = jnp.max(value, axis=0, keepdims=True)
            peaks[layer + 1 : layer + 2, cols] = jnp.maximum(highest, SILU_DIP)
            return
        for part in range(CHUNK // LANES):
            r = c * (CHUNK // LANES) + part
            day = inverse[r : r + 1, :] >= 0
            shown = jnp.where(
                day, value[: sizes[6], part * LANES : (part + 1) * LANES], 0.0
            )
            tend[:, r * LANES : (r + 1) * LANES] = shown
            field[r, 0:levels, :] = (
                tracer[pl.ds(r, levels, stride=rows), :] + shown[0:levels]
            )
        out_copy(c).start()

    w_copy(0).start()
    for c in range(chunks):
        x_copy(c).start()
    for i in range(10):
        small_copy(i).start()
    w_copy(1).start()
    w_tail[...] = jnp.zeros(w_tail.shape, F32)
    x_tail[...] = jnp.zeros(x_tail.shape, F32)
    weights_in[5][sizes[6] :, :] = jnp.zeros(
        (weights_in[5].shape[0] - sizes[6], sizes[5]), F32
    )
    w_copy(0).wait()
    w_tail[0 : aligned - whole, :] = weights_in[0][whole:aligned, :]
    w_tail[aligned - whole : depth_in - whole, :] = weights_in[0][aligned:depth_in, :]
    prepare(0, 0, 1)
    for layer in range(2, 6):
        w_copy(layer).start()
    x_copy(0).wait()
    prepare_inputs(0)

    for layer in range(6):
        if 0 < layer < 5:
            w_copy(layer + 1).wait()
        for c in range(chunks):
            main = main_product(layer, c)
            if layer == 0 and c == 0:
                for i in range(10):
                    small_copy(i).wait()
                bias_columns(0)
                for i in range(1, chunks):
                    x_copy(i).wait()
                    prepare_inputs(i)
                w_copy(1).wait()
            if layer < 5:
                prepare(layer + 1, c, chunks)
            rest = rest_product(layer, c)
            if layer == 4 and c == 0:
                for r in range(rows):
                    field[r, levels : levels + 1, :] = along[r : r + 1, :]
                    field[r, levels + 1 : levels + 2, :] = across[r : r + 1, :]
                    field[r, levels + 2 : levels_wide, :] = jnp.zeros(
                        (levels_wide - levels - 2, LANES), F32
                    )
            if layer < 5 and c == chunks - 1:
                bias_columns(layer + 1)
            finish(layer, c, main, rest)

    odd = lax.rem(lax.axis_index(axis), 2)
    leaving = [
        pltpu.make_async_copy(
            field.at[pl.ds((rows - HALO) * odd, HALO)], pay_a, field_sems.at[0]
        ),
        pltpu.make_async_copy(
            field.at[pl.ds((rows - HALO) * (1 - odd), HALO)], pay_b, field_sems.at[1]
        ),
        pltpu.make_async_copy(field, field_hbm.at[pl.ds(0, rows)], field_sems.at[2]),
    ]
    for copy in leaving:
        copy.start()
    for copy in leaving:
        copy.wait()
    for c in range(chunks):
        out_copy(c).wait()


def network(inverse, tracer, along, across, biases, x, weights, axis):
    sizes = [x.shape[0]] + [b.shape[0] for b in biases]
    width = x.shape[1]
    rows = along.shape[0]
    levels = tracer.shape[0] // rows
    levels_wide = round_up(levels + 2, 8)
    chunks = width // CHUNK
    padded = [round_up(s, LANES) for s in sizes]
    deepest = max(padded[:6])
    tail = padded[0] - sizes[0] // LANES * LANES
    hbm = pl.BlockSpec(memory_space=pl.ANY)
    total = sum(sizes[i] * sizes[i + 1] for i in range(6)) * width
    return pl.pallas_call(
        functools.partial(network_kernel, sizes=sizes, levels=levels, axis=axis),
        out_shape=(
            jax.ShapeDtypeStruct((sizes[6], width), F32),
            jax.ShapeDtypeStruct((ROOM, levels_wide, LANES), F32),
            jax.ShapeDtypeStruct((HALO, levels_wide, LANES), F32),
            jax.ShapeDtypeStruct((HALO, levels_wide, LANES), F32),
        ),
        in_specs=[hbm] * 17,
        out_specs=(hbm,) * 4,
        scratch_shapes=[
            pltpu.VMEM(x.shape, F32),
            *[pltpu.VMEM(w.shape, F32) for w in weights[:5]],
            pltpu.VMEM((padded[6], sizes[5]), F32),
            *[pltpu.VMEM((padded[i + 1], padded[i]), BF16) for i in range(6)],
            *[pltpu.VMEM((padded[i + 1], 2 * padded[i]), F8) for i in range(6)],
            *[pltpu.VMEM((padded[i + 1], LANES), F32) for i in range(6)],
            pltpu.VMEM(inverse.shape, jnp.int32),
            pltpu.VMEM(tracer.shape, F32),
            pltpu.VMEM(along.shape, F32),
            pltpu.VMEM(across.shape, F32),
            *[pltpu.VMEM(b.shape, F32) for b in biases],
            *[pltpu.VMEM((deepest, width), BF16)] * 2,
            *[pltpu.VMEM((2 * deepest, width), F8)] * 2,
            pltpu.VMEM((tail, sizes[1]), F32),
            pltpu.VMEM((tail, width), F32),
            pltpu.VMEM((8, padded[6]), F32),
            pltpu.VMEM((sizes[6], width), F32),
            pltpu.VMEM((8, width), F32),
            pltpu.VMEM((8, width), F32),
            pltpu.VMEM((rows, levels_wide, LANES), F32),
            pltpu.SemaphoreType.DMA((chunks,)),
            pltpu.SemaphoreType.DMA((6,)),
            pltpu.SemaphoreType.DMA((chunks,)),
            pltpu.SemaphoreType.DMA((10,)),
            pltpu.SemaphoreType.DMA((3,)),
        ],
        compiler_params=pltpu.CompilerParams(vmem_limit_bytes=NETWORK_VMEM),
        cost_estimate=pl.CostEstimate(
            flops=4 * total, bytes_accessed=14_000_000, transcendentals=3_000_000
        ),
        name="column_network",
    )(inverse, tracer, along, across, *biases, x, *weights)


def half_minmod(first, second):
    return 0.5 * (
        jnp.maximum(jnp.minimum(first, second), 0.0)
        + jnp.minimum(jnp.maximum(first, second), 0.0)
    )


def cat(values):
    return values[0] if len(values) == 1 else jnp.concatenate(values, axis=0)


def advect_kernel(
    field, got_a, got_b, out, wide, speeds, held, in_sems, out_sems, *, levels, axis
):
    rows = wide.shape[0] - 2 * HALO
    odd = lax.rem(lax.axis_index(axis), 2)
    arriving = [
        pltpu.make_async_copy(source, wide.at[pl.ds(start, source.shape[0])], in_sems.at[n])
        for n, (source, start) in enumerate(
            [
                (field, HALO),
                (got_a, (HALO + rows) * odd),
                (got_b, (HALO + rows) * (1 - odd)),
            ]
        )
    ]
    for copy in arriving:
        copy.start()

    def place(i):
        for kind in range(2):
            courant = jnp.broadcast_to(
                wide[i, levels + kind : levels + kind + 1, :], (8, LANES)
            )
            speeds[2 * kind, i] = jnp.maximum(courant, 0.0)
            speeds[2 * kind + 1, i] = jnp.minimum(courant, 0.0)

    for copy in arriving:
        copy.wait()
    for i in range(rows + 2 * HALO):
        place(i)
    groups = wide.shape[1] // GROUP
    span = GROUP * rows

    def leaving(g, start, size):
        return pltpu.make_async_copy(
            held.at[pl.ds(start, size)], out.at[pl.ds(start, size)], out_sems.at[g]
        )

    last = out.shape[0] - (groups - 1) * span

    def group(g, carry):
        wavefront(g, groups, levels, held, wide, speeds, rows)

        @pl.when(g < groups - 1)
        def _():
            leaving(g, pl.multiple_of(g * span, span), span).start()

        return carry

    lax.fori_loop(0, groups, group, 0)
    leaving(groups - 1, (groups - 1) * span, last).start()
    for g in range(groups - 1):
        leaving(g, g * span, span).wait()
    leaving(groups - 1, (groups - 1) * span, last).wait()


def wavefront(g, groups, levels, out, wide, speeds, rows):
    base = pl.multiple_of(g * GROUP, GROUP)
    blocks = GROUP // 8
    keep = levels - (groups - 1) * GROUP
    fields = [{}, {}, {}]
    steps, slopes, fluxes = [{}, {}, {}], [{}, {}, {}], [{}, {}, {}]
    reach = [(-4, rows + 3), (-2, rows + 1), (0, rows - 1)]
    shape = (blocks, 8, LANES)

    def load(i):
        return wide[i + HALO, pl.ds(base, GROUP), :].reshape(shape)

    def courant(kind, at):
        return cat([jnp.broadcast_to(speeds[kind, i + HALO], shape) for i in at])

    def pieces(value, count):
        return [value[n * blocks : (n + 1) * blocks] for n in range(count)]

    def face(active, at):
        ahead, behind = courant(0, at), courant(1, at)
        upper = cat([fields[k][i] - slopes[k][i] for k, i in zip(active, at)])
        lower = cat([fields[k][i - 1] + slopes[k][i - 1] for k, i in zip(active, at)])
        return ahead * lower + behind * upper

    rest = []
    for i in range(-HALO, -2):
        fields[0][i] = load(i)
    for t in range(-4, rows + 6):
        active = [k for k in range(3) if reach[k][0] <= t - 3 * k <= reach[k][1]]
        if t + 2 < rows + HALO:
            fields[0][t + 2] = load(t + 2)
        for k in active:
            c = t - 3 * k
            if c == reach[k][0]:
                f = fields[k]
                for i in (c - 1, c, c + 1):
                    steps[k][i] = f[i] - f[i - 1]
                for i in (c - 1, c):
                    slopes[k][i] = half_minmod(steps[k][i + 1], steps[k][i])
                fluxes[k][c] = face([k], [c])
        at = [t - 3 * k for k in active]
        here = cat([fields[k][i] for k, i in zip(active, at)])
        back = here - pltpu.roll(here, 1, 2)
        new = cat(
            [fields[k][i + 2] - fields[k][i + 1] for k, i in zip(active, at)]
        )
        last = cat([steps[k][i + 1] for k, i in zip(active, at)])
        bend = half_minmod(pltpu.roll(back, LANES - 1, 2), back)
        slope = half_minmod(new, last)
        for k, i, a_step, a_slope in zip(
            active, at, pieces(new, len(at)), pieces(slope, len(at))
        ):
            steps[k][i + 2], slopes[k][i + 1] = a_step, a_slope
        side = courant(2, at) * pltpu.roll(here + bend, 1, 2)
        side = side + courant(3, at) * (here - bend)
        flux = face(active, [i + 1 for i in at])
        for k, i, a_flux in zip(active, at, pieces(flux, len(at))):
            fluxes[k][i + 1] = a_flux
        moved = cat([fluxes[k][i] for k, i in zip(active, at)]) - flux
        moved = here + (moved + (side - pltpu.roll(side, LANES - 1, 2)))
        for k, i, value in zip(active, at, pieces(moved, len(at))):
            if k == 0:
                fields[1][i] = value
            elif k == 1:
                fields[2][i] = 0.75 * fields[0][i] + 0.25 * value
            else:
                value = 1.0 / 3.0 * fields[0][i] + 2.0 / 3.0 * value
                value = value.reshape(GROUP, LANES)
                out[pl.ds(base * rows + i, keep, stride=rows), :] = value[:keep]
                rest.append((i, value[keep:]))
    if keep < GROUP:

        @pl.when(g < groups - 1)
        def _():
            for i, value in rest:
                lines = pl.ds((base + keep) * rows + i, GROUP - keep, stride=rows)
                out[lines, :] = value


def stage_kernel(field, own, sem):
    copy = pltpu.make_async_copy(field.at[pl.ds(0, own.shape[0])], own, sem)
    copy.start()
    copy.wait()


def stage(field, rows):
    return pl.pallas_call(
        stage_kernel,
        out_shape=jax.ShapeDtypeStruct((rows, *field.shape[1:]), F32),
        in_specs=[pl.BlockSpec(memory_space=pl.ANY)],
        out_specs=pl.BlockSpec(memory_space=pltpu.VMEM),
        scratch_shapes=[pltpu.SemaphoreType.DMA],
        compiler_params=pltpu.CompilerParams(vmem_limit_bytes=ADVECT_VMEM),
        cost_estimate=pl.CostEstimate(
            flops=0, bytes_accessed=4_000_000, transcendentals=0
        ),
        name="stage_rows",
    )(field)


def advect(field, got_a, got_b, levels, axis):
    rows, levels_wide, across = field.shape
    hbm = pl.BlockSpec(memory_space=pl.ANY)
    return pl.pallas_call(
        functools.partial(advect_kernel, levels=levels, axis=axis),
        out_shape=jax.ShapeDtypeStruct((levels * rows, across), F32),
        in_specs=[hbm] * 3,
        out_specs=hbm,
        scratch_shapes=[
            pltpu.VMEM((rows + 2 * HALO, levels_wide, across), F32),
            pltpu.VMEM((4, rows + 2 * HALO, 8, across), F32),
            pltpu.VMEM((levels * rows, across), F32),
            pltpu.SemaphoreType.DMA((3,)),
            pltpu.SemaphoreType.DMA((levels_wide // GROUP,)),
        ],
        compiler_params=pltpu.CompilerParams(vmem_limit_bytes=ADVECT_VMEM),
        name="advect_sections",
    )(field, got_a, got_b)


def shards(inputs, tracer, speed_along, speed_across, inverse_list, *params):
    weights, biases = list(params[0::2]), params[1::2]
    weights[5] = weights[5].T
    levels, rows, across = tracer.shape
    tendencies, field, pay_a, pay_b = network(
        inverse_list.reshape(rows, across),
        tracer.reshape(levels * rows, across),
        speed_along,
        speed_across,
        biases,
        inputs.T,
        weights,
        "gx",
    )
    count = lax.axis_size("gx")
    outer = [(i, (i - 1 if i % 2 == 0 else i + 1) % count) for i in range(count)]
    inner = [(i, i + 1 if i % 2 == 0 else i - 1) for i in range(count)]
    got_a = lax.ppermute(pay_a, "gx", outer)
    got_b = lax.ppermute(pay_b, "gx", inner)
    advected = advect(stage(field, rows), got_a, got_b, levels, "gx")
    return tendencies.T, advected.reshape(levels, rows, across)


def solution(mesh):
    placed = (
        P(("member", "gx"), None),
        P(None, ("member", "gx"), None),
        P(("member", "gx"), None),
        P(("member", "gx"), None),
        P(("member", "gx")),
        *[P()] * 12,
    )
    return jax.shard_map(
        shards,
        mesh=mesh,
        in_specs=placed,
        out_specs=(P(("member", "gx"), None), P(None, ("member", "gx"), None)),
        check_vma=False,
    )
```

```python
import functools
import jax
import jax.numpy as jnp
from jax import lax
from jax.experimental import pallas as pl
from jax.experimental.pallas import tpu as pltpu
from jax.sharding import PartitionSpec as P

F32, BF16, F8 = jnp.float32, jnp.bfloat16, jnp.float8_e4m3fn
LANES = 128
CHUNK = 512
HALO = 6
GROUP = 32
WEIGHT_MAX = (0.25, 0.3125, 0.3125, 0.375, 0.3125, 0.3125)
BIAS_MAX = 3.0
INPUT_MAX = 6.0
SILU_DIP = 0.28
TOP = 440.0
INPUT_SCALE = 72.0
MIXED = (0, 1, 3, 4)
WEIGHT_STEP = 2.0**10
LOW_STEP = 2.0**8
NETWORK_VMEM = 60_000_000
ADVECT_VMEM = 54_000_000
ROOM = 128


def round_up(value, unit):
    return -(-value // unit) * unit


def network_kernel(*refs, sizes, levels, axis):
    small_hbm, x_hbm, weights_hbm, refs = refs[:10], refs[10], refs[11:17], refs[17:]
    (tend_hbm, field_hbm, pay_a, pay_b), refs = refs[:4], refs[4:]
    x_in, weights_in, refs = refs[0], refs[1:7], refs[7:]
    cats, cats8, columns, refs = refs[:6], refs[6:12], refs[12:18], refs[18:]
    inverse, tracer, along, across, *biases = refs[:10]
    holds, holds8, refs = refs[10:12], refs[12:14], refs[14:]
    w_tail, x_tail, b_six, tend, peaks, shrinks, field, *sems = refs
    x_sems, w_sems, out_sems, small_sems, field_sems = sems

    chunks = x_hbm.shape[1] // CHUNK
    rows, levels_wide = field.shape[0], field.shape[1]
    depth_in = sizes[0]
    aligned = depth_in // 8 * 8
    whole = depth_in // LANES * LANES
    padded = [round_up(sizes[layer], LANES) for layer in range(6)]

    def x_copy(c):
        part = pl.ds(c * CHUNK, CHUNK)
        return pltpu.make_async_copy(x_hbm.at[:, part], x_in.at[:, part], x_sems.at[c])

    def w_copy(layer):
        target = weights_in[layer]
        if layer == 5:
            target = target.at[pl.ds(0, sizes[6])]
        return pltpu.make_async_copy(weights_hbm[layer], target, w_sems.at[layer])

    def small_copy(i):
        target = (inverse, tracer, along, across, *biases)[i]
        return pltpu.make_async_copy(small_hbm[i], target, small_sems.at[i])

    def out_copy(c):
        part = pl.ds(c * CHUNK, CHUNK)
        return pltpu.make_async_copy(
            tend.at[:, part], tend_hbm.at[:, part], out_sems.at[c]
        )

    def bias_columns(layer):
        count = sizes[layer + 1]
        source = biases[layer]
        if count % LANES:
            b_six[0:1, :] = jnp.zeros((1, b_six.shape[1]), F32)
            b_six[0:1, 0:count] = source[...].reshape(1, count)
            row = b_six[0:1, :]
        else:
            row = source[...].reshape(1, count)
        scale = 0.5 if layer < 5 else 1.0
        for n in range(0, count, LANES):
            block = jnp.broadcast_to(row[:, n : n + LANES], (LANES, LANES)).T * scale
            columns[layer][n : n + LANES, :] = block

    def put_weights(layer, lines, k, block):
        depth = padded[layer]
        if layer < 5:
            block = block * 0.5
        high = block.astype(BF16)
        low = block - high.astype(F32)
        cats[layer][lines, k : k + LANES] = high
        if layer not in MIXED:
            cats[layer][lines, depth + k : depth + k + LANES] = high
            cats[layer][lines, 2 * depth + k : 2 * depth + k + LANES] = low.astype(BF16)
            return
        step = WEIGHT_STEP * (2.0 if layer < 5 else 1.0)
        lanes, far = slice(k, k + LANES), slice(depth + k, depth + k + LANES)
        cats8[layer][lines, lanes] = (high * BF16(step)).astype(F8)
        cats8[layer][lines, far] = (low * (step * LOW_STEP)).astype(F8)

    def prepare(layer, part, parts):
        work = [
            (n, k)
            for n in range(0, round_up(sizes[layer + 1], LANES), LANES)
            for k in range(0, padded[layer], LANES)
        ]
        for n, k in work[part * len(work) // parts : (part + 1) * len(work) // parts]:
            lines, lanes = slice(n, n + LANES), slice(k, k + LANES)
            if layer == 5:
                block = weights_in[5][lines, lanes]
            elif layer == 0 and k >= whole:
                block = w_tail[:, lines].T
            else:
                block = weights_in[layer][lanes, lines].T
            put_weights(layer, lines, k, block)

    def put_rows(layer, start, cols, value, scale):
        depth = padded[layer]
        high = value.astype(BF16)
        low = value - high.astype(F32)
        size = value.shape[0]
        hold, hold8 = holds[layer % 2], holds8[layer % 2]
        near = slice(start, start + size)
        middle = slice(depth + start, depth + start + size)
        hold[near, cols] = high
        if layer not in MIXED:
            hold[middle, cols] = low.astype(BF16)
            hold[2 * depth + start : 2 * depth + start + size, cols] = high
            return
        hold8[near, cols] = (low * (scale * LOW_STEP)).astype(F8)
        hold8[middle, cols] = (high * scale.astype(BF16)).astype(F8)

    first_scale = jnp.full((1, CHUNK), INPUT_SCALE, F32)

    def prepare_inputs(c):
        cols = slice(c * CHUNK, (c + 1) * CHUNK)
        x_tail[0 : aligned - whole, cols] = x_in[whole:aligned, cols]
        x_tail[aligned - whole : depth_in - whole, cols] = x_in[aligned:depth_in, cols]
        for k in range(0, whole, LANES):
            put_rows(0, k, cols, x_in[k : k + LANES, cols], first_scale)
        put_rows(0, whole, cols, x_tail[:, cols], first_scale)

    def main_product(layer, c):
        cols = slice(c * CHUNK, (c + 1) * CHUNK)
        return jnp.dot(
            cats[layer][...],
            holds[layer % 2][0 : cats[layer].shape[1], cols],
            preferred_element_type=F32,
        )

    def rest_product(layer, c):
        if layer not in MIXED:
            return None
        cols = slice(c * CHUNK, (c + 1) * CHUNK)
        return jnp.dot(
            cats8[layer][...],
            holds8[layer % 2][0 : 2 * padded[layer], cols],
            preferred_element_type=F32,
        )

    def finish(layer, c, main, rest):
        cols = slice(c * CHUNK, (c + 1) * CHUNK)
        unit = 1.0 / (WEIGHT_STEP * LOW_STEP * (2.0 if layer < 5 else 1.0))
        value = main
        if layer in MIXED:
            shrink = shrinks[layer : layer + 1, cols] if layer else 1.0 / first_scale
            value = value + rest * (shrink * unit)
        peak = peaks[layer : layer + 1, cols] if layer else INPUT_MAX
        bias = columns[layer][...]
        value = value + jnp.concatenate([bias] * (CHUNK // LANES), axis=1)
        if layer < 5:
            value = value + value * jnp.tanh(value)
            limit = (sizes[layer] * WEIGHT_MAX[layer]) * peak + BIAS_MAX
            limit = jnp.broadcast_to(jnp.asarray(limit, F32), (1, CHUNK))
            scale = (TOP / limit).astype(BF16).astype(F32)
            put_rows(layer + 1, 0, cols, value, scale)
            if layer + 1 in MIXED:
                shrinks[layer + 1 : layer + 2, cols] = 1.0 / scale
            if layer + 2 in MIXED:
                highest = jnp.max(value, axis=0, keepdims=True)
                peaks[layer + 1 : layer + 2, cols] = jnp.maximum(highest, SILU_DIP)
            return
        for part in range(CHUNK // LANES):
            r = c * (CHUNK // LANES) + part
            day = inverse[r : r + 1, :] >= 0
            shown = jnp.where(
                day, value[: sizes[6], part * LANES : (part + 1) * LANES], 0.0
            )
            tend[:, r * LANES : (r + 1) * LANES] = shown
            field[r, 0:levels, :] = (
                tracer[pl.ds(r, levels, stride=rows), :] + shown[0:levels]
            )
        out_copy(c).start()

    w_copy(0).start()
    for c in range(chunks):
        x_copy(c).start()
    for i in range(10):
        small_copy(i).start()
    w_copy(1).start()
    w_tail[...] = jnp.zeros(w_tail.shape, F32)
    x_tail[...] = jnp.zeros(x_tail.shape, F32)
    weights_in[5][sizes[6] :, :] = jnp.zeros(
        (weights_in[5].shape[0] - sizes[6], sizes[5]), F32
    )
    w_copy(0).wait()
    w_tail[0 : aligned - whole, :] = weights_in[0][whole:aligned, :]
    w_tail[aligned - whole : depth_in - whole, :] = weights_in[0][aligned:depth_in, :]
    prepare(0, 0, 1)
    for layer in range(2, 6):
        w_copy(layer).start()
    x_copy(0).wait()
    prepare_inputs(0)

    for layer in range(6):
        if 0 < layer < 5:
            w_copy(layer + 1).wait()
        for c in range(chunks):
            main = main_product(layer, c)
            if layer == 0 and c == 0:
                for i in range(10):
                    small_copy(i).wait()
                bias_columns(0)
                for i in range(1, chunks):
                    x_copy(i).wait()
                    prepare_inputs(i)
                w_copy(1).wait()
            if layer < 5:
                prepare(layer + 1, c, chunks)
            rest = rest_product(layer, c)
            if layer == 4 and c == 0:
                for r in range(rows):
                    field[r, levels : levels + 1, :] = along[r : r + 1, :]
                    field[r, levels + 1 : levels + 2, :] = across[r : r + 1, :]
                    field[r, levels + 2 : levels_wide, :] = jnp.zeros(
                        (levels_wide - levels - 2, LANES), F32
                    )
            if layer < 5 and c == chunks - 1:
                bias_columns(layer + 1)
            finish(layer, c, main, rest)

    odd = lax.rem(lax.axis_index(axis), 2)
    leaving = [
        pltpu.make_async_copy(
            field.at[pl.ds((rows - HALO) * odd, HALO)], pay_a, field_sems.at[0]
        ),
        pltpu.make_async_copy(
            field.at[pl.ds((rows - HALO) * (1 - odd), HALO)], pay_b, field_sems.at[1]
        ),
        pltpu.make_async_copy(field, field_hbm.at[pl.ds(0, rows)], field_sems.at[2]),
    ]
    for copy in leaving:
        copy.start()
    for copy in leaving:
        copy.wait()
    for c in range(chunks):
        out_copy(c).wait()


def network(inverse, tracer, along, across, biases, x, weights, axis):
    sizes = [x.shape[0]] + [b.shape[0] for b in biases]
    width = x.shape[1]
    rows = along.shape[0]
    levels = tracer.shape[0] // rows
    levels_wide = round_up(levels + 2, 8)
    chunks = width // CHUNK
    padded = [round_up(s, LANES) for s in sizes]
    deepest = max(padded[:6])
    tail = padded[0] - sizes[0] // LANES * LANES
    hbm = pl.BlockSpec(memory_space=pl.ANY)
    total = sum(sizes[i] * sizes[i + 1] for i in range(6)) * width
    return pl.pallas_call(
        functools.partial(network_kernel, sizes=sizes, levels=levels, axis=axis),
        out_shape=(
            jax.ShapeDtypeStruct((sizes[6], width), F32),
            jax.ShapeDtypeStruct((ROOM, levels_wide, LANES), F32),
            jax.ShapeDtypeStruct((HALO, levels_wide, LANES), F32),
            jax.ShapeDtypeStruct((HALO, levels_wide, LANES), F32),
        ),
        in_specs=[hbm] * 17,
        out_specs=(hbm,) * 4,
        scratch_shapes=[
            pltpu.VMEM(x.shape, F32),
            *[pltpu.VMEM(w.shape, F32) for w in weights[:5]],
            pltpu.VMEM((padded[6], sizes[5]), F32),
            *[
                pltpu.VMEM((padded[i + 1], padded[i] * (1 if i in MIXED else 3)), BF16)
                for i in range(6)
            ],
            *[pltpu.VMEM((padded[i + 1], 2 * padded[i]), F8) for i in range(6)],
            *[pltpu.VMEM((padded[i + 1], LANES), F32) for i in range(6)],
            pltpu.VMEM(inverse.shape, jnp.int32),
            pltpu.VMEM(tracer.shape, F32),
            pltpu.VMEM(along.shape, F32),
            pltpu.VMEM(across.shape, F32),
            *[pltpu.VMEM(b.shape, F32) for b in biases],
            *[pltpu.VMEM((3 * deepest, width), BF16)] * 2,
            *[pltpu.VMEM((2 * deepest, width), F8)] * 2,
            pltpu.VMEM((tail, sizes[1]), F32),
            pltpu.VMEM((tail, width), F32),
            pltpu.VMEM((8, padded[6]), F32),
            pltpu.VMEM((sizes[6], width), F32),
            pltpu.VMEM((8, width), F32),
            pltpu.VMEM((8, width), F32),
            pltpu.VMEM((rows, levels_wide, LANES), F32),
            pltpu.SemaphoreType.DMA((chunks,)),
            pltpu.SemaphoreType.DMA((6,)),
            pltpu.SemaphoreType.DMA((chunks,)),
            pltpu.SemaphoreType.DMA((10,)),
            pltpu.SemaphoreType.DMA((3,)),
        ],
        compiler_params=pltpu.CompilerParams(vmem_limit_bytes=NETWORK_VMEM),
        cost_estimate=pl.CostEstimate(
            flops=4 * total, bytes_accessed=14_000_000, transcendentals=3_000_000
        ),
        name="column_network",
    )(inverse, tracer, along, across, *biases, x, *weights)


def half_minmod(first, second):
    return 0.5 * (
        jnp.maximum(jnp.minimum(first, second), 0.0)
        + jnp.minimum(jnp.maximum(first, second), 0.0)
    )


def cat(values):
    return values[0] if len(values) == 1 else jnp.concatenate(values, axis=0)


def advect_kernel(
    field, got_a, got_b, out, wide, speeds, held, out_sems, *, levels, axis
):
    rows = field.shape[0]
    odd = lax.rem(lax.axis_index(axis), 2)
    wide[HALO : HALO + rows] = field[...]
    wide[pl.ds((HALO + rows) * odd, HALO)] = got_a[...]
    wide[pl.ds((HALO + rows) * (1 - odd), HALO)] = got_b[...]

    def place(i):
        for kind in range(2):
            courant = jnp.broadcast_to(
                wide[i, levels + kind : levels + kind + 1, :], (8, LANES)
            )
            speeds[2 * kind, i] = jnp.maximum(courant, 0.0)
            speeds[2 * kind + 1, i] = jnp.minimum(courant, 0.0)

    for i in range(rows + 2 * HALO):
        place(i)
    groups = wide.shape[1] // GROUP
    span = GROUP * rows

    def leaving(g, start, size):
        return pltpu.make_async_copy(
            held.at[pl.ds(start, size)], out.at[pl.ds(start, size)], out_sems.at[g]
        )

    last = out.shape[0] - (groups - 1) * span

    def group(g, carry):
        wavefront(g, groups, levels, held, wide, speeds, rows)

        @pl.when(g < groups - 1)
        def _():
            leaving(g, pl.multiple_of(g * span, span), span).start()

        return carry

    lax.fori_loop(0, groups, group, 0)
    leaving(groups - 1, (groups - 1) * span, last).start()
    for g in range(groups - 1):
        leaving(g, g * span, span).wait()
    leaving(groups - 1, (groups - 1) * span, last).wait()


def wavefront(g, groups, levels, out, wide, speeds, rows):
    base = pl.multiple_of(g * GROUP, GROUP)
    blocks = GROUP // 8
    keep = levels - (groups - 1) * GROUP
    fields = [{}, {}, {}]
    steps, slopes, fluxes = [{}, {}, {}], [{}, {}, {}], [{}, {}, {}]
    reach = [(-4, rows + 3), (-2, rows + 1), (0, rows - 1)]
    shape = (blocks, 8, LANES)

    def load(i):
        return wide[i + HALO, pl.ds(base, GROUP), :].reshape(shape)

    def courant(kind, at):
        return cat([jnp.broadcast_to(speeds[kind, i + HALO], shape) for i in at])

    def pieces(value, count):
        return [value[n * blocks : (n + 1) * blocks] for n in range(count)]

    def face(active, at):
        ahead, behind = courant(0, at), courant(1, at)
        upper = cat([fields[k][i] - slopes[k][i] for k, i in zip(active, at)])
        lower = cat([fields[k][i - 1] + slopes[k][i - 1] for k, i in zip(active, at)])
        return ahead * lower + behind * upper

    rest = []
    for i in range(-HALO, -2):
        fields[0][i] = load(i)
    for t in range(-4, rows + 6):
        active = [k for k in range(3) if reach[k][0] <= t - 3 * k <= reach[k][1]]
        if t + 2 < rows + HALO:
            fields[0][t + 2] = load(t + 2)
        for k in active:
            c = t - 3 * k
            if c == reach[k][0]:
                f = fields[k]
                for i in (c - 1, c, c + 1):
                    steps[k][i] = f[i] - f[i - 1]
                for i in (c - 1, c):
                    slopes[k][i] = half_minmod(steps[k][i + 1], steps[k][i])
                fluxes[k][c] = face([k], [c])
        at = [t - 3 * k for k in active]
        here = cat([fields[k][i] for k, i in zip(active, at)])
        back = here - pltpu.roll(here, 1, 2)
        new = cat(
            [fields[k][i + 2] - fields[k][i + 1] for k, i in zip(active, at)]
        )
        last = cat([steps[k][i + 1] for k, i in zip(active, at)])
        bend = half_minmod(pltpu.roll(back, LANES - 1, 2), back)
        slope = half_minmod(new, last)
        for k, i, a_step, a_slope in zip(
            active, at, pieces(new, len(at)), pieces(slope, len(at))
        ):
            steps[k][i + 2], slopes[k][i + 1] = a_step, a_slope
        side = courant(2, at) * pltpu.roll(here + bend, 1, 2)
        side = side + courant(3, at) * (here - bend)
        flux = face(active, [i + 1 for i in at])
        for k, i, a_flux in zip(active, at, pieces(flux, len(at))):
            fluxes[k][i + 1] = a_flux
        moved = cat([fluxes[k][i] for k, i in zip(active, at)]) - flux
        moved = here + (moved + (side - pltpu.roll(side, LANES - 1, 2)))
        for k, i, value in zip(active, at, pieces(moved, len(at))):
            if k == 0:
                fields[1][i] = value
            elif k == 1:
                fields[2][i] = 0.75 * fields[0][i] + 0.25 * value
            else:
                value = 1.0 / 3.0 * fields[0][i] + 2.0 / 3.0 * value
                value = value.reshape(GROUP, LANES)
                out[pl.ds(base * rows + i, keep, stride=rows), :] = value[:keep]
                rest.append((i, value[keep:]))
    if keep < GROUP:

        @pl.when(g < groups - 1)
        def _():
            for i, value in rest:
                lines = pl.ds((base + keep) * rows + i, GROUP - keep, stride=rows)
                out[lines, :] = value


def stage_kernel(field, own, sem):
    copy = pltpu.make_async_copy(field.at[pl.ds(0, own.shape[0])], own, sem)
    copy.start()
    copy.wait()


def stage(field, rows):
    return pl.pallas_call(
        stage_kernel,
        out_shape=jax.ShapeDtypeStruct((rows, *field.shape[1:]), F32),
        in_specs=[pl.BlockSpec(memory_space=pl.ANY)],
        out_specs=pl.BlockSpec(memory_space=pltpu.VMEM),
        scratch_shapes=[pltpu.SemaphoreType.DMA],
        compiler_params=pltpu.CompilerParams(vmem_limit_bytes=ADVECT_VMEM),
        cost_estimate=pl.CostEstimate(
            flops=0, bytes_accessed=4_000_000, transcendentals=0
        ),
        name="stage_rows",
    )(field)


def advect(field, got_a, got_b, levels, axis):
    rows, levels_wide, across = field.shape
    vmem, hbm = pl.BlockSpec(memory_space=pltpu.VMEM), pl.BlockSpec(memory_space=pl.ANY)
    return pl.pallas_call(
        functools.partial(advect_kernel, levels=levels, axis=axis),
        out_shape=jax.ShapeDtypeStruct((levels * rows, across), F32),
        in_specs=[vmem] * 3,
        out_specs=hbm,
        scratch_shapes=[
            pltpu.VMEM((rows + 2 * HALO, levels_wide, across), F32),
            pltpu.VMEM((4, rows + 2 * HALO, 8, across), F32),
            pltpu.VMEM((levels * rows, across), F32),
            pltpu.SemaphoreType.DMA((levels_wide // GROUP,)),
        ],
        compiler_params=pltpu.CompilerParams(vmem_limit_bytes=ADVECT_VMEM),
        name="advect_sections",
    )(field, got_a, got_b)


def shards(inputs, tracer, speed_along, speed_across, inverse_list, *params):
    weights, biases = list(params[0::2]), params[1::2]
    weights[5] = weights[5].T
    levels, rows, across = tracer.shape
    tendencies, field, pay_a, pay_b = network(
        inverse_list.reshape(rows, across),
        tracer.reshape(levels * rows, across),
        speed_along,
        speed_across,
        biases,
        inputs.T,
        weights,
        "gx",
    )
    count = lax.axis_size("gx")
    outer = [(i, (i - 1 if i % 2 == 0 else i + 1) % count) for i in range(count)]
    inner = [(i, i + 1 if i % 2 == 0 else i - 1) for i in range(count)]
    got_a = lax.ppermute(pay_a, "gx", outer)
    got_b = lax.ppermute(pay_b, "gx", inner)
    advected = advect(stage(field, rows), got_a, got_b, levels, "gx")
    return tendencies.T, advected.reshape(levels, rows, across)


def solution(mesh):
    placed = (
        P(("member", "gx"), None),
        P(None, ("member", "gx"), None),
        P(("member", "gx"), None),
        P(("member", "gx"), None),
        P(("member", "gx")),
        *[P()] * 12,
    )
    return jax.shard_map(
        shards,
        mesh=mesh,
        in_specs=placed,
        out_specs=(P(("member", "gx"), None), P(None, ("member", "gx"), None)),
        check_vma=False,
    )
```

```python
import functools
import jax
import jax.numpy as jnp
from jax import lax
from jax.experimental import pallas as pl
from jax.experimental.pallas import tpu as pltpu
from jax.sharding import PartitionSpec as P

F32, BF16, F8 = jnp.float32, jnp.bfloat16, jnp.float8_e4m3fn
LANES = 128
CHUNK = 512
HALO = 6
GROUP = 32
WEIGHT_MAX = (0.25, 0.3125, 0.3125, 0.375, 0.3125, 0.3125)
BIAS_MAX = 3.0
INPUT_MAX = 6.0
SILU_DIP = 0.28
TOP = 440.0
INPUT_SCALE = 72.0
MIXED = (0, 1, 3, 4)
WEIGHT_STEP = 2.0**10
LOW_STEP = 2.0**8
NETWORK_VMEM = 60_000_000
ADVECT_VMEM = 54_000_000
ROOM = 128


def round_up(value, unit):
    return -(-value // unit) * unit


def network_kernel(*refs, sizes, levels, axis):
    small_hbm, x_hbm, weights_hbm, refs = refs[:10], refs[10], refs[11:17], refs[17:]
    (tend_hbm, field_hbm, pay_a, pay_b), refs = refs[:4], refs[4:]
    x_in, weights_in, refs = refs[0], refs[1:7], refs[7:]
    cats, cats8, columns, refs = refs[:6], refs[6:12], refs[12:18], refs[18:]
    inverse, tracer, along, across, *biases = refs[:10]
    holds, holds8, refs = refs[10:12], refs[12:14], refs[14:]
    w_tail, x_tail, b_six, tend, peaks, shrinks, field, *sems = refs
    x_sems, w_sems, out_sems, small_sems, field_sems = sems

    chunks = x_hbm.shape[1] // CHUNK
    rows, levels_wide = field.shape[0], field.shape[1]
    depth_in = sizes[0]
    aligned = depth_in // 8 * 8
    whole = depth_in // LANES * LANES
    padded = [round_up(sizes[layer], LANES) for layer in range(6)]

    def x_copy(c):
        part = pl.ds(c * CHUNK, CHUNK)
        return pltpu.make_async_copy(x_hbm.at[:, part], x_in.at[:, part], x_sems.at[c])

    def w_copy(layer):
        target = weights_in[layer]
        if layer == 5:
            target = target.at[pl.ds(0, sizes[6])]
        return pltpu.make_async_copy(weights_hbm[layer], target, w_sems.at[layer])

    def small_copy(i):
        target = (inverse, tracer, along, across, *biases)[i]
        return pltpu.make_async_copy(small_hbm[i], target, small_sems.at[i])

    def out_copy(c):
        part = pl.ds(c * CHUNK, CHUNK)
        return pltpu.make_async_copy(
            tend.at[:, part], tend_hbm.at[:, part], out_sems.at[c]
        )

    def bias_columns(layer):
        count = sizes[layer + 1]
        source = biases[layer]
        if count % LANES:
            b_six[0:1, :] = jnp.zeros((1, b_six.shape[1]), F32)
            b_six[0:1, 0:count] = source[...].reshape(1, count)
            row = b_six[0:1, :]
        else:
            row = source[...].reshape(1, count)
        scale = 0.5 if layer < 5 else 1.0
        for n in range(0, count, LANES):
            block = jnp.broadcast_to(row[:, n : n + LANES], (LANES, LANES)).T * scale
            columns[layer][n : n + LANES, :] = block

    def put_weights(layer, lines, k, block):
        depth = padded[layer]
        if layer < 5:
            block = block * 0.5
        high = block.astype(BF16)
        low = block - high.astype(F32)
        cats[layer][lines, k : k + LANES] = high
        if layer not in MIXED:
            cats[layer][lines, depth + k : depth + k + LANES] = high
            cats[layer][lines, 2 * depth + k : 2 * depth + k + LANES] = low.astype(BF16)
            return
        step = WEIGHT_STEP * (2.0 if layer < 5 else 1.0)
        lanes, far = slice(k, k + LANES), slice(depth + k, depth + k + LANES)
        cats8[layer][lines, lanes] = (high * BF16(step)).astype(F8)
        cats8[layer][lines, far] = (low * (step * LOW_STEP)).astype(F8)

    def prepare(layer, part, parts):
        work = [
            (n, k)
            for n in range(0, round_up(sizes[layer + 1], LANES), LANES)
            for k in range(0, padded[layer], LANES)
        ]
        for n, k in work[part * len(work) // parts : (part + 1) * len(work) // parts]:
            lines, lanes = slice(n, n + LANES), slice(k, k + LANES)
            if layer == 5:
                block = weights_in[5][lines, lanes]
            elif layer == 0 and k >= whole:
                block = w_tail[:, lines].T
            else:
                block = weights_in[layer][lanes, lines].T
            put_weights(layer, lines, k, block)

    def put_rows(layer, start, cols, value, scale):
        depth = padded[layer]
        high = value.astype(BF16)
        low = value - high.astype(F32)
        size = value.shape[0]
        hold, hold8 = holds[layer % 2], holds8[layer % 2]
        near = slice(start, start + size)
        middle = slice(depth + start, depth + start + size)
        hold[near, cols] = high
        if layer not in MIXED:
            hold[middle, cols] = low.astype(BF16)
            hold[2 * depth + start : 2 * depth + start + size, cols] = high
            return
        hold8[near, cols] = (low * (scale * LOW_STEP)).astype(F8)
        hold8[middle, cols] = (high * scale.astype(BF16)).astype(F8)

    first_scale = jnp.full((1, CHUNK), INPUT_SCALE, F32)

    def prepare_inputs(c):
        cols = slice(c * CHUNK, (c + 1) * CHUNK)
        x_tail[0 : aligned - whole, cols] = x_in[whole:aligned, cols]
        x_tail[aligned - whole : depth_in - whole, cols] = x_in[aligned:depth_in, cols]
        for k in range(0, whole, LANES):
            put_rows(0, k, cols, x_in[k : k + LANES, cols], first_scale)
        put_rows(0, whole, cols, x_tail[:, cols], first_scale)

    odd = lax.rem(lax.axis_index(axis), 2)
    leaving = [
        pltpu.make_async_copy(
            field.at[pl.ds((rows - HALO) * odd, HALO)], pay_a, field_sems.at[0]
        ),
        pltpu.make_async_copy(
            field.at[pl.ds((rows - HALO) * (1 - odd), HALO)], pay_b, field_sems.at[1]
        ),
        pltpu.make_async_copy(field, field_hbm.at[pl.ds(0, rows)], field_sems.at[2]),
    ]

    def main_product(layer, c):
        cols = slice(c * CHUNK, (c + 1) * CHUNK)
        return jnp.dot(
            cats[layer][...],
            holds[layer % 2][0 : cats[layer].shape[1], cols],
            preferred_element_type=F32,
        )

    def rest_product(layer, c):
        if layer not in MIXED:
            return None
        cols = slice(c * CHUNK, (c + 1) * CHUNK)
        return jnp.dot(
            cats8[layer][...],
            holds8[layer % 2][0 : 2 * padded[layer], cols],
            preferred_element_type=F32,
        )

    def finish(layer, c, main, rest):
        cols = slice(c * CHUNK, (c + 1) * CHUNK)
        unit = 1.0 / (WEIGHT_STEP * LOW_STEP * (2.0 if layer < 5 else 1.0))
        value = main
        if layer in MIXED:
            shrink = shrinks[layer : layer + 1, cols] if layer else 1.0 / first_scale
            value = value + rest * (shrink * unit)
        peak = peaks[layer : layer + 1, cols] if layer else INPUT_MAX
        bias = columns[layer][...]
        value = value + jnp.concatenate([bias] * (CHUNK // LANES), axis=1)
        if layer < 5:
            value = value + value * jnp.tanh(value)
            limit = (sizes[layer] * WEIGHT_MAX[layer]) * peak + BIAS_MAX
            limit = jnp.broadcast_to(jnp.asarray(limit, F32), (1, CHUNK))
            scale = (TOP / limit).astype(BF16).astype(F32)
            put_rows(layer + 1, 0, cols, value, scale)
            if layer + 1 in MIXED:
                shrinks[layer + 1 : layer + 2, cols] = 1.0 / scale
            if layer + 2 in MIXED:
                highest = jnp.max(value, axis=0, keepdims=True)
                peaks[layer + 1 : layer + 2, cols] = jnp.maximum(highest, SILU_DIP)
            return
        for first, stop in ((0, levels_wide), (levels_wide, sizes[6])):
            for part in range(CHUNK // LANES):
                r = c * (CHUNK // LANES) + part
                day = inverse[r : r + 1, :] >= 0
                lanes = slice(part * LANES, (part + 1) * LANES)
                shown = jnp.where(day, value[first:stop, lanes], 0.0)
                tend[first:stop, r * LANES : (r + 1) * LANES] = shown
                if first == 0:
                    field[r, 0:levels, :] = (
                        tracer[pl.ds(r, levels, stride=rows), :] + shown[0:levels]
                    )
            if first == 0 and c == chunks - 1:
                for copy in leaving:
                    copy.start()
        out_copy(c).start()

    w_copy(0).start()
    for c in range(chunks):
        x_copy(c).start()
    for i in range(10):
        small_copy(i).start()
    w_copy(1).start()
    w_tail[...] = jnp.zeros(w_tail.shape, F32)
    x_tail[...] = jnp.zeros(x_tail.shape, F32)
    weights_in[5][sizes[6] :, :] = jnp.zeros(
        (weights_in[5].shape[0] - sizes[6], sizes[5]), F32
    )
    w_copy(0).wait()
    w_tail[0 : aligned - whole, :] = weights_in[0][whole:aligned, :]
    w_tail[aligned - whole : depth_in - whole, :] = weights_in[0][aligned:depth_in, :]
    prepare(0, 0, 1)
    for layer in range(2, 6):
        w_copy(layer).start()
    x_copy(0).wait()
    prepare_inputs(0)

    for layer in range(6):
        if 0 < layer < 5:
            w_copy(layer + 1).wait()
        for c in range(chunks):
            main = main_product(layer, c)
            if layer == 0 and c == 0:
                for i in range(10):
                    small_copy(i).wait()
                bias_columns(0)
                for i in range(1, chunks):
                    x_copy(i).wait()
                    prepare_inputs(i)
                w_copy(1).wait()
            if layer < 5:
                prepare(layer + 1, c, chunks)
            rest = rest_product(layer, c)
            if layer == 4 and c == 0:
                for r in range(rows):
                    field[r, levels : levels + 1, :] = along[r : r + 1, :]
                    field[r, levels + 1 : levels + 2, :] = across[r : r + 1, :]
                    field[r, levels + 2 : levels_wide, :] = jnp.zeros(
                        (levels_wide - levels - 2, LANES), F32
                    )
            if layer < 5 and c == chunks - 1:
                bias_columns(layer + 1)
            finish(layer, c, main, rest)

    for copy in leaving:
        copy.wait()
    for c in range(chunks):
        out_copy(c).wait()


def network(inverse, tracer, along, across, biases, x, weights, axis):
    sizes = [x.shape[0]] + [b.shape[0] for b in biases]
    width = x.shape[1]
    rows = along.shape[0]
    levels = tracer.shape[0] // rows
    levels_wide = round_up(levels + 2, 8)
    chunks = width // CHUNK
    padded = [round_up(s, LANES) for s in sizes]
    deepest = max(padded[:6])
    tail = padded[0] - sizes[0] // LANES * LANES
    hbm = pl.BlockSpec(memory_space=pl.ANY)
    total = sum(sizes[i] * sizes[i + 1] for i in range(6)) * width
    return pl.pallas_call(
        functools.partial(network_kernel, sizes=sizes, levels=levels, axis=axis),
        out_shape=(
            jax.ShapeDtypeStruct((sizes[6], width), F32),
            jax.ShapeDtypeStruct((ROOM, levels_wide, LANES), F32),
            jax.ShapeDtypeStruct((HALO, levels_wide, LANES), F32),
            jax.ShapeDtypeStruct((HALO, levels_wide, LANES), F32),
        ),
        in_specs=[hbm] * 17,
        out_specs=(hbm,) * 4,
        scratch_shapes=[
            pltpu.VMEM(x.shape, F32),
            *[pltpu.VMEM(w.shape, F32) for w in weights[:5]],
            pltpu.VMEM((padded[6], sizes[5]), F32),
            *[
                pltpu.VMEM((padded[i + 1], padded[i] * (1 if i in MIXED else 3)), BF16)
                for i in range(6)
            ],
            *[pltpu.VMEM((padded[i + 1], 2 * padded[i]), F8) for i in range(6)],
            *[pltpu.VMEM((padded[i + 1], LANES), F32) for i in range(6)],
            pltpu.VMEM(inverse.shape, jnp.int32),
            pltpu.VMEM(tracer.shape, F32),
            pltpu.VMEM(along.shape, F32),
            pltpu.VMEM(across.shape, F32),
            *[pltpu.VMEM(b.shape, F32) for b in biases],
            *[pltpu.VMEM((3 * deepest, width), BF16)] * 2,
            *[pltpu.VMEM((2 * deepest, width), F8)] * 2,
            pltpu.VMEM((tail, sizes[1]), F32),
            pltpu.VMEM((tail, width), F32),
            pltpu.VMEM((8, padded[6]), F32),
            pltpu.VMEM((sizes[6], width), F32),
            pltpu.VMEM((8, width), F32),
            pltpu.VMEM((8, width), F32),
            pltpu.VMEM((rows, levels_wide, LANES), F32),
            pltpu.SemaphoreType.DMA((chunks,)),
            pltpu.SemaphoreType.DMA((6,)),
            pltpu.SemaphoreType.DMA((chunks,)),
            pltpu.SemaphoreType.DMA((10,)),
            pltpu.SemaphoreType.DMA((3,)),
        ],
        compiler_params=pltpu.CompilerParams(vmem_limit_bytes=NETWORK_VMEM),
        cost_estimate=pl.CostEstimate(
            flops=4 * total, bytes_accessed=14_000_000, transcendentals=3_000_000
        ),
        name="column_network",
    )(inverse, tracer, along, across, *biases, x, *weights)


def minmod(first, second):
    high, low = jnp.maximum(second, 0.0), jnp.minimum(second, 0.0)
    return jnp.maximum(jnp.minimum(first, high), low)


def cat(values):
    return values[0] if len(values) == 1 else jnp.concatenate(values, axis=0)


def advect_kernel(
    field, got_a, got_b, out, wide, speeds, held, out_sems, *, levels, axis
):
    rows = field.shape[0]
    odd = lax.rem(lax.axis_index(axis), 2)
    wide[HALO : HALO + rows] = field[...]
    wide[pl.ds((HALO + rows) * odd, HALO)] = got_a[...]
    wide[pl.ds((HALO + rows) * (1 - odd), HALO)] = got_b[...]

    def place(i):
        for kind in range(2):
            courant = jnp.broadcast_to(
                wide[i, levels + kind : levels + kind + 1, :], (8, LANES)
            )
            speeds[2 * kind, i] = jnp.maximum(courant, 0.0)
            speeds[2 * kind + 1, i] = jnp.minimum(courant, 0.0)

    for i in range(rows + 2 * HALO):
        place(i)
    groups = wide.shape[1] // GROUP
    span = GROUP * rows

    def leaving(g, start, size):
        return pltpu.make_async_copy(
            held.at[pl.ds(start, size)], out.at[pl.ds(start, size)], out_sems.at[g]
        )

    last = out.shape[0] - (groups - 1) * span

    def group(g, carry):
        wavefront(g, groups, levels, held, wide, speeds, rows)

        @pl.when(g < groups - 1)
        def _():
            leaving(g, pl.multiple_of(g * span, span), span).start()

        return carry

    lax.fori_loop(0, groups, group, 0)
    leaving(groups - 1, (groups - 1) * span, last).start()
    for g in range(groups - 1):
        leaving(g, g * span, span).wait()
    leaving(groups - 1, (groups - 1) * span, last).wait()


def wavefront(g, groups, levels, out, wide, speeds, rows):
    base = pl.multiple_of(g * GROUP, GROUP)
    blocks = GROUP // 8
    keep = levels - (groups - 1) * GROUP
    fields, halves = [{}, {}, {}], [{}, {}, {}]
    steps, slopes, fluxes = [{}, {}, {}], [{}, {}, {}], [{}, {}, {}]
    reach = [(-4, rows + 3), (-2, rows + 1), (0, rows - 1)]
    shape = (blocks, 8, LANES)

    def load(i):
        return wide[i + HALO, pl.ds(base, GROUP), :].reshape(shape)

    def courant(kind, at):
        return cat([jnp.broadcast_to(speeds[kind, i + HALO], shape) for i in at])

    def pieces(value, count):
        return [value[n * blocks : (n + 1) * blocks] for n in range(count)]

    def face(active, at):
        ahead, behind = courant(0, at), courant(1, at)
        upper = cat([fields[k][i] - slopes[k][i] for k, i in zip(active, at)])
        lower = cat([fields[k][i - 1] + slopes[k][i - 1] for k, i in zip(active, at)])
        return ahead * lower + behind * upper

    rest = []
    def put(k, i, value):
        fields[k][i], halves[k][i] = value, 0.5 * value

    for i in range(-HALO, -2):
        put(0, i, load(i))
    for t in range(-4, rows + 6):
        active = [k for k in range(3) if reach[k][0] <= t - 3 * k <= reach[k][1]]
        if t + 2 < rows + HALO:
            put(0, t + 2, load(t + 2))
        for k in active:
            c = t - 3 * k
            if c == reach[k][0]:
                for i in (c - 1, c, c + 1):
                    steps[k][i] = halves[k][i] - halves[k][i - 1]
                for i in (c - 1, c):
                    slopes[k][i] = minmod(steps[k][i + 1], steps[k][i])
                fluxes[k][c] = face([k], [c])
        at = [t - 3 * k for k in active]
        here = cat([fields[k][i] for k, i in zip(active, at)])
        half = cat([halves[k][i] for k, i in zip(active, at)])
        back = half - pltpu.roll(half, 1, 2)
        new = cat(
            [halves[k][i + 2] - halves[k][i + 1] for k, i in zip(active, at)]
        )
        last = cat([steps[k][i + 1] for k, i in zip(active, at)])
        bend = minmod(pltpu.roll(back, LANES - 1, 2), back)
        slope = minmod(new, last)
        for k, i, a_step, a_slope in zip(
            active, at, pieces(new, len(at)), pieces(slope, len(at))
        ):
            steps[k][i + 2], slopes[k][i + 1] = a_step, a_slope
        side = courant(2, at) * pltpu.roll(here + bend, 1, 2)
        side = side + courant(3, at) * (here - bend)
        flux = face(active, [i + 1 for i in at])
        for k, i, a_flux in zip(active, at, pieces(flux, len(at))):
            fluxes[k][i + 1] = a_flux
        moved = cat([fluxes[k][i] for k, i in zip(active, at)]) - flux
        moved = here + (moved + (side - pltpu.roll(side, LANES - 1, 2)))
        for k, i, value in zip(active, at, pieces(moved, len(at))):
            if k == 0:
                put(1, i, value)
            elif k == 1:
                put(2, i, 0.75 * fields[0][i] + 0.25 * value)
            else:
                value = 1.0 / 3.0 * fields[0][i] + 2.0 / 3.0 * value
                value = value.reshape(GROUP, LANES)
                out[pl.ds(base * rows + i, keep, stride=rows), :] = value[:keep]
                rest.append((i, value[keep:]))
    if keep < GROUP:

        @pl.when(g < groups - 1)
        def _():
            for i, value in rest:
                lines = pl.ds((base + keep) * rows + i, GROUP - keep, stride=rows)
                out[lines, :] = value


def stage_kernel(field, own, sem):
    copy = pltpu.make_async_copy(field.at[pl.ds(0, own.shape[0])], own, sem)
    copy.start()
    copy.wait()


def stage(field, rows):
    return pl.pallas_call(
        stage_kernel,
        out_shape=jax.ShapeDtypeStruct((rows, *field.shape[1:]), F32),
        in_specs=[pl.BlockSpec(memory_space=pl.ANY)],
        out_specs=pl.BlockSpec(memory_space=pltpu.VMEM),
        scratch_shapes=[pltpu.SemaphoreType.DMA],
        compiler_params=pltpu.CompilerParams(vmem_limit_bytes=ADVECT_VMEM),
        cost_estimate=pl.CostEstimate(
            flops=0, bytes_accessed=4_000_000, transcendentals=0
        ),
        name="stage_rows",
    )(field)


def advect(field, got_a, got_b, levels, axis):
    rows, levels_wide, across = field.shape
    vmem, hbm = pl.BlockSpec(memory_space=pltpu.VMEM), pl.BlockSpec(memory_space=pl.ANY)
    return pl.pallas_call(
        functools.partial(advect_kernel, levels=levels, axis=axis),
        out_shape=jax.ShapeDtypeStruct((levels * rows, across), F32),
        in_specs=[vmem] * 3,
        out_specs=hbm,
        scratch_shapes=[
            pltpu.VMEM((rows + 2 * HALO, levels_wide, across), F32),
            pltpu.VMEM((4, rows + 2 * HALO, 8, across), F32),
            pltpu.VMEM((levels * rows, across), F32),
            pltpu.SemaphoreType.DMA((levels_wide // GROUP,)),
        ],
        compiler_params=pltpu.CompilerParams(vmem_limit_bytes=ADVECT_VMEM),
        name="advect_sections",
    )(field, got_a, got_b)


def shards(inputs, tracer, speed_along, speed_across, inverse_list, *params):
    weights, biases = list(params[0::2]), params[1::2]
    weights[5] = weights[5].T
    levels, rows, across = tracer.shape
    tendencies, field, pay_a, pay_b = network(
        inverse_list.reshape(rows, across),
        tracer.reshape(levels * rows, across),
        speed_along,
        speed_across,
        biases,
        inputs.T,
        weights,
        "gx",
    )
    count = lax.axis_size("gx")
    outer = [(i, (i - 1 if i % 2 == 0 else i + 1) % count) for i in range(count)]
    inner = [(i, i + 1 if i % 2 == 0 else i - 1) for i in range(count)]
    got_a = lax.ppermute(pay_a, "gx", outer)
    got_b = lax.ppermute(pay_b, "gx", inner)
    advected = advect(stage(field, rows), got_a, got_b, levels, "gx")
    return tendencies.T, advected.reshape(levels, rows, across)


def solution(mesh):
    placed = (
        P(("member", "gx"), None),
        P(None, ("member", "gx"), None),
        P(("member", "gx"), None),
        P(("member", "gx"), None),
        P(("member", "gx")),
        *[P()] * 12,
    )
    return jax.shard_map(
        shards,
        mesh=mesh,
        in_specs=placed,
        out_specs=(P(("member", "gx"), None), P(None, ("member", "gx"), None)),
        check_vma=False,
    )
```

```python
import functools
import jax
import jax.numpy as jnp
from jax import lax
from jax.experimental import pallas as pl
from jax.experimental.pallas import tpu as pltpu
from jax.sharding import PartitionSpec as P

F32, BF16, F8 = jnp.float32, jnp.bfloat16, jnp.float8_e4m3fn
LANES = 128
CHUNK = 512
HALO = 6
GROUP = 32
WEIGHT_MAX = (0.25, 0.3125, 0.3125, 0.375, 0.3125, 0.3125)
BIAS_MAX = 3.0
INPUT_MAX = 6.0
SILU_DIP = 0.28
TOP = 440.0
INPUT_SCALE = 72.0
MIXED = (0, 1, 3, 4)
WEIGHT_STEP = 2.0**10
LOW_STEP = 2.0**8
NETWORK_VMEM = 60_000_000
ADVECT_VMEM = 54_000_000
ROOM = 128


def round_up(value, unit):
    return -(-value // unit) * unit


def network_kernel(*refs, sizes, levels, axis):
    small_hbm, x_hbm, weights_hbm, refs = refs[:10], refs[10], refs[11:17], refs[17:]
    (tend_hbm, field_hbm, pay_a, pay_b), refs = refs[:4], refs[4:]
    x_in, weights_in, refs = refs[0], refs[1:7], refs[7:]
    cats, cats8, columns, refs = refs[:6], refs[6:12], refs[12:18], refs[18:]
    inverse, tracer, along, across, *biases = refs[:10]
    holds, holds8, refs = refs[10:12], refs[12:14], refs[14:]
    w_tail, x_tail, b_six, tend, peaks, shrinks, field, *sems = refs
    x_sems, w_sems, out_sems, small_sems, field_sems = sems

    chunks = x_hbm.shape[1] // CHUNK
    rows, levels_wide = field.shape[0], field.shape[1]
    depth_in = sizes[0]
    aligned = depth_in // 8 * 8
    whole = depth_in // LANES * LANES
    padded = [round_up(sizes[layer], LANES) for layer in range(6)]

    def x_copy(c):
        part = pl.ds(c * CHUNK, CHUNK)
        return pltpu.make_async_copy(x_hbm.at[:, part], x_in.at[:, part], x_sems.at[c])

    def w_copy(layer):
        target = weights_in[layer]
        if layer == 5:
            target = target.at[pl.ds(0, sizes[6])]
        return pltpu.make_async_copy(weights_hbm[layer], target, w_sems.at[layer])

    def small_copy(i):
        target = (inverse, tracer, along, across, *biases)[i]
        return pltpu.make_async_copy(small_hbm[i], target, small_sems.at[i])

    def out_copy(c):
        part = pl.ds(c * CHUNK, CHUNK)
        return pltpu.make_async_copy(
            tend.at[:, part], tend_hbm.at[:, part], out_sems.at[c]
        )

    def bias_columns(layer):
        count = sizes[layer + 1]
        source = biases[layer]
        if count % LANES:
            b_six[0:1, :] = jnp.zeros((1, b_six.shape[1]), F32)
            b_six[0:1, 0:count] = source[...].reshape(1, count)
            row = b_six[0:1, :]
        else:
            row = source[...].reshape(1, count)
        scale = 0.5 if layer < 5 else 1.0
        for n in range(0, count, LANES):
            block = jnp.broadcast_to(row[:, n : n + LANES], (LANES, LANES)).T * scale
            columns[layer][n : n + LANES, :] = block

    def put_weights(layer, lines, k, block):
        depth = padded[layer]
        if layer < 5:
            block = block * 0.5
        high = block.astype(BF16)
        low = block - high.astype(F32)
        cats[layer][lines, k : k + LANES] = high
        if layer not in MIXED:
            cats[layer][lines, depth + k : depth + k + LANES] = high
            cats[layer][lines, 2 * depth + k : 2 * depth + k + LANES] = low.astype(BF16)
            return
        step = WEIGHT_STEP * (2.0 if layer < 5 else 1.0)
        lanes, far = slice(k, k + LANES), slice(depth + k, depth + k + LANES)
        cats8[layer][lines, lanes] = (high * BF16(step)).astype(F8)
        cats8[layer][lines, far] = (low * (step * LOW_STEP)).astype(F8)

    def prepare(layer, part, parts):
        work = [
            (n, k)
            for n in range(0, round_up(sizes[layer + 1], LANES), LANES)
            for k in range(0, padded[layer], LANES)
        ]
        for n, k in work[part * len(work) // parts : (part + 1) * len(work) // parts]:
            lines, lanes = slice(n, n + LANES), slice(k, k + LANES)
            if layer == 5:
                block = weights_in[5][lines, lanes]
            elif layer == 0 and k >= whole:
                block = w_tail[:, lines].T
            else:
                block = weights_in[layer][lanes, lines].T
            put_weights(layer, lines, k, block)

    def put_rows(layer, start, cols, value, scale):
        depth = padded[layer]
        high = value.astype(BF16)
        low = value - high.astype(F32)
        size = value.shape[0]
        hold, hold8 = holds[layer % 2], holds8[layer % 2]
        near = slice(start, start + size)
        middle = slice(depth + start, depth + start + size)
        hold[near, cols] = high
        if layer not in MIXED:
            hold[middle, cols] = low.astype(BF16)
            hold[2 * depth + start : 2 * depth + start + size, cols] = high
            return
        hold8[near, cols] = (low * (scale * LOW_STEP)).astype(F8)
        hold8[middle, cols] = (high * scale.astype(BF16)).astype(F8)

    first_scale = jnp.full((1, CHUNK), INPUT_SCALE, F32)

    def prepare_inputs(c):
        cols = slice(c * CHUNK, (c + 1) * CHUNK)
        x_tail[0 : aligned - whole, cols] = x_in[whole:aligned, cols]
        x_tail[aligned - whole : depth_in - whole, cols] = x_in[aligned:depth_in, cols]
        for k in range(0, whole, LANES):
            put_rows(0, k, cols, x_in[k : k + LANES, cols], first_scale)
        put_rows(0, whole, cols, x_tail[:, cols], first_scale)

    def main_product(layer, c):
        cols = slice(c * CHUNK, (c + 1) * CHUNK)
        return jnp.dot(
            cats[layer][...],
            holds[layer % 2][0 : cats[layer].shape[1], cols],
            preferred_element_type=F32,
        )

    def rest_product(layer, c):
        if layer not in MIXED:
            return None
        cols = slice(c * CHUNK, (c + 1) * CHUNK)
        return jnp.dot(
            cats8[layer][...],
            holds8[layer % 2][0 : 2 * padded[layer], cols],
            preferred_element_type=F32,
        )

    def finish(layer, c, main, rest):
        cols = slice(c * CHUNK, (c + 1) * CHUNK)
        unit = 1.0 / (WEIGHT_STEP * LOW_STEP * (2.0 if layer < 5 else 1.0))
        value = main
        if layer in MIXED:
            shrink = shrinks[layer : layer + 1, cols] if layer else 1.0 / first_scale
            value = value + rest * (shrink * unit)
        peak = peaks[layer : layer + 1, cols] if layer else INPUT_MAX
        bias = columns[layer][...]
        value = value + jnp.concatenate([bias] * (CHUNK // LANES), axis=1)
        if layer < 5:
            value = value + value * jnp.tanh(value)
            limit = (sizes[layer] * WEIGHT_MAX[layer]) * peak + BIAS_MAX
            limit = jnp.broadcast_to(jnp.asarray(limit, F32), (1, CHUNK))
            scale = (TOP / limit).astype(BF16).astype(F32)
            put_rows(layer + 1, 0, cols, value, scale)
            if layer + 1 in MIXED:
                shrinks[layer + 1 : layer + 2, cols] = 1.0 / scale
            if layer + 2 in MIXED:
                highest = jnp.max(value, axis=0, keepdims=True)
                peaks[layer + 1 : layer + 2, cols] = jnp.maximum(highest, SILU_DIP)
            return
        for part in range(CHUNK // LANES):
            r = c * (CHUNK // LANES) + part
            day = inverse[r : r + 1, :] >= 0
            shown = jnp.where(
                day, value[: sizes[6], part * LANES : (part + 1) * LANES], 0.0
            )
            tend[:, r * LANES : (r + 1) * LANES] = shown
            field[r, 0:levels, :] = (
                tracer[pl.ds(r, levels, stride=rows), :] + shown[0:levels]
            )
        out_copy(c).start()

    w_copy(0).start()
    for c in range(chunks):
        x_copy(c).start()
    for i in range(10):
        small_copy(i).start()
    w_copy(1).start()
    w_tail[...] = jnp.zeros(w_tail.shape, F32)
    x_tail[...] = jnp.zeros(x_tail.shape, F32)
    weights_in[5][sizes[6] :, :] = jnp.zeros(
        (weights_in[5].shape[0] - sizes[6], sizes[5]), F32
    )
    w_copy(0).wait()
    w_tail[0 : aligned - whole, :] = weights_in[0][whole:aligned, :]
    w_tail[aligned - whole : depth_in - whole, :] = weights_in[0][aligned:depth_in, :]
    prepare(0, 0, 1)
    for layer in range(2, 6):
        w_copy(layer).start()
    x_copy(0).wait()
    prepare_inputs(0)

    for layer in range(6):
        if 0 < layer < 5:
            w_copy(layer + 1).wait()
        for c in range(chunks):
            main = main_product(layer, c)
            if layer == 0 and c == 0:
                for i in range(10):
                    small_copy(i).wait()
                bias_columns(0)
                for i in range(1, chunks):
                    x_copy(i).wait()
                    prepare_inputs(i)
                w_copy(1).wait()
            if layer < 5:
                prepare(layer + 1, c, chunks)
            rest = rest_product(layer, c)
            if layer == 4 and c == 0:
                for r in range(rows):
                    field[r, levels : levels + 1, :] = along[r : r + 1, :]
                    field[r, levels + 1 : levels + 2, :] = across[r : r + 1, :]
                    field[r, levels + 2 : levels_wide, :] = jnp.zeros(
                        (levels_wide - levels - 2, LANES), F32
                    )
            if layer < 5 and c == chunks - 1:
                bias_columns(layer + 1)
            finish(layer, c, main, rest)

    odd = lax.rem(lax.axis_index(axis), 2)
    leaving = [
        pltpu.make_async_copy(
            field.at[pl.ds((rows - HALO) * odd, HALO)], pay_a, field_sems.at[0]
        ),
        pltpu.make_async_copy(
            field.at[pl.ds((rows - HALO) * (1 - odd), HALO)], pay_b, field_sems.at[1]
        ),
        pltpu.make_async_copy(field, field_hbm.at[pl.ds(0, rows)], field_sems.at[2]),
    ]
    for copy in leaving:
        copy.start()
    for copy in leaving:
        copy.wait()
    for c in range(chunks):
        out_copy(c).wait()


def network(inverse, tracer, along, across, biases, x, weights, axis):
    sizes = [x.shape[0]] + [b.shape[0] for b in biases]
    width = x.shape[1]
    rows = along.shape[0]
    levels = tracer.shape[0] // rows
    levels_wide = round_up(levels + 2, 8)
    chunks = width // CHUNK
    padded = [round_up(s, LANES) for s in sizes]
    deepest = max(padded[:6])
    tail = padded[0] - sizes[0] // LANES * LANES
    hbm = pl.BlockSpec(memory_space=pl.ANY)
    total = sum(sizes[i] * sizes[i + 1] for i in range(6)) * width
    return pl.pallas_call(
        functools.partial(network_kernel, sizes=sizes, levels=levels, axis=axis),
        out_shape=(
            jax.ShapeDtypeStruct((sizes[6], width), F32),
            jax.ShapeDtypeStruct((ROOM, levels_wide, LANES), F32),
            jax.ShapeDtypeStruct((HALO, levels_wide, LANES), F32),
            jax.ShapeDtypeStruct((HALO, levels_wide, LANES), F32),
        ),
        in_specs=[hbm] * 17,
        out_specs=(hbm,) * 4,
        scratch_shapes=[
            pltpu.VMEM(x.shape, F32),
            *[pltpu.VMEM(w.shape, F32) for w in weights[:5]],
            pltpu.VMEM((padded[6], sizes[5]), F32),
            *[
                pltpu.VMEM((padded[i + 1], padded[i] * (1 if i in MIXED else 3)), BF16)
                for i in range(6)
            ],
            *[pltpu.VMEM((padded[i + 1], 2 * padded[i]), F8) for i in range(6)],
            *[pltpu.VMEM((padded[i + 1], LANES), F32) for i in range(6)],
            pltpu.VMEM(inverse.shape, jnp.int32),
            pltpu.VMEM(tracer.shape, F32),
            pltpu.VMEM(along.shape, F32),
            pltpu.VMEM(across.shape, F32),
            *[pltpu.VMEM(b.shape, F32) for b in biases],
            *[pltpu.VMEM((3 * deepest, width), BF16)] * 2,
            *[pltpu.VMEM((2 * deepest, width), F8)] * 2,
            pltpu.VMEM((tail, sizes[1]), F32),
            pltpu.VMEM((tail, width), F32),
            pltpu.VMEM((8, padded[6]), F32),
            pltpu.VMEM((sizes[6], width), F32),
            pltpu.VMEM((8, width), F32),
            pltpu.VMEM((8, width), F32),
            pltpu.VMEM((rows, levels_wide, LANES), F32),
            pltpu.SemaphoreType.DMA((chunks,)),
            pltpu.SemaphoreType.DMA((6,)),
            pltpu.SemaphoreType.DMA((chunks,)),
            pltpu.SemaphoreType.DMA((10,)),
            pltpu.SemaphoreType.DMA((3,)),
        ],
        compiler_params=pltpu.CompilerParams(vmem_limit_bytes=NETWORK_VMEM),
        cost_estimate=pl.CostEstimate(
            flops=4 * total, bytes_accessed=14_000_000, transcendentals=3_000_000
        ),
        name="column_network",
    )(inverse, tracer, along, across, *biases, x, *weights)


def minmod(first, second):
    high, low = jnp.maximum(second, 0.0), jnp.minimum(second, 0.0)
    return jnp.maximum(jnp.minimum(first, high), low)


def cat(values):
    return values[0] if len(values) == 1 else jnp.concatenate(values, axis=0)


def advect_kernel(
    field, got_a, got_b, out, wide, speeds, held, out_sems, *, levels, axis
):
    rows = field.shape[0]
    odd = lax.rem(lax.axis_index(axis), 2)
    wide[HALO : HALO + rows] = field[...]
    wide[pl.ds((HALO + rows) * odd, HALO)] = got_a[...]
    wide[pl.ds((HALO + rows) * (1 - odd), HALO)] = got_b[...]

    def place(i):
        for kind in range(2):
            courant = jnp.broadcast_to(
                wide[i, levels + kind : levels + kind + 1, :], (8, LANES)
            )
            speeds[2 * kind, i] = jnp.maximum(courant, 0.0)
            speeds[2 * kind + 1, i] = jnp.minimum(courant, 0.0)

    for i in range(rows + 2 * HALO):
        place(i)
    groups = wide.shape[1] // GROUP
    span = GROUP * rows

    def leaving(g, start, size):
        return pltpu.make_async_copy(
            held.at[pl.ds(start, size)], out.at[pl.ds(start, size)], out_sems.at[g]
        )

    last = out.shape[0] - (groups - 1) * span

    def group(g, carry):
        wavefront(g, groups, levels, held, wide, speeds, rows)

        @pl.when(g < groups - 1)
        def _():
            leaving(g, pl.multiple_of(g * span, span), span).start()

        return carry

    lax.fori_loop(0, groups, group, 0)
    leaving(groups - 1, (groups - 1) * span, last).start()
    for g in range(groups - 1):
        leaving(g, g * span, span).wait()
    leaving(groups - 1, (groups - 1) * span, last).wait()


def wavefront(g, groups, levels, out, wide, speeds, rows):
    base = pl.multiple_of(g * GROUP, GROUP)
    blocks = GROUP // 8
    keep = levels - (groups - 1) * GROUP
    fields, halves, sides = [{}, {}, {}], [{}, {}, {}], [{}, {}, {}]
    steps, slopes, fluxes = [{}, {}, {}], [{}, {}, {}], [{}, {}, {}]
    reach = [(-4, rows + 3), (-2, rows + 1), (0, rows - 1)]
    shape = (blocks, 8, LANES)

    def load(i):
        return wide[i + HALO, pl.ds(base, GROUP), :].reshape(shape)

    def courant(kind, at):
        return cat([jnp.broadcast_to(speeds[kind, i + HALO], shape) for i in at])

    def pieces(value, count):
        return [value[n * blocks : (n + 1) * blocks] for n in range(count)]

    def face(active, at):
        ahead, behind = courant(0, at), courant(1, at)
        upper = cat([fields[k][i] - slopes[k][i] for k, i in zip(active, at)])
        lower = cat([fields[k][i - 1] + slopes[k][i - 1] for k, i in zip(active, at)])
        return ahead * lower + behind * upper

    rest = []
    def put(k, i, value):
        fields[k][i], halves[k][i] = value, 0.5 * value

    def sideways(places):
        at = [i for _, i in places]
        here = cat([fields[k][i] for k, i in places])
        half = cat([halves[k][i] for k, i in places])
        back = half - pltpu.roll(half, 1, 2)
        bend = minmod(pltpu.roll(back, LANES - 1, 2), back)
        side = courant(2, at) * pltpu.roll(here + bend, 1, 2)
        side = side + courant(3, at) * (here - bend)
        side = side - pltpu.roll(side, LANES - 1, 2)
        for (k, i), value in zip(places, pieces(side, len(at))):
            sides[k][i] = value

    for i in range(-HALO, 0):
        put(0, i, load(i))
    for t in range(-4, rows + 8):
        active = [k for k in range(3) if reach[k][0] <= t - 4 * k <= reach[k][1]]
        if t + 4 < rows + HALO:
            put(0, t + 4, load(t + 4))
        fresh = [k for k in active if t - 4 * k == reach[k][0]]
        for k in fresh:
            c = reach[k][0]
            for i in (c - 1, c, c + 1):
                steps[k][i] = halves[k][i] - halves[k][i - 1]
            for i in (c - 1, c):
                slopes[k][i] = minmod(steps[k][i + 1], steps[k][i])
            fluxes[k][c] = face([k], [c])
        if fresh:
            sideways([(k, reach[k][0] + n) for k in fresh for n in (0, 1)])
        at = [t - 4 * k for k in active]
        here = cat([fields[k][i] for k, i in zip(active, at)])
        new = cat(
            [halves[k][i + 2] - halves[k][i + 1] for k, i in zip(active, at)]
        )
        last = cat([steps[k][i + 1] for k, i in zip(active, at)])
        slope = minmod(new, last)
        for k, i, a_step, a_slope in zip(
            active, at, pieces(new, len(at)), pieces(slope, len(at))
        ):
            steps[k][i + 2], slopes[k][i + 1] = a_step, a_slope
        flux = face(active, [i + 1 for i in at])
        for k, i, a_flux in zip(active, at, pieces(flux, len(at))):
            fluxes[k][i + 1] = a_flux
        moved = cat([fluxes[k][i] for k, i in zip(active, at)]) - flux
        moved = here + (moved + cat([sides[k][i] for k, i in zip(active, at)]))
        for k, i, value in zip(active, at, pieces(moved, len(at))):
            if k == 0:
                put(1, i, value)
            elif k == 1:
                put(2, i, 0.75 * fields[0][i] + 0.25 * value)
            else:
                value = 1.0 / 3.0 * fields[0][i] + 2.0 / 3.0 * value
                value = value.reshape(GROUP, LANES)
                out[pl.ds(base * rows + i, keep, stride=rows), :] = value[:keep]
                rest.append((i, value[keep:]))
        ahead = [
            (k, i + n)
            for k, i in zip(active, at)
            for n in (2, 3)
            if (i - reach[k][0]) % 2 == 0 and i + n <= reach[k][1]
        ]
        if ahead:
            sideways(ahead)
    if keep < GROUP:

        @pl.when(g < groups - 1)
        def _():
            for i, value in rest:
                lines = pl.ds((base + keep) * rows + i, GROUP - keep, stride=rows)
                out[lines, :] = value


def stage_kernel(field, own, sem):
    copy = pltpu.make_async_copy(field.at[pl.ds(0, own.shape[0])], own, sem)
    copy.start()
    copy.wait()


def stage(field, rows):
    return pl.pallas_call(
        stage_kernel,
        out_shape=jax.ShapeDtypeStruct((rows, *field.shape[1:]), F32),
        in_specs=[pl.BlockSpec(memory_space=pl.ANY)],
        out_specs=pl.BlockSpec(memory_space=pltpu.VMEM),
        scratch_shapes=[pltpu.SemaphoreType.DMA],
        compiler_params=pltpu.CompilerParams(vmem_limit_bytes=ADVECT_VMEM),
        cost_estimate=pl.CostEstimate(
            flops=0, bytes_accessed=4_000_000, transcendentals=0
        ),
        name="stage_rows",
    )(field)


def advect(field, got_a, got_b, levels, axis):
    rows, levels_wide, across = field.shape
    vmem, hbm = pl.BlockSpec(memory_space=pltpu.VMEM), pl.BlockSpec(memory_space=pl.ANY)
    return pl.pallas_call(
        functools.partial(advect_kernel, levels=levels, axis=axis),
        out_shape=jax.ShapeDtypeStruct((levels * rows, across), F32),
        in_specs=[vmem] * 3,
        out_specs=hbm,
        scratch_shapes=[
            pltpu.VMEM((rows + 2 * HALO, levels_wide, across), F32),
            pltpu.VMEM((4, rows + 2 * HALO, 8, across), F32),
            pltpu.VMEM((levels * rows, across), F32),
            pltpu.SemaphoreType.DMA((levels_wide // GROUP,)),
        ],
        compiler_params=pltpu.CompilerParams(vmem_limit_bytes=ADVECT_VMEM),
        name="advect_sections",
    )(field, got_a, got_b)


def shards(inputs, tracer, speed_along, speed_across, inverse_list, *params):
    weights, biases = list(params[0::2]), params[1::2]
    weights[5] = weights[5].T
    levels, rows, across = tracer.shape
    tendencies, field, pay_a, pay_b = network(
        inverse_list.reshape(rows, across),
        tracer.reshape(levels * rows, across),
        speed_along,
        speed_across,
        biases,
        inputs.T,
        weights,
        "gx",
    )
    count = lax.axis_size("gx")
    outer = [(i, (i - 1 if i % 2 == 0 else i + 1) % count) for i in range(count)]
    inner = [(i, i + 1 if i % 2 == 0 else i - 1) for i in range(count)]
    got_a = lax.ppermute(pay_a, "gx", outer)
    got_b = lax.ppermute(pay_b, "gx", inner)
    advected = advect(stage(field, rows), got_a, got_b, levels, "gx")
    return tendencies.T, advected.reshape(levels, rows, across)


def solution(mesh):
    placed = (
        P(("member", "gx"), None),
        P(None, ("member", "gx"), None),
        P(("member", "gx"), None),
        P(("member", "gx"), None),
        P(("member", "gx")),
        *[P()] * 12,
    )
    return jax.shard_map(
        shards,
        mesh=mesh,
        in_specs=placed,
        out_specs=(P(("member", "gx"), None), P(None, ("member", "gx"), None)),
        check_vma=False,
    )
```

```python
import functools
import jax
import jax.numpy as jnp
from jax import lax
from jax.experimental import pallas as pl
from jax.experimental.pallas import tpu as pltpu
from jax.sharding import PartitionSpec as P

F32, BF16, F8 = jnp.float32, jnp.bfloat16, jnp.float8_e4m3fn
LANES = 128
CHUNK = 512
HALO = 6
GROUP = 32
WEIGHT_MAX = (0.25, 0.3125, 0.3125, 0.375, 0.3125, 0.3125)
BIAS_MAX = 3.0
INPUT_MAX = 6.0
SILU_DIP = 0.28
TOP = 440.0
INPUT_SCALE = 72.0
MIXED = (0, 1, 2, 3, 4, 5)
WEIGHT_STEP = 2.0**10
LOW_STEP = 2.0**8
NETWORK_VMEM = 60_000_000
ADVECT_VMEM = 54_000_000
ROOM = 128


def round_up(value, unit):
    return -(-value // unit) * unit


def network_kernel(*refs, sizes, levels, axis):
    small_hbm, x_hbm, weights_hbm, refs = refs[:10], refs[10], refs[11:17], refs[17:]
    (tend_hbm, field_hbm, pay_a, pay_b), refs = refs[:4], refs[4:]
    x_in, weights_in, refs = refs[0], refs[1:7], refs[7:]
    cats, cats8, columns, refs = refs[:6], refs[6:12], refs[12:18], refs[18:]
    inverse, tracer, along, across, *biases = refs[:10]
    holds, holds8, refs = refs[10:12], refs[12:14], refs[14:]
    w_tail, x_tail, b_six, tend, peaks, shrinks, field, *sems = refs
    x_sems, w_sems, out_sems, small_sems, field_sems = sems

    chunks = x_hbm.shape[1] // CHUNK
    rows, levels_wide = field.shape[0], field.shape[1]
    depth_in = sizes[0]
    aligned = depth_in // 8 * 8
    whole = depth_in // LANES * LANES
    padded = [round_up(sizes[layer], LANES) for layer in range(6)]

    def x_copy(c):
        part = pl.ds(c * CHUNK, CHUNK)
        return pltpu.make_async_copy(x_hbm.at[:, part], x_in.at[:, part], x_sems.at[c])

    def w_copy(layer):
        target = weights_in[layer]
        if layer == 5:
            target = target.at[pl.ds(0, sizes[6])]
        return pltpu.make_async_copy(weights_hbm[layer], target, w_sems.at[layer])

    def small_copy(i):
        target = (inverse, tracer, along, across, *biases)[i]
        return pltpu.make_async_copy(small_hbm[i], target, small_sems.at[i])

    def out_copy(c):
        part = pl.ds(c * CHUNK, CHUNK)
        return pltpu.make_async_copy(
            tend.at[:, part], tend_hbm.at[:, part], out_sems.at[c]
        )

    def bias_columns(layer):
        count = sizes[layer + 1]
        source = biases[layer]
        if count % LANES:
            b_six[0:1, :] = jnp.zeros((1, b_six.shape[1]), F32)
            b_six[0:1, 0:count] = source[...].reshape(1, count)
            row = b_six[0:1, :]
        else:
            row = source[...].reshape(1, count)
        scale = 0.5 if layer < 5 else 1.0
        for n in range(0, count, LANES):
            block = jnp.broadcast_to(row[:, n : n + LANES], (LANES, LANES)).T * scale
            columns[layer][n : n + LANES, :] = block

    def put_weights(layer, lines, k, block):
        depth = padded[layer]
        if layer < 5:
            block = block * 0.5
        high = block.astype(BF16)
        low = block - high.astype(F32)
        cats[layer][lines, k : k + LANES] = high
        if layer not in MIXED:
            cats[layer][lines, depth + k : depth + k + LANES] = high
            cats[layer][lines, 2 * depth + k : 2 * depth + k + LANES] = low.astype(BF16)
            return
        step = WEIGHT_STEP * (2.0 if layer < 5 else 1.0)
        lanes, far = slice(k, k + LANES), slice(depth + k, depth + k + LANES)
        cats8[layer][lines, lanes] = (high * BF16(step)).astype(F8)
        cats8[layer][lines, far] = (low * (step * LOW_STEP)).astype(F8)

    def prepare(layer, part, parts):
        work = [
            (n, k)
            for n in range(0, round_up(sizes[layer + 1], LANES), LANES)
            for k in range(0, padded[layer], LANES)
        ]
        for n, k in work[part * len(work) // parts : (part + 1) * len(work) // parts]:
            lines, lanes = slice(n, n + LANES), slice(k, k + LANES)
            if layer == 5:
                block = weights_in[5][lines, lanes]
            elif layer == 0 and k >= whole:
                block = w_tail[:, lines].T
            else:
                block = weights_in[layer][lanes, lines].T
            put_weights(layer, lines, k, block)

    def put_rows(layer, start, cols, value, scale):
        depth = padded[layer]
        high = value.astype(BF16)
        low = value - high.astype(F32)
        size = value.shape[0]
        hold, hold8 = holds[layer % 2], holds8[layer % 2]
        near = slice(start, start + size)
        middle = slice(depth + start, depth + start + size)
        hold[near, cols] = high
        if layer not in MIXED:
            hold[middle, cols] = low.astype(BF16)
            hold[2 * depth + start : 2 * depth + start + size, cols] = high
            return
        hold8[near, cols] = (low * (scale * LOW_STEP)).astype(F8)
        hold8[middle, cols] = (high * scale.astype(BF16)).astype(F8)

    first_scale = jnp.full((1, CHUNK), INPUT_SCALE, F32)

    def prepare_inputs(c):
        cols = slice(c * CHUNK, (c + 1) * CHUNK)
        x_tail[0 : aligned - whole, cols] = x_in[whole:aligned, cols]
        x_tail[aligned - whole : depth_in - whole, cols] = x_in[aligned:depth_in, cols]
        for k in range(0, whole, LANES):
            put_rows(0, k, cols, x_in[k : k + LANES, cols], first_scale)
        put_rows(0, whole, cols, x_tail[:, cols], first_scale)

    def main_product(layer, c):
        cols = slice(c * CHUNK, (c + 1) * CHUNK)
        return jnp.dot(
            cats[layer][...],
            holds[layer % 2][0 : cats[layer].shape[1], cols],
            preferred_element_type=F32,
        )

    def rest_product(layer, c):
        if layer not in MIXED:
            return None
        cols = slice(c * CHUNK, (c + 1) * CHUNK)
        return jnp.dot(
            cats8[layer][...],
            holds8[layer % 2][0 : 2 * padded[layer], cols],
            preferred_element_type=F32,
        )

    def finish(layer, c, main, rest):
        cols = slice(c * CHUNK, (c + 1) * CHUNK)
        unit = 1.0 / (WEIGHT_STEP * LOW_STEP * (2.0 if layer < 5 else 1.0))
        value = main
        if layer in MIXED:
            shrink = shrinks[layer : layer + 1, cols] if layer else 1.0 / first_scale
            value = value + rest * (shrink * unit)
        peak = peaks[layer : layer + 1, cols] if layer else INPUT_MAX
        bias = columns[layer][...]
        value = value + jnp.concatenate([bias] * (CHUNK // LANES), axis=1)
        if layer < 5:
            value = value + value * jnp.tanh(value)
            limit = (sizes[layer] * WEIGHT_MAX[layer]) * peak + BIAS_MAX
            limit = jnp.broadcast_to(jnp.asarray(limit, F32), (1, CHUNK))
            scale = (TOP / limit).astype(BF16).astype(F32)
            put_rows(layer + 1, 0, cols, value, scale)
            if layer + 1 in MIXED:
                shrinks[layer + 1 : layer + 2, cols] = 1.0 / scale
            if layer + 2 in MIXED:
                highest = jnp.max(value, axis=0, keepdims=True)
                peaks[layer + 1 : layer + 2, cols] = jnp.maximum(highest, SILU_DIP)
            return
        for part in range(CHUNK // LANES):
            r = c * (CHUNK // LANES) + part
            day = inverse[r : r + 1, :] >= 0
            shown = jnp.where(
                day, value[: sizes[6], part * LANES : (part + 1) * LANES], 0.0
            )
            tend[:, r * LANES : (r + 1) * LANES] = shown
            field[r, 0:levels, :] = (
                tracer[pl.ds(r, levels, stride=rows), :] + shown[0:levels]
            )
        out_copy(c).start()

    w_copy(0).start()
    for c in range(chunks):
        x_copy(c).start()
    for i in range(10):
        small_copy(i).start()
    w_copy(1).start()
    w_tail[...] = jnp.zeros(w_tail.shape, F32)
    x_tail[...] = jnp.zeros(x_tail.shape, F32)
    weights_in[5][sizes[6] :, :] = jnp.zeros(
        (weights_in[5].shape[0] - sizes[6], sizes[5]), F32
    )
    w_copy(0).wait()
    w_tail[0 : aligned - whole, :] = weights_in[0][whole:aligned, :]
    w_tail[aligned - whole : depth_in - whole, :] = weights_in[0][aligned:depth_in, :]
    prepare(0, 0, 1)
    for layer in range(2, 6):
        w_copy(layer).start()
    x_copy(0).wait()
    prepare_inputs(0)

    for layer in range(6):
        if 0 < layer < 5:
            w_copy(layer + 1).wait()
        for c in range(chunks):
            main = main_product(layer, c)
            if layer == 0 and c == 0:
                for i in range(10):
                    small_copy(i).wait()
                bias_columns(0)
                for i in range(1, chunks):
                    x_copy(i).wait()
                    prepare_inputs(i)
                w_copy(1).wait()
            if layer < 5:
                prepare(layer + 1, c, chunks)
            rest = rest_product(layer, c)
            if layer == 4 and c == 0:
                for r in range(rows):
                    field[r, levels : levels + 1, :] = along[r : r + 1, :]
                    field[r, levels + 1 : levels + 2, :] = across[r : r + 1, :]
                    field[r, levels + 2 : levels_wide, :] = jnp.zeros(
                        (levels_wide - levels - 2, LANES), F32
                    )
            if layer < 5 and c == chunks - 1:
                bias_columns(layer + 1)
            finish(layer, c, main, rest)

    odd = lax.rem(lax.axis_index(axis), 2)
    leaving = [
        pltpu.make_async_copy(
            field.at[pl.ds((rows - HALO) * odd, HALO)], pay_a, field_sems.at[0]
        ),
        pltpu.make_async_copy(
            field.at[pl.ds((rows - HALO) * (1 - odd), HALO)], pay_b, field_sems.at[1]
        ),
        pltpu.make_async_copy(field, field_hbm.at[pl.ds(0, rows)], field_sems.at[2]),
    ]
    for copy in leaving:
        copy.start()
    for copy in leaving:
        copy.wait()
    for c in range(chunks):
        out_copy(c).wait()


def network(inverse, tracer, along, across, biases, x, weights, axis):
    sizes = [x.shape[0]] + [b.shape[0] for b in biases]
    width = x.shape[1]
    rows = along.shape[0]
    levels = tracer.shape[0] // rows
    levels_wide = round_up(levels + 2, 8)
    chunks = width // CHUNK
    padded = [round_up(s, LANES) for s in sizes]
    deepest = max(padded[:6])
    tail = padded[0] - sizes[0] // LANES * LANES
    hbm = pl.BlockSpec(memory_space=pl.ANY)
    total = sum(sizes[i] * sizes[i + 1] for i in range(6)) * width
    return pl.pallas_call(
        functools.partial(network_kernel, sizes=sizes, levels=levels, axis=axis),
        out_shape=(
            jax.ShapeDtypeStruct((sizes[6], width), F32),
            jax.ShapeDtypeStruct((ROOM, levels_wide, LANES), F32),
            jax.ShapeDtypeStruct((HALO, levels_wide, LANES), F32),
            jax.ShapeDtypeStruct((HALO, levels_wide, LANES), F32),
        ),
        in_specs=[hbm] * 17,
        out_specs=(hbm,) * 4,
        scratch_shapes=[
            pltpu.VMEM(x.shape, F32),
            *[pltpu.VMEM(w.shape, F32) for w in weights[:5]],
            pltpu.VMEM((padded[6], sizes[5]), F32),
            *[
                pltpu.VMEM((padded[i + 1], padded[i] * (1 if i in MIXED else 3)), BF16)
                for i in range(6)
            ],
            *[pltpu.VMEM((padded[i + 1], 2 * padded[i]), F8) for i in range(6)],
            *[pltpu.VMEM((padded[i + 1], LANES), F32) for i in range(6)],
            pltpu.VMEM(inverse.shape, jnp.int32),
            pltpu.VMEM(tracer.shape, F32),
            pltpu.VMEM(along.shape, F32),
            pltpu.VMEM(across.shape, F32),
            *[pltpu.VMEM(b.shape, F32) for b in biases],
            *[pltpu.VMEM((3 * deepest, width), BF16)] * 2,
            *[pltpu.VMEM((2 * deepest, width), F8)] * 2,
            pltpu.VMEM((tail, sizes[1]), F32),
            pltpu.VMEM((tail, width), F32),
            pltpu.VMEM((8, padded[6]), F32),
            pltpu.VMEM((sizes[6], width), F32),
            pltpu.VMEM((8, width), F32),
            pltpu.VMEM((8, width), F32),
            pltpu.VMEM((rows, levels_wide, LANES), F32),
            pltpu.SemaphoreType.DMA((chunks,)),
            pltpu.SemaphoreType.DMA((6,)),
            pltpu.SemaphoreType.DMA((chunks,)),
            pltpu.SemaphoreType.DMA((10,)),
            pltpu.SemaphoreType.DMA((3,)),
        ],
        compiler_params=pltpu.CompilerParams(vmem_limit_bytes=NETWORK_VMEM),
        cost_estimate=pl.CostEstimate(
            flops=4 * total, bytes_accessed=14_000_000, transcendentals=3_000_000
        ),
        name="column_network",
    )(inverse, tracer, along, across, *biases, x, *weights)


def half_minmod(first, second):
    return 0.5 * (
        jnp.maximum(jnp.minimum(first, second), 0.0)
        + jnp.minimum(jnp.maximum(first, second), 0.0)
    )


def cat(values):
    return values[0] if len(values) == 1 else jnp.concatenate(values, axis=0)


def advect_kernel(
    field, got_a, got_b, out, wide, speeds, held, out_sems, *, levels, axis
):
    rows = field.shape[0]
    odd = lax.rem(lax.axis_index(axis), 2)
    wide[HALO : HALO + rows] = field[...]
    wide[pl.ds((HALO + rows) * odd, HALO)] = got_a[...]
    wide[pl.ds((HALO + rows) * (1 - odd), HALO)] = got_b[...]

    def place(i):
        for kind in range(2):
            courant = jnp.broadcast_to(
                wide[i, levels + kind : levels + kind + 1, :], (8, LANES)
            )
            speeds[2 * kind, i] = jnp.maximum(courant, 0.0)
            speeds[2 * kind + 1, i] = jnp.minimum(courant, 0.0)

    for i in range(rows + 2 * HALO):
        place(i)
    groups = wide.shape[1] // GROUP
    span = GROUP * rows

    def leaving(g, start, size):
        return pltpu.make_async_copy(
            held.at[pl.ds(start, size)], out.at[pl.ds(start, size)], out_sems.at[g]
        )

    last = out.shape[0] - (groups - 1) * span

    def group(g, carry):
        wavefront(g, groups, levels, held, wide, speeds, rows)

        @pl.when(g < groups - 1)
        def _():
            leaving(g, pl.multiple_of(g * span, span), span).start()

        return carry

    lax.fori_loop(0, groups, group, 0)
    leaving(groups - 1, (groups - 1) * span, last).start()
    for g in range(groups - 1):
        leaving(g, g * span, span).wait()
    leaving(groups - 1, (groups - 1) * span, last).wait()


def wavefront(g, groups, levels, out, wide, speeds, rows):
    base = pl.multiple_of(g * GROUP, GROUP)
    blocks = GROUP // 8
    keep = levels - (groups - 1) * GROUP
    fields = [{}, {}, {}]
    steps, slopes, fluxes = [{}, {}, {}], [{}, {}, {}], [{}, {}, {}]
    reach = [(-4, rows + 3), (-2, rows + 1), (0, rows - 1)]
    shape = (blocks, 8, LANES)

    def load(i):
        return wide[i + HALO, pl.ds(base, GROUP), :].reshape(shape)

    def courant(kind, at):
        return cat([jnp.broadcast_to(speeds[kind, i + HALO], shape) for i in at])

    def pieces(value, count):
        return [value[n * blocks : (n + 1) * blocks] for n in range(count)]

    def face(active, at):
        ahead, behind = courant(0, at), courant(1, at)
        upper = cat([fields[k][i] - slopes[k][i] for k, i in zip(active, at)])
        lower = cat([fields[k][i - 1] + slopes[k][i - 1] for k, i in zip(active, at)])
        return ahead * lower + behind * upper

    rest = []
    for i in range(-HALO, -2):
        fields[0][i] = load(i)
    for t in range(-4, rows + 6):
        active = [k for k in range(3) if reach[k][0] <= t - 3 * k <= reach[k][1]]
        if t + 2 < rows + HALO:
            fields[0][t + 2] = load(t + 2)
        for k in active:
            c = t - 3 * k
            if c == reach[k][0]:
                f = fields[k]
                for i in (c - 1, c, c + 1):
                    steps[k][i] = f[i] - f[i - 1]
                for i in (c - 1, c):
                    slopes[k][i] = half_minmod(steps[k][i + 1], steps[k][i])
                fluxes[k][c] = face([k], [c])
        at = [t - 3 * k for k in active]
        here = cat([fields[k][i] for k, i in zip(active, at)])
        back = here - pltpu.roll(here, 1, 2)
        new = cat(
            [fields[k][i + 2] - fields[k][i + 1] for k, i in zip(active, at)]
        )
        last = cat([steps[k][i + 1] for k, i in zip(active, at)])
        bend = half_minmod(pltpu.roll(back, LANES - 1, 2), back)
        slope = half_minmod(new, last)
        for k, i, a_step, a_slope in zip(
            active, at, pieces(new, len(at)), pieces(slope, len(at))
        ):
            steps[k][i + 2], slopes[k][i + 1] = a_step, a_slope
        side = courant(2, at) * pltpu.roll(here + bend, 1, 2)
        side = side + courant(3, at) * (here - bend)
        flux = face(active, [i + 1 for i in at])
        for k, i, a_flux in zip(active, at, pieces(flux, len(at))):
            fluxes[k][i + 1] = a_flux
        moved = cat([fluxes[k][i] for k, i in zip(active, at)]) - flux
        moved = here + (moved + (side - pltpu.roll(side, LANES - 1, 2)))
        for k, i, value in zip(active, at, pieces(moved, len(at))):
            if k == 0:
                fields[1][i] = value
            elif k == 1:
                fields[2][i] = 0.75 * fields[0][i] + 0.25 * value
            else:
                value = 1.0 / 3.0 * fields[0][i] + 2.0 / 3.0 * value
                value = value.reshape(GROUP, LANES)
                out[pl.ds(base * rows + i, keep, stride=rows), :] = value[:keep]
                rest.append((i, value[keep:]))
    if keep < GROUP:

        @pl.when(g < groups - 1)
        def _():
            for i, value in rest:
                lines = pl.ds((base + keep) * rows + i, GROUP - keep, stride=rows)
                out[lines, :] = value


def stage_kernel(field, own, sem):
    copy = pltpu.make_async_copy(field.at[pl.ds(0, own.shape[0])], own, sem)
    copy.start()
    copy.wait()


def stage(field, rows):
    return pl.pallas_call(
        stage_kernel,
        out_shape=jax.ShapeDtypeStruct((rows, *field.shape[1:]), F32),
        in_specs=[pl.BlockSpec(memory_space=pl.ANY)],
        out_specs=pl.BlockSpec(memory_space=pltpu.VMEM),
        scratch_shapes=[pltpu.SemaphoreType.DMA],
        compiler_params=pltpu.CompilerParams(vmem_limit_bytes=ADVECT_VMEM),
        cost_estimate=pl.CostEstimate(
            flops=0, bytes_accessed=4_000_000, transcendentals=0
        ),
        name="stage_rows",
    )(field)


def advect(field, got_a, got_b, levels, axis):
    rows, levels_wide, across = field.shape
    vmem, hbm = pl.BlockSpec(memory_space=pltpu.VMEM), pl.BlockSpec(memory_space=pl.ANY)
    return pl.pallas_call(
        functools.partial(advect_kernel, levels=levels, axis=axis),
        out_shape=jax.ShapeDtypeStruct((levels * rows, across), F32),
        in_specs=[vmem] * 3,
        out_specs=hbm,
        scratch_shapes=[
            pltpu.VMEM((rows + 2 * HALO, levels_wide, across), F32),
            pltpu.VMEM((4, rows + 2 * HALO, 8, across), F32),
            pltpu.VMEM((levels * rows, across), F32),
            pltpu.SemaphoreType.DMA((levels_wide // GROUP,)),
        ],
        compiler_params=pltpu.CompilerParams(vmem_limit_bytes=ADVECT_VMEM),
        name="advect_sections",
    )(field, got_a, got_b)


def shards(inputs, tracer, speed_along, speed_across, inverse_list, *params):
    weights, biases = list(params[0::2]), params[1::2]
    weights[5] = weights[5].T
    levels, rows, across = tracer.shape
    tendencies, field, pay_a, pay_b = network(
        inverse_list.reshape(rows, across),
        tracer.reshape(levels * rows, across),
        speed_along,
        speed_across,
        biases,
        inputs.T,
        weights,
        "gx",
    )
    count = lax.axis_size("gx")
    outer = [(i, (i - 1 if i % 2 == 0 else i + 1) % count) for i in range(count)]
    inner = [(i, i + 1 if i % 2 == 0 else i - 1) for i in range(count)]
    got_a = lax.ppermute(pay_a, "gx", outer)
    got_b = lax.ppermute(pay_b, "gx", inner)
    advected = advect(stage(field, rows), got_a, got_b, levels, "gx")
    return tendencies.T, advected.reshape(levels, rows, across)


def solution(mesh):
    placed = (
        P(("member", "gx"), None),
        P(None, ("member", "gx"), None),
        P(("member", "gx"), None),
        P(("member", "gx"), None),
        P(("member", "gx")),
        *[P()] * 12,
    )
    return jax.shard_map(
        shards,
        mesh=mesh,
        in_specs=placed,
        out_specs=(P(("member", "gx"), None), P(None, ("member", "gx"), None)),
        check_vma=False,
    )
```
